512 devices in a mesh: elec: 64 (over z, x, core), cell: 8 (over y).
Axes of the slice: x: 4, y: 8, z: 8, core: 2. Of those that a mesh axis runs over, the one named last changes fastest.
Arguments:
- fields: bfloat16 [2, 3, 512, 65536], P(None, None, 'elec', 'cell'), may hold values from -6 to 6
- residual: float32 [65536, 8, 2], P(('elec', 'cell')), may hold values from -0.0024414062 to 0.0024414062
- quad_group: int32 [65536, 1], P(('elec', 'cell')), may hold values from 0 to 63; in each aligned block of 128 rows (0 to 127, 128 to 255, ...) at most 4 rows name the same one
- offsets: int32 [65536, 3], P(('elec', 'cell')), may hold values from 0 to 7
- b_step: int32 [65536, 1], P(('elec', 'cell')), may hold values from 1 to 7
- sides: int32 [65536, 2], P(('elec', 'cell')), may hold values from -1 to 1, as said below
Outputs:
- gradient: float32 [8, 2, 8, 8192], P(None, None, 'cell', 'elec')
The draws below stay inside these ranges and needn't reach their ends.
Inputs may be any that keep to these rules, and one draw needn't show every extreme that they name: `quad_group`: within the quadrupoles of one device (aligned blocks of 128 rows), no group is named more than 4 times, a bound that some block reaches. In every quadrupole at least one of the two sides is -1.
All inputs are finite; a program needn't handle non-finite values.
Results may differ from the reference program's by a relative error of at most 0.0029.
Values may be sent and summed in bfloat16 or wider, within the bound.
A program may use at most 128 MiB of HBM per device.

```python
import math
import jax
import jax.numpy as jnp
import numpy as np
from jax import lax

ELECTRODES = 512
FRAMES = 8
Q_DEV = 128
CELL_DEV = 8192
E_DEV = 8
CAP = 4
QUADS = 65536
CELLS = 65536
N_ELEC = 64
N_CELL = 8


def draw_sides(key, part):
    key = jax.random.fold_in(key, 7)
    first_key, second_key = jax.random.split(key)
    first = jax.random.randint(first_key, (QUADS,), -1, 2, dtype=jnp.int32)
    other = jax.random.randint(second_key, (QUADS,), 0, 2, dtype=jnp.int32)
    second = jnp.where(first == -1, other, -1).astype(jnp.int32)
    return jnp.stack([first, second], axis=1)


def place_ends(result, own_key, smallest, largest):
    longest = result.shape.index(max(result.shape))
    spots = []
    for shift in (0, 1):
        where = [jax.random.randint(jax.random.fold_in(own_key, axis), (), 0, length) for axis, length in enumerate(result.shape)]
        where[longest] = (where[longest] + shift) % result.shape[longest]
        spots.append(tuple(where))
    return result.at[spots[0]].set(smallest).at[spots[1]].set(largest)


def level_of(rng, dims, cuts, least, high):
    loudness, own = 1.0, jax.random.fold_in(rng, 6)
    for axis_at, parts in cuts:
        heights = jnp.exp(jax.random.uniform(jax.random.fold_in(own, axis_at), (parts,), jnp.float32, least / len(cuts), high / len(cuts)))
        loudness = loudness * jnp.repeat(heights, dims[axis_at] // parts).reshape([-1 if axis == axis_at else 1 for axis in range(len(dims))])
    return loudness


def shared_out(own_key, own, number, rows, count, top, bound, lean):
    order = jax.random.permutation(own_key, count)
    packed, usual = load_shares(count, rows * top, bound, lean, True), load_shares(count, rows * top, bound, lean, False)
    places = jnp.arange(count)

    def named(sizes, turn):
        used = int((sizes > 0).sum())
        fixed = max(1, used // 4)
        moved = fixed + (places - fixed + turn * (used - fixed)) % max(1, count - fixed)
        return jnp.zeros((count,), jnp.int32).at[order[jnp.where(places < fixed, places, moved)]].set(jnp.asarray(sizes, jnp.int32))

    sizes = jnp.where(number % 4 == 0, named(packed, number // 4), named(usual, number - number // 4 - 1))
    mixed = jax.random.permutation(jax.random.fold_in(own, 3), count)
    source_of, receiver = mixed[0:count // 2 * 2:2], mixed[1:count // 2 * 2:2]
    slack = jnp.minimum(sizes[source_of] - 1, bound - sizes[receiver]) // 2
    slack = jnp.where((source_of == order[0]) | (receiver == order[0]) | (sizes[receiver] == 0), 0, jnp.maximum(slack, 0))
    moved = jax.random.randint(jax.random.fold_in(own, 4), (count // 2,), 0, 1 << 20) % (slack + 1)
    sizes = sizes.at[source_of].add(-moved).at[receiver].add(moved)
    members = jnp.searchsorted(jnp.cumsum(sizes), jnp.arange(rows * top), side="right").astype(jnp.int32)
    listing = members.reshape(top, rows).T
    listing = listing[jax.random.permutation(jax.random.fold_in(own, 1), rows)]
    turn = jax.random.randint(jax.random.fold_in(own, 2), (rows, 1), 0, top)
    return jnp.take_along_axis(listing, (jnp.arange(top)[None, :] + turn) % top, axis=1)


def load_shares(number_of, total, limit, slope, full):
    portions = [(1 << 20) // math.isqrt(standing ** slope) + 1 for standing in range(1, number_of + 1)]
    largest = limit if full else min(limit, max(-(-total // number_of), total * portions[0] // sum(portions)))
    least = 1 if total - largest >= number_of - 1 else 0
    given, rest = [largest] + [least] * (number_of - 1), total - largest - least * (number_of - 1)
    while rest > 0:
        candidates = [i for i in range(1, number_of) if given[i] < largest] or [i for i in range(1, number_of) if given[i] < limit]
        whole, left = sum([portions[i] for i in candidates]), rest
        for i in candidates:
            extra = min(limit - given[i], max(1, left * portions[i] // whole), rest)
            given[i] = given[i] + extra
            rest = rest - extra
    return np.array(given)


def bell_draw(stream_key, dims, deviation, most, shards=(), held_as=jnp.bfloat16):
    entries = jax.random.normal(stream_key, dims, jnp.float32) * deviation
    if len(shards) > 0:
        entries = level_of(stream_key, dims, shards, -0.22, 0.18) * entries
    return jnp.clip(entries, min=-most, max=most).astype(held_as)


def setup_inputs(seed: int = 0) -> dict:
    keys = jax.random.split(jax.random.key(seed), 7)
    fields = bell_draw(keys[0], (2, 3, ELECTRODES, CELLS), 1.0, 6.0, ((2, 64), (3, 8)))
    residual = bell_draw(keys[1], (QUADS, FRAMES, 2), (96 * QUADS) ** -0.5, 0.0024414062, ((0, 512),), jnp.float32)
    quad_group_keys = jax.random.split(jax.random.fold_in(keys[2], 1), QUADS // Q_DEV)
    quad_group_turns = jax.random.permutation(jax.random.fold_in(keys[2], 3), QUADS // Q_DEV)
    quad_group = jax.vmap(lambda own, number: shared_out(jax.random.fold_in(keys[2], 2), own, number, Q_DEV, N_ELEC, 1, CAP, 2))(quad_group_keys, quad_group_turns).reshape((QUADS, 1))
    offsets = place_ends(jax.random.randint(keys[3], (QUADS, 3), 0, E_DEV), jax.random.fold_in(keys[3], 1), 0, E_DEV - 1).astype(jnp.int32)
    b_step = place_ends(jax.random.randint(keys[4], (QUADS, 1), 1, E_DEV), jax.random.fold_in(keys[4], 1), 1, E_DEV - 1).astype(jnp.int32)
    sides = draw_sides(jax.random.fold_in(keys[6], 71), 0)
    return dict(fields=fields, residual=residual, quad_group=quad_group, offsets=offsets, b_step=b_step, sides=sides)


def locate(quad_group, offsets, b_step, sides, groups, per_group):
    owner = quad_group[:, 0]
    source_a = offsets[:, 0]
    source_b = (source_a + b_step[:, 0]) % per_group
    group_m = jnp.clip(owner + sides[:, 0], 0, groups - 1)
    group_n = jnp.clip(owner + sides[:, 1], 0, groups - 1)
    column_m = (group_m - owner + 1) * per_group + offsets[:, 1]
    column_n = (group_n - owner + 1) * per_group + offsets[:, 2]
    return owner, source_a, source_b, column_m, column_n


def correlate(row_blocks, window, center):
    rows_wide = row_blocks.astype(jnp.float32)
    window_wide = window.astype(jnp.float32)
    center_wide = center.astype(jnp.float32)
    adjoint_real = jnp.einsum('tej,cjk->tcek', rows_wide[:, 0], window_wide[0]) + jnp.einsum('tej,cjk->tcek', rows_wide[:, 1], window_wide[1])
    adjoint_imag = jnp.einsum('tej,cjk->tcek', rows_wide[:, 1], window_wide[0]) - jnp.einsum('tej,cjk->tcek', rows_wide[:, 0], window_wide[1])
    real_part = -(jnp.einsum('cek,tcek->tk', center_wide[0], adjoint_real) + jnp.einsum('cek,tcek->tk', center_wide[1], adjoint_imag))
    imag_part = -(jnp.einsum('cek,tcek->tk', center_wide[0], adjoint_imag) - jnp.einsum('cek,tcek->tk', center_wide[1], adjoint_real))
    return jnp.stack([real_part, imag_part], axis=1)


def reference(fields, residual, quad_group, offsets, b_step, sides):
    per_group = ELECTRODES // N_ELEC
    owner, source_a, source_b, column_m, column_n = locate(quad_group, offsets, b_step, sides, N_ELEC, per_group)
    elec_a = owner * per_group + source_a
    elec_b = owner * per_group + source_b
    elec_m = (owner - 1) * per_group + column_m
    elec_n = (owner - 1) * per_group + column_n
    band_rows = jnp.zeros((ELECTRODES, ELECTRODES, FRAMES, 2), jnp.float32)
    band_rows = band_rows.at[elec_a, elec_m].add(residual)
    band_rows = band_rows.at[elec_a, elec_n].add(-residual)
    band_rows = band_rows.at[elec_b, elec_m].add(-residual)
    band_rows = band_rows.at[elec_b, elec_n].add(residual)
    sources = jnp.transpose(band_rows, (2, 3, 0, 1)).astype(jnp.bfloat16)
    sources = lax.optimization_barrier(sources)
    padded = jnp.pad(sources, ((0, 0), (0, 0), (0, 0), (per_group, per_group)))
    cell_count = CELLS
    block_cells = math.gcd(cell_count, 8192)
    block_count = cell_count // block_cells
    zero_index = jnp.zeros((), jnp.int32)

    def group_term(accumulated, group):
        group = group.astype(jnp.int32)
        row_start = (group * per_group).astype(jnp.int32)
        row_blocks = lax.dynamic_slice(padded, (zero_index, zero_index, row_start, row_start), (FRAMES, 2, per_group, 3 * per_group))
        lower = (jnp.maximum(group - 1, 0) * per_group).astype(jnp.int32)
        upper = (jnp.minimum(group + 1, N_ELEC - 1) * per_group).astype(jnp.int32)
        below_gate = (group > 0).astype(jnp.bfloat16)
        above_gate = (group < N_ELEC - 1).astype(jnp.bfloat16)

        def block_term(number):
            first_cell = (number * block_cells).astype(jnp.int32)
            center = lax.dynamic_slice(fields, (zero_index, zero_index, row_start, first_cell), (2, 3, per_group, block_cells))
            below = lax.dynamic_slice(fields, (zero_index, zero_index, lower, first_cell), (2, 3, per_group, block_cells)) * below_gate
            above = lax.dynamic_slice(fields, (zero_index, zero_index, upper, first_cell), (2, 3, per_group, block_cells)) * above_gate
            window = jnp.concatenate([below, center, above], axis=2)
            return correlate(row_blocks, window, center)

        pieces = lax.map(block_term, jnp.arange(block_count, dtype=jnp.int32))
        return accumulated + jnp.transpose(pieces, (1, 2, 0, 3)).reshape(FRAMES, 2, cell_count), None

    start_value = jnp.zeros((FRAMES, 2, cell_count), jnp.float32)
    gradient, unused = lax.scan(group_term, start_value, jnp.arange(N_ELEC, dtype=jnp.int32))
    return gradient.reshape(FRAMES, 2, N_CELL, CELL_DEV)
```

```python
import functools

import jax
import jax.numpy as jnp
from jax import lax
from jax.experimental import pallas as pl
from jax.experimental.pallas import tpu as pltpu
from jax.sharding import PartitionSpec as P

X_CHIPS = 4
PER_GROUP = 8
FRAMES = 8
CAP = 4
SLOT = 32
WINDOW = 3 * PER_GROUP
F32 = jnp.float32
BF16 = jnp.bfloat16


def iota(shape, dim):
    return lax.broadcasted_iota(jnp.int32, shape, dim)


def split3(value):
    high = value.astype(BF16)
    rest = value - high.astype(F32)
    middle = rest.astype(BF16)
    low = (rest - middle.astype(F32)).astype(BF16)
    return high, middle, low


def dot_nt(left, right):
    return lax.dot_general(left, right, (((1,), (1,)), ((), ())), preferred_element_type=F32)


def drain(ref, sem):
    pltpu.make_async_copy(ref, ref, sem).wait()


def kernel(
    sizes,
    fields, resid_in, group_in, offs_in, bstep_in, sides_in,
    out,
    resid, group, offs, bstep, sides,
    own, low, high, mid,
    slots, a_buf, b_send, b_buf, c_send, c_buf, weights,
    part, core_recv, x_send, x_recv, z_send, z_recv,
    in_sem, own_sem, halo_send_sem, halo_recv_sem,
    stage_send_sem, stage_recv_sem,
    core_send_sem, core_recv_sem, x_send_sem, x_recv_sem, z_send_sem, z_recv_sem,
):
    nz, nx, ny = sizes
    lines = 2 * nx
    groups = nz * lines
    quads = resid.shape[1]
    elec = lax.axis_index("elec")
    cell = lax.axis_index("cell")
    z = elec // lines
    p = elec % lines
    x = p // 2
    core = p % 2

    inputs = [
        pltpu.make_async_copy(source, target, in_sem.at[number])
        for number, (source, target) in enumerate(
            zip((resid_in, group_in, offs_in, bstep_in, sides_in), (resid, group, offs, bstep, sides))
        )
    ]
    for copy in inputs:
        copy.start()

    def line_peer(d):
        return {"elec": z * lines + (p + d) % lines}

    def z_peer(d):
        return {"elec": ((z + d) % nz) * lines + p}

    def x_peer(d):
        return {"elec": z * lines + ((x + d) % nx) * 2 + core}

    def y_peer(d):
        return {"cell": (cell + d) % ny}

    core_peer = {"elec": z * lines + x * 2 + 1 - core}
    next_peer = {"elec": (elec + 1) % groups}
    prev_peer = {"elec": (elec + groups - 1) % groups}

    if groups < 64:
        b_buf[...] = jnp.zeros_like(b_buf)
    barrier = pltpu.get_barrier_semaphore()
    peers = (
        [line_peer(d) for d in range(1, lines)]
        + [z_peer(d) for d in range(1, nz)]
        + [y_peer(d) for d in range(1, ny)]
        + [next_peer, prev_peer]
    )
    for peer in peers:
        pl.semaphore_signal(barrier, inc=1, device_id=peer, device_id_type=pl.DeviceIdType.MESH)

    own_copy = pltpu.make_async_copy(fields, own, own_sem)
    own_copy.start()

    def send(source, target, send_sem, recv_sem, peer):
        pltpu.make_async_remote_copy(
            src_ref=source, dst_ref=target, send_sem=send_sem, recv_sem=recv_sem,
            device_id=peer, device_id_type=pl.DeviceIdType.MESH,
        ).start()

    def send_halo(c):
        send(fields.at[:, c], low.at[:, c], halo_send_sem.at[0], halo_recv_sem.at[0], next_peer)
        send(fields.at[:, c], high.at[:, c], halo_send_sem.at[1], halo_recv_sem.at[1], prev_peer)

    for copy in inputs:
        copy.wait()
    owner = group[...]
    source_a = offs[pl.ds(0, 1), :]
    source_b = (source_a + bstep[...]) % PER_GROUP
    group_m = jnp.clip(owner + sides[pl.ds(0, 1), :], 0, groups - 1)
    group_n = jnp.clip(owner + sides[pl.ds(1, 1), :], 0, groups - 1)
    column_m = (group_m - owner + 1) * PER_GROUP + offs[pl.ds(1, 1), :]
    column_n = (group_n - owner + 1) * PER_GROUP + offs[pl.ds(2, 1), :]
    row = iota((groups, quads), 0)
    names = (row % nz) * lines + row // nz
    member = jnp.where(names == owner, 1.0, 0.0).astype(F32)
    earlier = jnp.where(iota((quads, quads), 0) < iota((quads, quads), 1), 1.0, 0.0).astype(BF16)
    before = jnp.dot(member.astype(BF16), earlier, preferred_element_type=F32)
    rank = jnp.sum(member * before, axis=0, keepdims=True)
    place = iota((8, quads), 0)
    indices = jnp.where(
        place == 0, source_a,
        jnp.where(place == 1, source_b, jnp.where(place == 2, column_m, jnp.where(place == 3, column_n, 0))),
    ).astype(F32)
    real = -resid[pl.ds(0, FRAMES, stride=2), :]
    imag = -resid[pl.ds(1, FRAMES, stride=2), :]
    entry = jnp.concatenate([real, imag, indices, jnp.zeros_like(indices)], axis=0)
    entries = jnp.concatenate(
        [jnp.where(rank == float(k), entry, 0.0) for k in range(CAP)], axis=0
    )
    named = member.astype(BF16)
    sorted_rows = sum(dot_nt(named, piece) for piece in split3(entries)[::-1])
    for line in range(lines):
        slots[line] = sorted_rows[line * nz:(line + 1) * nz, :]

    pl.semaphore_wait(barrier, len(peers))

    for d in range(1, lines):
        send(slots.at[(p + d) % lines], a_buf.at[pl.ds((d - 1) * nz, nz)],
             stage_send_sem.at[0], stage_recv_sem.at[0], line_peer(d))
    for c in range(3):
        send_halo(c)
    a_buf[pl.ds((lines - 1) * nz, nz), :] = slots[p]
    own_copy.wait()
    for part_index in range(2):
        for c in range(3):
            mid[part_index, c] = own[part_index, c].astype(F32)
    arrived = a_buf.at[pl.ds(0, (lines - 1) * nz)]
    drain(arrived, stage_recv_sem.at[0])
    for to in range(nz):
        b_send[to] = a_buf[pl.ds(to, lines, stride=nz), :]
    for d in range(1, nz):
        send(b_send.at[(z + d) % nz], b_buf.at[pl.ds((d - 1) * lines, lines)],
             stage_send_sem.at[1], stage_recv_sem.at[1], z_peer(d))
    b_buf[pl.ds((nz - 1) * lines, lines), :] = b_send[z]
    drain(b_buf.at[pl.ds(0, (nz - 1) * lines)], stage_recv_sem.at[1])

    received = b_buf[...]
    both = jnp.concatenate([received, pltpu.roll(received, 64, 1)], axis=0)
    turned = both.T
    terms = []
    columns = []
    for half in range(2):
        block = turned[half * SLOT:(half + 1) * SLOT, :]
        at_a = block[16:17].astype(jnp.int32)
        at_b = block[17:18].astype(jnp.int32)
        at_m = block[18:19].astype(jnp.int32)
        at_n = block[19:20].astype(jnp.int32)
        pieces = []
        for o in range(2):
            values = block[o * 8:(o + 1) * 8]
            for e in range(PER_GROUP):
                sign = jnp.where(at_a == e, 1.0, 0.0) - jnp.where(at_b == e, 1.0, 0.0)
                pieces.append(values * sign)
        terms.append(jnp.concatenate(pieces, axis=0))
        place = iota((WINDOW, 128), 0)
        columns.append((jnp.where(place == at_m, 1.0, 0.0) - jnp.where(place == at_n, 1.0, 0.0)).astype(BF16))
    band = jnp.zeros((WINDOW, 128), F32)
    for half in range(2):
        for piece in split3(terms[half])[::-1]:
            band = band + dot_nt(columns[half], piece)
    c_send[...] = band
    for d in range(1, ny):
        send(c_send, c_buf.at[d - 1], stage_send_sem.at[2], stage_recv_sem.at[2], y_peer(d))
    drain(c_buf, stage_recv_sem.at[2])
    for d in range(ny - 1):
        band = band + c_buf[d]
    band = band.astype(BF16).astype(F32)
    upper = jnp.concatenate([band, jnp.zeros((128 - WINDOW, 128), F32)], axis=0).T
    lower = jnp.concatenate([upper[64:], -upper[:64]], axis=0)
    first = upper + pltpu.roll(lower, WINDOW, 1)
    second = pltpu.roll(first, 2 * WINDOW, 1)
    third = pltpu.roll(first, 4 * WINDOW, 1)
    lane = iota((128, 128), 1)
    nothing = jnp.zeros((128, 128), BF16)
    weights[pl.ds(0, 128), pl.ds(0, 128)] = first.astype(BF16)
    weights[pl.ds(0, 128), pl.ds(128, 128)] = nothing
    weights[pl.ds(128, 128), pl.ds(0, 128)] = second.astype(BF16)
    weights[pl.ds(128, 128), pl.ds(128, 128)] = nothing
    weights[pl.ds(256, 128), pl.ds(0, 128)] = jnp.where(lane >= 4 * WINDOW, third, 0.0).astype(BF16)
    weights[pl.ds(256, 128), pl.ds(128, 128)] = jnp.where(lane < 2 * WINDOW, third, 0.0).astype(BF16)

    drain(low, halo_recv_sem.at[0])
    drain(high, halo_recv_sem.at[1])

    def z_step(s):
        return nz // 2 + (1 - 2 * (s % 2)) * ((s + 1) // 2)

    def compute(s):
        base = ((z + z_step(s)) % nz) * (lines * 128)
        matrix = weights[...][:, :3 * 2 * WINDOW]
        for chip in range(nx):
            lanes = pl.ds(pl.multiple_of(base + chip * 256, 256), 256)
            total_real = jnp.zeros((FRAMES, 256), F32)
            total_imag = jnp.zeros((FRAMES, 256), F32)
            window = []
            for c in range(3):
                for i in range(2):
                    window += [low[i, c, :, lanes].astype(F32), mid[i, c, :, lanes], high[i, c, :, lanes].astype(F32)]
            window = jnp.concatenate(window, axis=0).astype(BF16)
            adjoint = jnp.dot(matrix, window, preferred_element_type=F32)
            for c in range(3):
                for e in range(PER_GROUP):
                    mid_real = mid[0, c, pl.ds(e, 1), lanes]
                    mid_imag = mid[1, c, pl.ds(e, 1), lanes]
                    at = c * 128 + e * 8
                    adj_real = adjoint[at:at + 8]
                    adj_imag = adjoint[at + 64:at + 72]
                    total_real = total_real + mid_real * adj_real + mid_imag * adj_imag
                    total_imag = total_imag + mid_real * adj_imag - mid_imag * adj_real
            for k in range(2):
                part[s, k, chip, pl.ds(0, 8), :] = total_real[:, k * 128:(k + 1) * 128]
                part[s, k, chip, pl.ds(8, 8), :] = total_imag[:, k * 128:(k + 1) * 128]
        send(part.at[s, 1 - core], core_recv.at[s], core_send_sem, core_recv_sem.at[s], core_peer)

    def add_core(s):
        drain(core_recv.at[s], core_recv_sem.at[s])
        x_send[s] = part[s, core] + core_recv[s]
        for d in range(1, nx):
            send(x_send.at[s, (x + d) % nx], x_recv.at[s, d - 1], x_send_sem, x_recv_sem.at[s], x_peer(d))

    def add_x(s):
        drain(x_recv.at[s], x_recv_sem.at[s])
        total = x_send[s, x]
        for d in range(nx - 1):
            total = total + x_recv[s, d]
        return total

    def pass_z(s):
        z_send[s] = add_x(s)
        send(z_send.at[s], z_recv.at[s], z_send_sem, z_recv_sem, z_peer(z_step(s)))

    core_lag = 2
    x_lag = 5

    def step(s, carry):
        @pl.when(s < nz)
        def _():
            compute(s)

        @pl.when((s >= core_lag) & (s < nz + core_lag))
        def _():
            add_core(s - core_lag)

        @pl.when((s >= x_lag) & (s < nz - 1 + x_lag))
        def _():
            pass_z(s - x_lag)

        return carry

    lax.fori_loop(0, nz - 1 + x_lag, step, 0)
    total = add_x(nz - 1)
    drain(z_recv, z_recv_sem)
    for s in range(nz - 1):
        total = total + z_recv[s]
    out[pl.ds(0, FRAMES, stride=2), :] = total[0:8]
    out[pl.ds(1, FRAMES, stride=2), :] = total[8:16]

    drain(low, halo_send_sem.at[0])
    drain(high, halo_send_sem.at[1])
    drain(arrived, stage_send_sem.at[0])
    drain(b_buf.at[pl.ds(0, (nz - 1) * lines)], stage_send_sem.at[1])
    drain(c_buf, stage_send_sem.at[2])
    drain(core_recv, core_send_sem)
    drain(x_recv, x_send_sem)
    drain(z_recv, z_send_sem)


def local(fields, residual, quad_group, offsets, b_step, sides):
    groups = lax.axis_size("elec")
    ny = lax.axis_size("cell")
    nx = X_CHIPS
    lines = 2 * nx
    nz = groups // lines
    cells = fields.shape[3]
    count = residual.shape[0]
    resid = jnp.transpose(residual, (1, 2, 0)).reshape(2 * FRAMES, count)
    vmem = pl.BlockSpec(memory_space=pltpu.VMEM)
    field_shape = (2, 3, PER_GROUP, cells)
    dma = pltpu.SemaphoreType.DMA
    gradient = pl.pallas_call(
        functools.partial(kernel, (nz, nx, ny)),
        out_shape=jax.ShapeDtypeStruct((2 * FRAMES, 128), F32),
        in_specs=[pl.BlockSpec(memory_space=pltpu.HBM)] * 6,
        out_specs=vmem,
        scratch_shapes=[
            pltpu.VMEM((2 * FRAMES, count), F32),
            pltpu.VMEM((1, count), jnp.int32),
            pltpu.VMEM((3, count), jnp.int32),
            pltpu.VMEM((1, count), jnp.int32),
            pltpu.VMEM((2, count), jnp.int32),
            pltpu.VMEM(field_shape, BF16),
            pltpu.VMEM(field_shape, BF16),
            pltpu.VMEM(field_shape, BF16),
            pltpu.VMEM(field_shape, F32),
            pltpu.VMEM((lines, nz, 128), F32),
            pltpu.VMEM((groups, 128), F32),
            pltpu.VMEM((nz, lines, 128), F32),
            pltpu.VMEM((64, 128), F32),
            pltpu.VMEM((WINDOW, 128), F32),
            pltpu.VMEM((ny - 1, WINDOW, 128), F32),
            pltpu.VMEM((384, 256), BF16),
            pltpu.VMEM((nz, 2, nx, 16, 128), F32),
            pltpu.VMEM((nz, nx, 16, 128), F32),
            pltpu.VMEM((nz, nx, 16, 128), F32),
            pltpu.VMEM((nz, nx - 1, 16, 128), F32),
            pltpu.VMEM((nz, 16, 128), F32),
            pltpu.VMEM((nz - 1, 16, 128), F32),
            dma((5,)), dma, dma((2,)), dma((2,)),
            dma((3,)), dma((3,)),
            dma, dma((nz,)), dma, dma((nz,)), dma, dma,
        ],
        compiler_params=pltpu.CompilerParams(
            collective_id=0, has_side_effects=True, vmem_limit_bytes=63 * 1024 * 1024
        ),
    )(fields, resid, quad_group.T, offsets.T, b_step.T, sides.T)
    return gradient.reshape(FRAMES, 2, 1, 128)


def solution(mesh):
    return jax.shard_map(
        local,
        mesh=mesh,
        in_specs=(
            P(None, None, "elec", "cell"),
            P(("elec", "cell"), None, None),
            P(("elec", "cell"), None),
            P(("elec", "cell"), None),
            P(("elec", "cell"), None),
            P(("elec", "cell"), None),
        ),
        out_specs=P(None, None, "cell", "elec"),
        check_vma=False,
    )
```

```python
import functools

import jax
import jax.numpy as jnp
from jax import lax
from jax.experimental import pallas as pl
from jax.experimental.pallas import tpu as pltpu
from jax.sharding import PartitionSpec as P

X_CHIPS = 4
PER_GROUP = 8
FRAMES = 8
CAP = 4
SLOT = 32
WINDOW = 3 * PER_GROUP
F32 = jnp.float32
BF16 = jnp.bfloat16


def iota(shape, dim):
    return lax.broadcasted_iota(jnp.int32, shape, dim)


def split3(value):
    high = value.astype(BF16)
    rest = value - high.astype(F32)
    middle = rest.astype(BF16)
    low = (rest - middle.astype(F32)).astype(BF16)
    return high, middle, low


def dot_nt(left, right):
    return lax.dot_general(left, right, (((1,), (1,)), ((), ())), preferred_element_type=F32)


def drain(ref, sem):
    pltpu.make_async_copy(ref, ref, sem).wait()


def kernel(
    sizes,
    fields, resid_in, group_in, offs_in, bstep_in, sides_in,
    out,
    resid, group, offs, bstep, sides,
    own, low, high, mid,
    slots, a_buf, b_send, b_buf, c_send, c_buf, weights,
    part, core_recv, x_send, x_recv, z_send, z_recv,
    in_sem, own_sem, halo_send_sem, halo_recv_sem,
    stage_send_sem, stage_recv_sem,
    core_send_sem, core_recv_sem, x_send_sem, x_recv_sem, z_send_sem, z_recv_sem,
):
    nz, nx, ny = sizes
    lines = 2 * nx
    groups = nz * lines
    quads = resid.shape[1]
    halo_ends = (nz // 4, nz // 2)
    elec = lax.axis_index("elec")
    cell = lax.axis_index("cell")
    z = elec // lines
    p = elec % lines
    x = p // 2
    core = p % 2

    inputs = [
        pltpu.make_async_copy(source, target, in_sem.at[number])
        for number, (source, target) in enumerate(
            zip((resid_in, group_in, offs_in, bstep_in, sides_in), (resid, group, offs, bstep, sides))
        )
    ]
    for copy in inputs:
        copy.start()

    def line_peer(d):
        return {"elec": z * lines + (p + d) % lines}

    def z_peer(d):
        return {"elec": ((z + d) % nz) * lines + p}

    def x_peer(d):
        return {"elec": z * lines + ((x + d) % nx) * 2 + core}

    def y_peer(d):
        return {"cell": (cell + d) % ny}

    core_peer = {"elec": z * lines + x * 2 + 1 - core}
    next_peer = {"elec": (elec + 1) % groups}
    prev_peer = {"elec": (elec + groups - 1) % groups}

    if groups < 64:
        b_buf[...] = jnp.zeros_like(b_buf)
    barrier = pltpu.get_barrier_semaphore()
    peers = (
        [line_peer(d) for d in range(1, lines)]
        + [z_peer(d) for d in range(1, nz)]
        + [y_peer(d) for d in range(1, ny)]
        + [next_peer, prev_peer]
    )
    for peer in peers:
        pl.semaphore_signal(barrier, inc=1, device_id=peer, device_id_type=pl.DeviceIdType.MESH)

    own_copy = pltpu.make_async_copy(fields, own, own_sem)
    own_copy.start()

    def send(source, target, send_sem, recv_sem, peer):
        pltpu.make_async_remote_copy(
            src_ref=source, dst_ref=target, send_sem=send_sem, recv_sem=recv_sem,
            device_id=peer, device_id_type=pl.DeviceIdType.MESH,
        ).start()

    def z_step(s):
        return nz // 2 + (1 - 2 * (s % 2)) * ((s + 1) // 2)

    chunk = lines * 128

    def chunk_lanes(row, s):
        return pl.ds(pl.multiple_of(((row + z_step(s)) % nz) * chunk, chunk), chunk)

    def send_halo(s):
        for way, (peer, target, turn) in enumerate(((next_peer, low, 1), (prev_peer, high, groups - 1))):
            lanes = chunk_lanes((elec + turn) % groups // lines, s)
            send(fields.at[:, :, :, lanes], target.at[:, :, :, lanes],
                 halo_send_sem.at[way], halo_recv_sem.at[way, s], peer)

    for copy in inputs:
        copy.wait()
    owner = group[...]
    source_a = offs[pl.ds(0, 1), :]
    source_b = (source_a + bstep[...]) % PER_GROUP
    group_m = jnp.clip(owner + sides[pl.ds(0, 1), :], 0, groups - 1)
    group_n = jnp.clip(owner + sides[pl.ds(1, 1), :], 0, groups - 1)
    column_m = (group_m - owner + 1) * PER_GROUP + offs[pl.ds(1, 1), :]
    column_n = (group_n - owner + 1) * PER_GROUP + offs[pl.ds(2, 1), :]
    row = iota((groups, quads), 0)
    names = (row % nz) * lines + row // nz
    member = jnp.where(names == owner, 1.0, 0.0).astype(F32)
    earlier = jnp.where(iota((quads, quads), 0) < iota((quads, quads), 1), 1.0, 0.0).astype(BF16)
    before = jnp.dot(member.astype(BF16), earlier, preferred_element_type=F32)
    rank = jnp.sum(member * before, axis=0, keepdims=True)
    place = iota((8, quads), 0)
    indices = jnp.where(
        place == 0, source_a,
        jnp.where(place == 1, source_b, jnp.where(place == 2, column_m, jnp.where(place == 3, column_n, 0))),
    ).astype(F32)
    real = -resid[pl.ds(0, FRAMES, stride=2), :]
    imag = -resid[pl.ds(1, FRAMES, stride=2), :]
    entry = jnp.concatenate([real, imag, indices, jnp.zeros_like(indices)], axis=0)
    entries = jnp.concatenate(
        [jnp.where(rank == float(k), entry, 0.0) for k in range(CAP)], axis=0
    )
    named = member.astype(BF16)
    sorted_rows = sum(dot_nt(named, piece) for piece in split3(entries)[::-1])
    for line in range(lines):
        slots[line] = sorted_rows[line * nz:(line + 1) * nz, :]

    pl.semaphore_wait(barrier, len(peers))

    for d in range(1, lines):
        send(slots.at[(p + d) % lines], a_buf.at[pl.ds((d - 1) * nz, nz)],
             stage_send_sem.at[0], stage_recv_sem.at[0], line_peer(d))
    for s in range(0, halo_ends[0]):
        send_halo(s)
    a_buf[pl.ds((lines - 1) * nz, nz), :] = slots[p]
    own_copy.wait()
    for part_index in range(2):
        for c in range(3):
            mid[part_index, c] = own[part_index, c].astype(F32)
    arrived = a_buf.at[pl.ds(0, (lines - 1) * nz)]
    drain(arrived, stage_recv_sem.at[0])
    for to in range(nz):
        b_send[to] = a_buf[pl.ds(to, lines, stride=nz), :]
    for d in range(1, nz):
        send(b_send.at[(z + d) % nz], b_buf.at[pl.ds((d - 1) * lines, lines)],
             stage_send_sem.at[1], stage_recv_sem.at[1], z_peer(d))
    for s in range(halo_ends[0], halo_ends[1]):
        send_halo(s)
    b_buf[pl.ds((nz - 1) * lines, lines), :] = b_send[z]
    drain(b_buf.at[pl.ds(0, (nz - 1) * lines)], stage_recv_sem.at[1])

    received = b_buf[...]
    both = jnp.concatenate([received, pltpu.roll(received, 64, 1)], axis=0)
    turned = both.T
    terms = []
    columns = []
    for half in range(2):
        block = turned[half * SLOT:(half + 1) * SLOT, :]
        at_a = block[16:17].astype(jnp.int32)
        at_b = block[17:18].astype(jnp.int32)
        at_m = block[18:19].astype(jnp.int32)
        at_n = block[19:20].astype(jnp.int32)
        pieces = []
        for o in range(2):
            values = block[o * 8:(o + 1) * 8]
            for e in range(PER_GROUP):
                sign = jnp.where(at_a == e, 1.0, 0.0) - jnp.where(at_b == e, 1.0, 0.0)
                pieces.append(values * sign)
        terms.append(jnp.concatenate(pieces, axis=0))
        place = iota((WINDOW, 128), 0)
        columns.append((jnp.where(place == at_m, 1.0, 0.0) - jnp.where(place == at_n, 1.0, 0.0)).astype(BF16))
    band = jnp.zeros((WINDOW, 128), F32)
    for half in range(2):
        for piece in split3(terms[half])[::-1]:
            band = band + dot_nt(columns[half], piece)
    c_send[...] = band
    for d in range(1, ny):
        send(c_send, c_buf.at[d - 1], stage_send_sem.at[2], stage_recv_sem.at[2], y_peer(d))
    for s in range(halo_ends[1], nz):
        send_halo(s)
    drain(c_buf, stage_recv_sem.at[2])
    for d in range(ny - 1):
        band = band + c_buf[d]
    band = band.astype(BF16).astype(F32)
    upper = jnp.concatenate([band, jnp.zeros((128 - WINDOW, 128), F32)], axis=0).T
    lower = jnp.concatenate([upper[64:], -upper[:64]], axis=0)
    first = upper + pltpu.roll(lower, WINDOW, 1)
    second = pltpu.roll(first, 2 * WINDOW, 1)
    third = pltpu.roll(first, 4 * WINDOW, 1)
    lane = iota((128, 128), 1)
    nothing = jnp.zeros((128, 128), BF16)
    weights[pl.ds(0, 128), pl.ds(0, 128)] = first.astype(BF16)
    weights[pl.ds(0, 128), pl.ds(128, 128)] = nothing
    weights[pl.ds(128, 128), pl.ds(0, 128)] = second.astype(BF16)
    weights[pl.ds(128, 128), pl.ds(128, 128)] = nothing
    weights[pl.ds(256, 128), pl.ds(0, 128)] = jnp.where(lane >= 4 * WINDOW, third, 0.0).astype(BF16)
    weights[pl.ds(256, 128), pl.ds(128, 128)] = jnp.where(lane < 2 * WINDOW, third, 0.0).astype(BF16)

    def compute(s):
        base = ((z + z_step(s)) % nz) * chunk
        lanes = chunk_lanes(z, s)
        drain(low.at[:, :, :, lanes], halo_recv_sem.at[0, s])
        drain(high.at[:, :, :, lanes], halo_recv_sem.at[1, s])
        matrix = weights[...][:, :3 * 2 * WINDOW]
        for chip in range(nx):
            lanes = pl.ds(pl.multiple_of(base + chip * 256, 256), 256)
            total_real = jnp.zeros((FRAMES, 256), F32)
            total_imag = jnp.zeros((FRAMES, 256), F32)
            window = []
            for c in range(3):
                for i in range(2):
                    window += [low[i, c, :, lanes].astype(F32), mid[i, c, :, lanes], high[i, c, :, lanes].astype(F32)]
            window = jnp.concatenate(window, axis=0).astype(BF16)
            adjoint = jnp.dot(matrix, window, preferred_element_type=F32)
            for c in range(3):
                for e in range(PER_GROUP):
                    mid_real = mid[0, c, pl.ds(e, 1), lanes]
                    mid_imag = mid[1, c, pl.ds(e, 1), lanes]
                    at = c * 128 + e * 8
                    adj_real = adjoint[at:at + 8]
                    adj_imag = adjoint[at + 64:at + 72]
                    total_real = total_real + mid_real * adj_real + mid_imag * adj_imag
                    total_imag = total_imag + mid_real * adj_imag - mid_imag * adj_real
            for k in range(2):
                part[s, k, chip, pl.ds(0, 8), :] = total_real[:, k * 128:(k + 1) * 128]
                part[s, k, chip, pl.ds(8, 8), :] = total_imag[:, k * 128:(k + 1) * 128]
        send(part.at[s, 1 - core], core_recv.at[s], core_send_sem, core_recv_sem.at[s], core_peer)

    def add_core(s):
        drain(core_recv.at[s], core_recv_sem.at[s])
        x_send[s] = part[s, core] + core_recv[s]
        for d in range(1, nx):
            send(x_send.at[s, (x + d) % nx], x_recv.at[s, d - 1], x_send_sem, x_recv_sem.at[s], x_peer(d))

    def add_x(s):
        drain(x_recv.at[s], x_recv_sem.at[s])
        total = x_send[s, x]
        for d in range(nx - 1):
            total = total + x_recv[s, d]
        return total

    def pass_z(s):
        z_send[s] = add_x(s)
        send(z_send.at[s], z_recv.at[s], z_send_sem, z_recv_sem, z_peer(z_step(s)))

    core_lag = 2
    x_lag = 5

    def step(s, carry):
        @pl.when(s < nz)
        def _():
            compute(s)

        @pl.when((s >= core_lag) & (s < nz + core_lag))
        def _():
            add_core(s - core_lag)

        @pl.when((s >= x_lag) & (s < nz - 1 + x_lag))
        def _():
            pass_z(s - x_lag)

        return carry

    lax.fori_loop(0, nz - 1 + x_lag, step, 0)
    total = add_x(nz - 1)
    drain(z_recv, z_recv_sem)
    for s in range(nz - 1):
        total = total + z_recv[s]
    out[pl.ds(0, FRAMES, stride=2), :] = total[0:8]
    out[pl.ds(1, FRAMES, stride=2), :] = total[8:16]

    drain(low, halo_send_sem.at[0])
    drain(high, halo_send_sem.at[1])
    drain(arrived, stage_send_sem.at[0])
    drain(b_buf.at[pl.ds(0, (nz - 1) * lines)], stage_send_sem.at[1])
    drain(c_buf, stage_send_sem.at[2])
    drain(core_recv, core_send_sem)
    drain(x_recv, x_send_sem)
    drain(z_recv, z_send_sem)


def local(fields, residual, quad_group, offsets, b_step, sides):
    groups = lax.axis_size("elec")
    ny = lax.axis_size("cell")
    nx = X_CHIPS
    lines = 2 * nx
    nz = groups // lines
    cells = fields.shape[3]
    count = residual.shape[0]
    resid = jnp.transpose(residual, (1, 2, 0)).reshape(2 * FRAMES, count)
    vmem = pl.BlockSpec(memory_space=pltpu.VMEM)
    field_shape = (2, 3, PER_GROUP, cells)
    dma = pltpu.SemaphoreType.DMA
    gradient = pl.pallas_call(
        functools.partial(kernel, (nz, nx, ny)),
        out_shape=jax.ShapeDtypeStruct((2 * FRAMES, 128), F32),
        in_specs=[pl.BlockSpec(memory_space=pltpu.HBM)] * 6,
        out_specs=vmem,
        scratch_shapes=[
            pltpu.VMEM((2 * FRAMES, count), F32),
            pltpu.VMEM((1, count), jnp.int32),
            pltpu.VMEM((3, count), jnp.int32),
            pltpu.VMEM((1, count), jnp.int32),
            pltpu.VMEM((2, count), jnp.int32),
            pltpu.VMEM(field_shape, BF16),
            pltpu.VMEM(field_shape, BF16),
            pltpu.VMEM(field_shape, BF16),
            pltpu.VMEM(field_shape, F32),
            pltpu.VMEM((lines, nz, 128), F32),
            pltpu.VMEM((groups, 128), F32),
            pltpu.VMEM((nz, lines, 128), F32),
            pltpu.VMEM((64, 128), F32),
            pltpu.VMEM((WINDOW, 128), F32),
            pltpu.VMEM((ny - 1, WINDOW, 128), F32),
            pltpu.VMEM((384, 256), BF16),
            pltpu.VMEM((nz, 2, nx, 16, 128), F32),
            pltpu.VMEM((nz, nx, 16, 128), F32),
            pltpu.VMEM((nz, nx, 16, 128), F32),
            pltpu.VMEM((nz, nx - 1, 16, 128), F32),
            pltpu.VMEM((nz, 16, 128), F32),
            pltpu.VMEM((nz - 1, 16, 128), F32),
            dma((5,)), dma, dma((2,)), dma((2, nz)),
            dma((3,)), dma((3,)),
            dma, dma((nz,)), dma, dma((nz,)), dma, dma,
        ],
        compiler_params=pltpu.CompilerParams(
            collective_id=0, has_side_effects=True, vmem_limit_bytes=63 * 1024 * 1024
        ),
    )(fields, resid, quad_group.T, offsets.T, b_step.T, sides.T)
    return gradient.reshape(FRAMES, 2, 1, 128)


def solution(mesh):
    return jax.shard_map(
        local,
        mesh=mesh,
        in_specs=(
            P(None, None, "elec", "cell"),
            P(("elec", "cell"), None, None),
            P(("elec", "cell"), None),
            P(("elec", "cell"), None),
            P(("elec", "cell"), None),
            P(("elec", "cell"), None),
        ),
        out_specs=P(None, None, "cell", "elec"),
        check_vma=False,
    )
```

```python
import functools

import jax
import jax.numpy as jnp
from jax import lax
from jax.experimental import pallas as pl
from jax.experimental.pallas import tpu as pltpu
from jax.sharding import PartitionSpec as P

X_CHIPS = 4
PER_GROUP = 8
FRAMES = 8
CAP = 4
SLOT = 32
WINDOW = 3 * PER_GROUP
F32 = jnp.float32
BF16 = jnp.bfloat16


def iota(shape, dim):
    return lax.broadcasted_iota(jnp.int32, shape, dim)


def split3(value):
    high = value.astype(BF16)
    rest = value - high.astype(F32)
    middle = rest.astype(BF16)
    low = (rest - middle.astype(F32)).astype(BF16)
    return high, middle, low


def dot_nt(left, right):
    return lax.dot_general(left, right, (((1,), (1,)), ((), ())), preferred_element_type=F32)


def drain(ref, sem):
    pltpu.make_async_copy(ref, ref, sem).wait()


def kernel(
    sizes,
    fields, resid_in, group_in, offs_in, bstep_in, sides_in,
    out,
    resid, group, offs, bstep, sides,
    own, low, high,
    slots, a_buf, b_send, b_buf, c_send, c_buf, weights,
    part, core_recv, sums, shares,
    in_sem, own_sem, halo_send_sem, halo_recv_sem,
    stage_send_sem, stage_recv_sem,
    core_send_sem, core_recv_sem, share_send_sem, share_recv_sem,
):
    nz, nx, ny = sizes
    lines = 2 * nx
    groups = nz * lines
    quads = resid.shape[1]
    halo_ends = (nz // 4, nz // 2)
    elec = lax.axis_index("elec")
    cell = lax.axis_index("cell")
    z = elec // lines
    p = elec % lines
    x = p // 2
    core = p % 2

    inputs = [
        pltpu.make_async_copy(source, target, in_sem.at[number])
        for number, (source, target) in enumerate(
            zip((resid_in, group_in, offs_in, bstep_in, sides_in), (resid, group, offs, bstep, sides))
        )
    ]
    for copy in inputs:
        copy.start()

    def line_peer(d):
        return {"elec": z * lines + (p + d) % lines}

    def z_peer(d):
        return {"elec": ((z + d) % nz) * lines + p}

    def chip_peer(dz, dx):
        return {"elec": ((z + dz) % nz) * lines + ((x + dx) % nx) * 2 + core}

    def y_peer(d):
        return {"cell": (cell + d) % ny}

    core_peer = {"elec": z * lines + x * 2 + 1 - core}
    next_peer = {"elec": (elec + 1) % groups}
    prev_peer = {"elec": (elec + groups - 1) % groups}

    if groups < 64:
        b_buf[...] = jnp.zeros_like(b_buf)
    barrier = pltpu.get_barrier_semaphore()
    peers = (
        [line_peer(d) for d in range(1, lines)]
        + [chip_peer(dz, dx) for dz in range(1, nz) for dx in range(nx)]
        + [y_peer(d) for d in range(1, ny)]
        + [next_peer, prev_peer]
    )
    for peer in peers:
        pl.semaphore_signal(barrier, inc=1, device_id=peer, device_id_type=pl.DeviceIdType.MESH)

    own_copy = pltpu.make_async_copy(fields, own, own_sem)
    own_copy.start()

    def send(source, target, send_sem, recv_sem, peer):
        pltpu.make_async_remote_copy(
            src_ref=source, dst_ref=target, send_sem=send_sem, recv_sem=recv_sem,
            device_id=peer, device_id_type=pl.DeviceIdType.MESH,
        ).start()

    def z_step(s):
        return nz // 2 + (1 - 2 * (s % 2)) * ((s + 1) // 2)

    chunk = lines * 128

    def chunk_lanes(row, s):
        return pl.ds(pl.multiple_of(((row + z_step(s)) % nz) * chunk, chunk), chunk)

    def send_halo(s):
        for way, (peer, target, turn) in enumerate(((next_peer, low, 1), (prev_peer, high, groups - 1))):
            lanes = chunk_lanes((elec + turn) % groups // lines, s)
            send(fields.at[:, :, :, lanes], target.at[:, :, :, lanes],
                 halo_send_sem.at[way], halo_recv_sem.at[way, s], peer)

    for copy in inputs:
        copy.wait()
    owner = group[...]
    source_a = offs[pl.ds(0, 1), :]
    source_b = (source_a + bstep[...]) % PER_GROUP
    group_m = jnp.clip(owner + sides[pl.ds(0, 1), :], 0, groups - 1)
    group_n = jnp.clip(owner + sides[pl.ds(1, 1), :], 0, groups - 1)
    column_m = (group_m - owner + 1) * PER_GROUP + offs[pl.ds(1, 1), :]
    column_n = (group_n - owner + 1) * PER_GROUP + offs[pl.ds(2, 1), :]
    row = iota((groups, quads), 0)
    names = (row % nz) * lines + row // nz
    member = jnp.where(names == owner, 1.0, 0.0).astype(F32)
    earlier = jnp.where(iota((quads, quads), 0) < iota((quads, quads), 1), 1.0, 0.0).astype(BF16)
    before = jnp.dot(member.astype(BF16), earlier, preferred_element_type=F32)
    rank = jnp.sum(member * before, axis=0, keepdims=True)
    place = iota((8, quads), 0)
    indices = jnp.where(
        place == 0, source_a,
        jnp.where(place == 1, source_b, jnp.where(place == 2, column_m, jnp.where(place == 3, column_n, 0))),
    ).astype(F32)
    real = -resid[pl.ds(0, FRAMES, stride=2), :]
    imag = -resid[pl.ds(1, FRAMES, stride=2), :]
    entry = jnp.concatenate([real, imag, indices, jnp.zeros_like(indices)], axis=0)
    entries = jnp.concatenate(
        [jnp.where(rank == float(k), entry, 0.0) for k in range(CAP)], axis=0
    )
    named = member.astype(BF16)
    sorted_rows = sum(dot_nt(named, piece) for piece in split3(entries)[::-1])
    for line in range(lines):
        slots[line] = sorted_rows[line * nz:(line + 1) * nz, :]

    pl.semaphore_wait(barrier, len(peers))

    for d in range(1, lines):
        send(slots.at[(p + d) % lines], a_buf.at[pl.ds((d - 1) * nz, nz)],
             stage_send_sem.at[0], stage_recv_sem.at[0], line_peer(d))
    for s in range(0, halo_ends[0]):
        send_halo(s)
    a_buf[pl.ds((lines - 1) * nz, nz), :] = slots[p]
    own_copy.wait()
    arrived = a_buf.at[pl.ds(0, (lines - 1) * nz)]
    drain(arrived, stage_recv_sem.at[0])
    for to in range(nz):
        b_send[to] = a_buf[pl.ds(to, lines, stride=nz), :]
    for d in range(1, nz):
        send(b_send.at[(z + d) % nz], b_buf.at[pl.ds((d - 1) * lines, lines)],
             stage_send_sem.at[1], stage_recv_sem.at[1], z_peer(d))
    for s in range(halo_ends[0], halo_ends[1]):
        send_halo(s)
    b_buf[pl.ds((nz - 1) * lines, lines), :] = b_send[z]
    drain(b_buf.at[pl.ds(0, (nz - 1) * lines)], stage_recv_sem.at[1])

    received = b_buf[...]
    both = jnp.concatenate([received, pltpu.roll(received, 64, 1)], axis=0)
    turned = both.T
    terms = []
    columns = []
    for half in range(2):
        block = turned[half * SLOT:(half + 1) * SLOT, :]
        at_a = block[16:17].astype(jnp.int32)
        at_b = block[17:18].astype(jnp.int32)
        at_m = block[18:19].astype(jnp.int32)
        at_n = block[19:20].astype(jnp.int32)
        place = iota((PER_GROUP, 128), 0)
        sign = jnp.where(place == at_a, 1.0, 0.0) - jnp.where(place == at_b, 1.0, 0.0)
        terms.append(jnp.concatenate([block[k:k + 1] * sign for k in range(2 * FRAMES)], axis=0))
        place = iota((WINDOW, 128), 0)
        columns.append((jnp.where(place == at_m, 1.0, 0.0) - jnp.where(place == at_n, 1.0, 0.0)).astype(BF16))
    band = jnp.zeros((WINDOW, 128), F32)
    for half in range(2):
        for piece in split3(terms[half])[::-1]:
            band = band + dot_nt(columns[half], piece)
    c_send[...] = band
    for d in range(1, ny):
        send(c_send, c_buf.at[d - 1], stage_send_sem.at[2], stage_recv_sem.at[2], y_peer(d))
    for s in range(halo_ends[1], nz):
        send_halo(s)
    drain(c_buf, stage_recv_sem.at[2])
    for d in range(ny - 1):
        band = band + c_buf[d]
    band = band.astype(BF16).astype(F32)
    upper = jnp.concatenate([band, jnp.zeros((128 - WINDOW, 128), F32)], axis=0).T
    lower = jnp.concatenate([upper[64:], -upper[:64]], axis=0)
    first = upper + pltpu.roll(lower, WINDOW, 1)
    second = pltpu.roll(first, 2 * WINDOW, 1)
    third = pltpu.roll(first, 4 * WINDOW, 1)
    lane = iota((128, 128), 1)
    nothing = jnp.zeros((128, 128), BF16)
    weights[pl.ds(0, 128), pl.ds(0, 128)] = first.astype(BF16)
    weights[pl.ds(0, 128), pl.ds(128, 128)] = nothing
    weights[pl.ds(128, 128), pl.ds(0, 128)] = second.astype(BF16)
    weights[pl.ds(128, 128), pl.ds(128, 128)] = nothing
    weights[pl.ds(256, 128), pl.ds(0, 128)] = jnp.where(lane >= 4 * WINDOW, third, 0.0).astype(BF16)
    weights[pl.ds(256, 128), pl.ds(128, 128)] = jnp.where(lane < 2 * WINDOW, third, 0.0).astype(BF16)

    sublane = iota((PER_GROUP, 128), 0)

    def fold(first, second, width):
        keep = sublane % (2 * width) < width
        return jnp.where(keep, first, second) + pltpu.roll(
            jnp.where(keep, second, first), PER_GROUP - width, 0
        )

    def collect(rows):
        for width in (1, 2, 4):
            rows = [fold(rows[k], rows[k + 1], width) for k in range(0, len(rows), 2)]
        return rows[0]

    def compute(s):
        base = ((z + z_step(s)) % nz) * chunk
        arrived_lanes = chunk_lanes(z, s)
        drain(low.at[:, :, :, arrived_lanes], halo_recv_sem.at[0, s])
        drain(high.at[:, :, :, arrived_lanes], halo_recv_sem.at[1, s])
        matrix = weights[...][:, :3 * 2 * WINDOW]
        for chip in range(nx):
            lanes = pl.ds(pl.multiple_of(base + chip * 256, 256), 256)
            middle = [[own[i, c, :, lanes].astype(F32) for i in range(2)] for c in range(3)]
            window = []
            for c in range(3):
                for i in range(2):
                    window += [low[i, c, :, lanes].astype(F32), middle[c][i], high[i, c, :, lanes].astype(F32)]
            window = jnp.concatenate(window, axis=0).astype(BF16)
            adjoint = jnp.dot(matrix, window, preferred_element_type=F32)
            for k in range(2):
                half = slice(k * 128, (k + 1) * 128)
                real = []
                imag = []
                for t in range(FRAMES):
                    total_real = jnp.zeros((PER_GROUP, 128), F32)
                    total_imag = jnp.zeros((PER_GROUP, 128), F32)
                    for c in range(3):
                        at = c * 128 + t * 8
                        adj_real = adjoint[at:at + 8, half]
                        adj_imag = adjoint[at + 64:at + 72, half]
                        mid_real = middle[c][0][:, half]
                        mid_imag = middle[c][1][:, half]
                        total_real = total_real + mid_real * adj_real + mid_imag * adj_imag
                        total_imag = total_imag + mid_real * adj_imag - mid_imag * adj_real
                    real.append(total_real)
                    imag.append(total_imag)
                part[s, k, chip, pl.ds(0, 8), :] = collect(real)
                part[s, k, chip, pl.ds(8, 8), :] = collect(imag)
        send(part.at[s, 1 - core], core_recv.at[s], core_send_sem, core_recv_sem.at[s], core_peer)

    def share(s, d):
        send(sums.at[s, (x + d) % nx], shares.at[s * nx + (d + nx - 1) % nx],
             share_send_sem, share_recv_sem.at[s], chip_peer(z_step(s), d))

    def add_core(s):
        drain(core_recv.at[s], core_recv_sem.at[s])
        sums[s] = part[s, core] + core_recv[s]
        for d in range(1, nx):
            share(s, d)

        @pl.when(s < nz - 1)
        def _():
            share(s, 0)

    core_lag = 2

    def step(s, carry):
        @pl.when(s < nz)
        def _():
            compute(s)

        @pl.when(s >= core_lag)
        def _():
            add_core(s - core_lag)

        return carry

    lax.fori_loop(0, nz + core_lag, step, 0)
    total = sums[nz - 1, x]
    for s in range(nz):
        count = nx if s < nz - 1 else nx - 1
        drain(shares.at[pl.ds(s * nx, count)], share_recv_sem.at[s])
        for d in range(count):
            total = total + shares[s * nx + d]
    out[pl.ds(0, FRAMES, stride=2), :] = total[0:8]
    out[pl.ds(1, FRAMES, stride=2), :] = total[8:16]

    drain(low, halo_send_sem.at[0])
    drain(high, halo_send_sem.at[1])
    drain(arrived, stage_send_sem.at[0])
    drain(b_buf.at[pl.ds(0, (nz - 1) * lines)], stage_send_sem.at[1])
    drain(c_buf, stage_send_sem.at[2])
    drain(core_recv, core_send_sem)
    drain(shares.at[pl.ds(0, nz * nx - 1)], share_send_sem)


def local(fields, residual, quad_group, offsets, b_step, sides):
    groups = lax.axis_size("elec")
    ny = lax.axis_size("cell")
    nx = X_CHIPS
    lines = 2 * nx
    nz = groups // lines
    cells = fields.shape[3]
    count = residual.shape[0]
    resid = jnp.transpose(residual, (1, 2, 0)).reshape(2 * FRAMES, count)
    vmem = pl.BlockSpec(memory_space=pltpu.VMEM)
    field_shape = (2, 3, PER_GROUP, cells)
    dma = pltpu.SemaphoreType.DMA
    gradient = pl.pallas_call(
        functools.partial(kernel, (nz, nx, ny)),
        out_shape=jax.ShapeDtypeStruct((2 * FRAMES, 128), F32),
        in_specs=[pl.BlockSpec(memory_space=pltpu.HBM)] * 6,
        out_specs=vmem,
        scratch_shapes=[
            pltpu.VMEM((2 * FRAMES, count), F32),
            pltpu.VMEM((1, count), jnp.int32),
            pltpu.VMEM((3, count), jnp.int32),
            pltpu.VMEM((1, count), jnp.int32),
            pltpu.VMEM((2, count), jnp.int32),
            pltpu.VMEM(field_shape, BF16),
            pltpu.VMEM(field_shape, BF16),
            pltpu.VMEM(field_shape, BF16),
            pltpu.VMEM((lines, nz, 128), F32),
            pltpu.VMEM((groups, 128), F32),
            pltpu.VMEM((nz, lines, 128), F32),
            pltpu.VMEM((64, 128), F32),
            pltpu.VMEM((WINDOW, 128), F32),
            pltpu.VMEM((ny - 1, WINDOW, 128), F32),
            pltpu.VMEM((384, 256), BF16),
            pltpu.VMEM((nz, 2, nx, 16, 128), F32),
            pltpu.VMEM((nz, nx, 16, 128), F32),
            pltpu.VMEM((nz, nx, 16, 128), F32),
            pltpu.VMEM((nz * nx, 16, 128), F32),
            dma((5,)), dma, dma((2,)), dma((2, nz)),
            dma((3,)), dma((3,)),
            dma, dma((nz,)), dma, dma((nz,)),
        ],
        compiler_params=pltpu.CompilerParams(
            collective_id=0, has_side_effects=True, vmem_limit_bytes=40 * 1024 * 1024
        ),
    )(*(
        pltpu.with_memory_space_constraint(value, pltpu.HBM)
        for value in (fields, resid, quad_group.T, offsets.T, b_step.T, sides.T)
    ))
    return gradient.reshape(FRAMES, 2, 1, 128)


def solution(mesh):
    return jax.shard_map(
        local,
        mesh=mesh,
        in_specs=(
            P(None, None, "elec", "cell"),
            P(("elec", "cell"), None, None),
            P(("elec", "cell"), None),
            P(("elec", "cell"), None),
            P(("elec", "cell"), None),
            P(("elec", "cell"), None),
        ),
        out_specs=P(None, None, "cell", "elec"),
        check_vma=False,
    )
```

```python
import functools

import jax
import jax.numpy as jnp
from jax import lax
from jax.experimental import pallas as pl
from jax.experimental.pallas import tpu as pltpu
from jax.sharding import PartitionSpec as P

X_CHIPS = 4
PER_GROUP = 8
FRAMES = 8
CAP = 4
SLOT = 32
WINDOW = 3 * PER_GROUP
F32 = jnp.float32
BF16 = jnp.bfloat16


def iota(shape, dim):
    return lax.broadcasted_iota(jnp.int32, shape, dim)


def split3(value):
    high = value.astype(BF16)
    rest = value - high.astype(F32)
    middle = rest.astype(BF16)
    low = (rest - middle.astype(F32)).astype(BF16)
    return high, middle, low


def dot_nt(left, right):
    return lax.dot_general(left, right, (((1,), (1,)), ((), ())), preferred_element_type=F32)


def drain(ref, sem):
    pltpu.make_async_copy(ref, ref, sem).wait()


def kernel(
    sizes,
    fields, resid_in, group_in, offs_in, bstep_in, sides_in,
    out,
    resid, group, offs, bstep, sides,
    own, low, high,
    slots, a_buf, b_send, b_buf, c_send, c_buf, weights,
    part, core_recv, sums, rounded, shares,
    in_sem, own_sem, halo_send_sem, halo_recv_sem,
    stage_send_sem, stage_recv_sem,
    core_send_sem, core_recv_sem, share_send_sem, share_recv_sem,
):
    nz, nx, ny = sizes
    lines = 2 * nx
    groups = nz * lines
    quads = resid.shape[1]
    halo_ends = (0, 3 * nz // 8)
    elec = lax.axis_index("elec")
    cell = lax.axis_index("cell")
    z = elec // lines
    p = elec % lines
    x = p // 2
    core = p % 2

    inputs = [
        pltpu.make_async_copy(source, target, in_sem.at[number])
        for number, (source, target) in enumerate(
            zip((resid_in, group_in, offs_in, bstep_in, sides_in), (resid, group, offs, bstep, sides))
        )
    ]
    for copy in inputs:
        copy.start()

    def line_peer(d):
        return {"elec": z * lines + (p + d) % lines}

    def z_peer(d):
        return {"elec": ((z + d) % nz) * lines + p}

    def chip_peer(dz, dx):
        return {"elec": ((z + dz) % nz) * lines + ((x + dx) % nx) * 2 + core}

    def y_peer(d):
        return {"cell": (cell + d) % ny}

    core_peer = {"elec": z * lines + x * 2 + 1 - core}
    next_peer = {"elec": (elec + 1) % groups}
    prev_peer = {"elec": (elec + groups - 1) % groups}

    if groups < 64:
        b_buf[...] = jnp.zeros_like(b_buf)
    barrier = pltpu.get_barrier_semaphore()
    peers = (
        [line_peer(d) for d in range(1, lines)]
        + [chip_peer(dz, dx) for dz in range(1, nz) for dx in range(nx)]
        + [y_peer(d) for d in range(1, ny)]
        + [next_peer, prev_peer]
    )
    for peer in peers:
        pl.semaphore_signal(barrier, inc=1, device_id=peer, device_id_type=pl.DeviceIdType.MESH)

    own_copy = pltpu.make_async_copy(fields, own, own_sem)
    own_copy.start()

    def send(source, target, send_sem, recv_sem, peer):
        pltpu.make_async_remote_copy(
            src_ref=source, dst_ref=target, send_sem=send_sem, recv_sem=recv_sem,
            device_id=peer, device_id_type=pl.DeviceIdType.MESH,
        ).start()

    def z_step(s):
        return nz // 2 + (1 - 2 * (s % 2)) * ((s + 1) // 2)

    chunk = lines * 128

    def chunk_lanes(row, s):
        return pl.ds(pl.multiple_of(((row + z_step(s)) % nz) * chunk, chunk), chunk)

    def send_halo(s):
        for way, (peer, target, turn) in enumerate(((next_peer, low, 1), (prev_peer, high, groups - 1))):
            lanes = chunk_lanes((elec + turn) % groups // lines, s)
            send(fields.at[:, :, :, lanes], target.at[:, :, :, lanes],
                 halo_send_sem.at[way], halo_recv_sem.at[way, s], peer)

    for copy in inputs:
        copy.wait()
    owner = group[...]
    source_a = offs[pl.ds(0, 1), :]
    source_b = (source_a + bstep[...]) % PER_GROUP
    group_m = jnp.clip(owner + sides[pl.ds(0, 1), :], 0, groups - 1)
    group_n = jnp.clip(owner + sides[pl.ds(1, 1), :], 0, groups - 1)
    column_m = (group_m - owner + 1) * PER_GROUP + offs[pl.ds(1, 1), :]
    column_n = (group_n - owner + 1) * PER_GROUP + offs[pl.ds(2, 1), :]
    row = iota((groups, quads), 0)
    names = (row % nz) * lines + row // nz
    member = jnp.where(names == owner, 1.0, 0.0).astype(F32)
    earlier = jnp.where(iota((quads, quads), 0) < iota((quads, quads), 1), 1.0, 0.0).astype(BF16)
    before = jnp.dot(member.astype(BF16), earlier, preferred_element_type=F32)
    rank = jnp.sum(member * before, axis=0, keepdims=True)
    place = iota((8, quads), 0)
    indices = jnp.where(
        place == 0, source_a,
        jnp.where(place == 1, source_b, jnp.where(place == 2, column_m, jnp.where(place == 3, column_n, 0))),
    ).astype(F32)
    real = -resid[pl.ds(0, FRAMES, stride=2), :]
    imag = -resid[pl.ds(1, FRAMES, stride=2), :]
    entry = jnp.concatenate([real, imag, indices, jnp.zeros_like(indices)], axis=0)
    entries = jnp.concatenate(
        [jnp.where(rank == float(k), entry, 0.0) for k in range(CAP)], axis=0
    )
    named = member.astype(BF16)
    sorted_rows = sum(dot_nt(named, piece) for piece in split3(entries)[::-1])
    for line in range(lines):
        slots[line] = sorted_rows[line * nz:(line + 1) * nz, :]

    pl.semaphore_wait(barrier, len(peers))

    for d in range(1, lines):
        send(slots.at[(p + d) % lines], a_buf.at[pl.ds((d - 1) * nz, nz)],
             stage_send_sem.at[0], stage_recv_sem.at[0], line_peer(d))
    for s in range(0, halo_ends[0]):
        send_halo(s)
    a_buf[pl.ds((lines - 1) * nz, nz), :] = slots[p]
    own_copy.wait()
    arrived = a_buf.at[pl.ds(0, (lines - 1) * nz)]
    drain(arrived, stage_recv_sem.at[0])
    for to in range(nz):
        b_send[to] = a_buf[pl.ds(to, lines, stride=nz), :]
    for d in range(1, nz):
        send(b_send.at[(z + d) % nz], b_buf.at[pl.ds((d - 1) * lines, lines)],
             stage_send_sem.at[1], stage_recv_sem.at[1], z_peer(d))
    for s in range(halo_ends[0], halo_ends[1]):
        send_halo(s)
    b_buf[pl.ds((nz - 1) * lines, lines), :] = b_send[z]
    drain(b_buf.at[pl.ds(0, (nz - 1) * lines)], stage_recv_sem.at[1])

    received = b_buf[...]
    both = jnp.concatenate([received, pltpu.roll(received, 64, 1)], axis=0)
    turned = both.T
    terms = []
    columns = []
    for half in range(2):
        block = turned[half * SLOT:(half + 1) * SLOT, :]
        at_a = block[16:17].astype(jnp.int32)
        at_b = block[17:18].astype(jnp.int32)
        at_m = block[18:19].astype(jnp.int32)
        at_n = block[19:20].astype(jnp.int32)
        place = iota((PER_GROUP, 128), 0)
        sign = jnp.where(place == at_a, 1.0, 0.0) - jnp.where(place == at_b, 1.0, 0.0)
        terms.append(jnp.concatenate([block[k:k + 1] * sign for k in range(2 * FRAMES)], axis=0))
        place = iota((WINDOW, 128), 0)
        columns.append((jnp.where(place == at_m, 1.0, 0.0) - jnp.where(place == at_n, 1.0, 0.0)).astype(BF16))
    band = jnp.zeros((WINDOW, 128), F32)
    for half in range(2):
        for piece in split3(terms[half])[::-1]:
            band = band + dot_nt(columns[half], piece)
    c_send[...] = band
    for d in range(1, ny):
        send(c_send, c_buf.at[d - 1], stage_send_sem.at[2], stage_recv_sem.at[2], y_peer(d))
    for s in range(halo_ends[1], nz):
        send_halo(s)
    drain(c_buf, stage_recv_sem.at[2])
    for d in range(ny - 1):
        band = band + c_buf[d]
    band = band.astype(BF16).astype(F32)
    upper = jnp.concatenate([band, jnp.zeros((128 - WINDOW, 128), F32)], axis=0).T
    lower = jnp.concatenate([upper[64:], -upper[:64]], axis=0)
    first = upper + pltpu.roll(lower, WINDOW, 1)
    second = pltpu.roll(first, 2 * WINDOW, 1)
    third = pltpu.roll(first, 4 * WINDOW, 1)
    lane = iota((128, 128), 1)
    nothing = jnp.zeros((128, 128), BF16)
    weights[pl.ds(0, 128), pl.ds(0, 128)] = first.astype(BF16)
    weights[pl.ds(0, 128), pl.ds(128, 128)] = nothing
    weights[pl.ds(128, 128), pl.ds(0, 128)] = second.astype(BF16)
    weights[pl.ds(128, 128), pl.ds(128, 128)] = nothing
    weights[pl.ds(256, 128), pl.ds(0, 128)] = jnp.where(lane >= 4 * WINDOW, third, 0.0).astype(BF16)
    weights[pl.ds(256, 128), pl.ds(128, 128)] = jnp.where(lane < 2 * WINDOW, third, 0.0).astype(BF16)

    sublane = iota((PER_GROUP, 128), 0)

    def fold(first, second, width):
        keep = sublane % (2 * width) < width
        return jnp.where(keep, first, second) + pltpu.roll(
            jnp.where(keep, second, first), PER_GROUP - width, 0
        )

    def collect(rows):
        for width in (1, 2, 4):
            rows = [fold(rows[k], rows[k + 1], width) for k in range(0, len(rows), 2)]
        return rows[0]

    def compute(s):
        base = ((z + z_step(s)) % nz) * chunk
        arrived_lanes = chunk_lanes(z, s)
        drain(low.at[:, :, :, arrived_lanes], halo_recv_sem.at[0, s])
        drain(high.at[:, :, :, arrived_lanes], halo_recv_sem.at[1, s])
        matrix = weights[...][:, :3 * 2 * WINDOW]
        for chip in range(nx):
            lanes = pl.ds(pl.multiple_of(base + chip * 256, 256), 256)
            middle = [[own[i, c, :, lanes].astype(F32) for i in range(2)] for c in range(3)]
            window = []
            for c in range(3):
                for i in range(2):
                    window += [low[i, c, :, lanes].astype(F32), middle[c][i], high[i, c, :, lanes].astype(F32)]
            window = jnp.concatenate(window, axis=0).astype(BF16)
            adjoint = jnp.dot(matrix, window, preferred_element_type=F32)
            for k in range(2):
                half = slice(k * 128, (k + 1) * 128)
                real = []
                imag = []
                for t in range(FRAMES):
                    total_real = jnp.zeros((PER_GROUP, 128), F32)
                    total_imag = jnp.zeros((PER_GROUP, 128), F32)
                    for c in range(3):
                        at = c * 128 + t * 8
                        adj_real = adjoint[at:at + 8, half]
                        adj_imag = adjoint[at + 64:at + 72, half]
                        mid_real = middle[c][0][:, half]
                        mid_imag = middle[c][1][:, half]
                        total_real = total_real + mid_real * adj_real + mid_imag * adj_imag
                        total_imag = total_imag + mid_real * adj_imag - mid_imag * adj_real
                    real.append(total_real)
                    imag.append(total_imag)
                part[s, k, chip, pl.ds(0, 8), :] = collect(real)
                part[s, k, chip, pl.ds(8, 8), :] = collect(imag)
        send(part.at[s, 1 - core], core_recv.at[s], core_send_sem, core_recv_sem.at[s], core_peer)

    def share(s, d):
        send(rounded.at[s, (x + d) % nx], shares.at[s * nx + (d + nx - 1) % nx],
             share_send_sem, share_recv_sem.at[s], chip_peer(z_step(s), d))

    def add_core(s):
        drain(core_recv.at[s], core_recv_sem.at[s])
        both_cores = part[s, core] + core_recv[s]
        sums[s] = both_cores
        rounded[s] = both_cores.astype(BF16)
        for d in range(1, nx):
            share(s, d)

        @pl.when(s < nz - 1)
        def _():
            share(s, 0)

    core_lag = 2

    def step(s, carry):
        @pl.when(s < nz)
        def _():
            compute(s)

        @pl.when(s >= core_lag)
        def _():
            add_core(s - core_lag)

        return carry

    lax.fori_loop(0, nz + core_lag, step, 0)
    total = sums[nz - 1, x]
    for s in range(nz):
        count = nx if s < nz - 1 else nx - 1
        drain(shares.at[pl.ds(s * nx, count)], share_recv_sem.at[s])
        for d in range(count):
            total = total + shares[s * nx + d].astype(F32)
    out[pl.ds(0, FRAMES, stride=2), :] = total[0:8]
    out[pl.ds(1, FRAMES, stride=2), :] = total[8:16]

    drain(low, halo_send_sem.at[0])
    drain(high, halo_send_sem.at[1])
    drain(arrived, stage_send_sem.at[0])
    drain(b_buf.at[pl.ds(0, (nz - 1) * lines)], stage_send_sem.at[1])
    drain(c_buf, stage_send_sem.at[2])
    drain(core_recv, core_send_sem)
    drain(shares.at[pl.ds(0, nz * nx - 1)], share_send_sem)


def local(fields, residual, quad_group, offsets, b_step, sides):
    groups = lax.axis_size("elec")
    ny = lax.axis_size("cell")
    nx = X_CHIPS
    lines = 2 * nx
    nz = groups // lines
    cells = fields.shape[3]
    count = residual.shape[0]
    resid = jnp.transpose(residual, (1, 2, 0)).reshape(2 * FRAMES, count)
    vmem = pl.BlockSpec(memory_space=pltpu.VMEM)
    field_shape = (2, 3, PER_GROUP, cells)
    dma = pltpu.SemaphoreType.DMA
    gradient = pl.pallas_call(
        functools.partial(kernel, (nz, nx, ny)),
        out_shape=jax.ShapeDtypeStruct((2 * FRAMES, 128), F32),
        in_specs=[pl.BlockSpec(memory_space=pltpu.HBM)] * 6,
        out_specs=vmem,
        scratch_shapes=[
            pltpu.VMEM((2 * FRAMES, count), F32),
            pltpu.VMEM((1, count), jnp.int32),
            pltpu.VMEM((3, count), jnp.int32),
            pltpu.VMEM((1, count), jnp.int32),
            pltpu.VMEM((2, count), jnp.int32),
            pltpu.VMEM(field_shape, BF16),
            pltpu.VMEM(field_shape, BF16),
            pltpu.VMEM(field_shape, BF16),
            pltpu.VMEM((lines, nz, 128), F32),
            pltpu.VMEM((groups, 128), F32),
            pltpu.VMEM((nz, lines, 128), F32),
            pltpu.VMEM((64, 128), F32),
            pltpu.VMEM((WINDOW, 128), F32),
            pltpu.VMEM((ny - 1, WINDOW, 128), F32),
            pltpu.VMEM((384, 256), BF16),
            pltpu.VMEM((nz, 2, nx, 16, 128), F32),
            pltpu.VMEM((nz, nx, 16, 128), F32),
            pltpu.VMEM((nz, nx, 16, 128), F32),
            pltpu.VMEM((nz, nx, 16, 128), BF16),
            pltpu.VMEM((nz * nx, 16, 128), BF16),
            dma((5,)), dma, dma((2,)), dma((2, nz)),
            dma((3,)), dma((3,)),
            dma, dma((nz,)), dma, dma((nz,)),
        ],
        compiler_params=pltpu.CompilerParams(
            collective_id=0, has_side_effects=True, vmem_limit_bytes=40 * 1024 * 1024
        ),
    )(*(
        pltpu.with_memory_space_constraint(value, pltpu.HBM)
        for value in (fields, resid, quad_group.T, offsets.T, b_step.T, sides.T)
    ))
    return gradient.reshape(FRAMES, 2, 1, 128)


def solution(mesh):
    return jax.shard_map(
        local,
        mesh=mesh,
        in_specs=(
            P(None, None, "elec", "cell"),
            P(("elec", "cell"), None, None),
            P(("elec", "cell"), None),
            P(("elec", "cell"), None),
            P(("elec", "cell"), None),
            P(("elec", "cell"), None),
        ),
        out_specs=P(None, None, "cell", "elec"),
        check_vma=False,
    )
```

```python
import functools

import jax
import jax.numpy as jnp
from jax import lax
from jax.experimental import pallas as pl
from jax.experimental.pallas import tpu as pltpu
from jax.sharding import PartitionSpec as P

X_CHIPS = 4
PER_GROUP = 8
FRAMES = 8
CAP = 4
SLOT = 32
WINDOW = 3 * PER_GROUP
F32 = jnp.float32
BF16 = jnp.bfloat16


def iota(shape, dim):
    return lax.broadcasted_iota(jnp.int32, shape, dim)


def split3(value):
    high = value.astype(BF16)
    rest = value - high.astype(F32)
    middle = rest.astype(BF16)
    low = (rest - middle.astype(F32)).astype(BF16)
    return high, middle, low


def dot_nt(left, right):
    return lax.dot_general(left, right, (((1,), (1,)), ((), ())), preferred_element_type=F32)


def drain(ref, sem):
    pltpu.make_async_copy(ref, ref, sem).wait()


def kernel(
    sizes,
    fields, resid_in, group_in, offs_in, bstep_in, sides_in,
    out,
    resid, group, offs, bstep, sides,
    own, low, high,
    slots, a_buf, b_send, b_buf, c_send, c_buf, weights,
    part, core_recv, rounded, shares, near, near_shares,
    in_sem, own_sem, halo_send_sem, halo_recv_sem,
    stage_send_sem, stage_recv_sem,
    core_send_sem, core_recv_sem, share_send_sem, share_recv_sem, near_send_sem, near_recv_sem,
):
    nz, nx, ny = sizes
    lines = 2 * nx
    groups = nz * lines
    quads = resid.shape[1]
    halo_ends = (0, 3 * nz // 8)
    elec = lax.axis_index("elec")
    cell = lax.axis_index("cell")
    z = elec // lines
    p = elec % lines
    x = p // 2
    core = p % 2

    inputs = [
        pltpu.make_async_copy(source, target, in_sem.at[number])
        for number, (source, target) in enumerate(
            zip((resid_in, group_in, offs_in, bstep_in, sides_in), (resid, group, offs, bstep, sides))
        )
    ]
    for copy in inputs:
        copy.start()

    def line_peer(d):
        return {"elec": z * lines + (p + d) % lines}

    def z_peer(d):
        return {"elec": ((z + d) % nz) * lines + p}

    def chip_peer(dz, dx):
        return {"elec": ((z + dz) % nz) * lines + ((x + dx) % nx) * 2 + core}

    def y_peer(d):
        return {"cell": (cell + d) % ny}

    core_peer = {"elec": z * lines + x * 2 + 1 - core}
    next_peer = {"elec": (elec + 1) % groups}
    prev_peer = {"elec": (elec + groups - 1) % groups}

    if groups < 64:
        b_buf[...] = jnp.zeros_like(b_buf)
    barrier = pltpu.get_barrier_semaphore()
    peers = (
        [line_peer(d) for d in range(1, lines)]
        + [chip_peer(dz, dx) for dz in range(1, nz) for dx in range(nx)]
        + [y_peer(d) for d in range(1, ny)]
        + [next_peer, prev_peer]
    )
    for peer in peers:
        pl.semaphore_signal(barrier, inc=1, device_id=peer, device_id_type=pl.DeviceIdType.MESH)

    own_copy = pltpu.make_async_copy(fields, own, own_sem)
    own_copy.start()

    def send(source, target, send_sem, recv_sem, peer):
        pltpu.make_async_remote_copy(
            src_ref=source, dst_ref=target, send_sem=send_sem, recv_sem=recv_sem,
            device_id=peer, device_id_type=pl.DeviceIdType.MESH,
        ).start()

    def z_step(s):
        return nz // 2 + (1 - 2 * (s % 2)) * ((s + 1) // 2)

    chunk = lines * 128

    def chunk_lanes(row, s):
        return pl.ds(pl.multiple_of(((row + z_step(s)) % nz) * chunk, chunk), chunk)

    def send_halo(s):
        for way, (peer, target, turn) in enumerate(((next_peer, low, 1), (prev_peer, high, groups - 1))):
            lanes = chunk_lanes((elec + turn) % groups // lines, s)
            send(fields.at[:, :, :, lanes], target.at[:, :, :, lanes],
                 halo_send_sem.at[way], halo_recv_sem.at[way, s], peer)

    for copy in inputs:
        copy.wait()
    owner = group[...]
    source_a = offs[pl.ds(0, 1), :]
    source_b = (source_a + bstep[...]) % PER_GROUP
    group_m = jnp.clip(owner + sides[pl.ds(0, 1), :], 0, groups - 1)
    group_n = jnp.clip(owner + sides[pl.ds(1, 1), :], 0, groups - 1)
    column_m = (group_m - owner + 1) * PER_GROUP + offs[pl.ds(1, 1), :]
    column_n = (group_n - owner + 1) * PER_GROUP + offs[pl.ds(2, 1), :]
    row = iota((groups, quads), 0)
    names = (row % nz) * lines + row // nz
    member = jnp.where(names == owner, 1.0, 0.0).astype(F32)
    earlier = jnp.where(iota((quads, quads), 0) < iota((quads, quads), 1), 1.0, 0.0).astype(BF16)
    before = jnp.dot(member.astype(BF16), earlier, preferred_element_type=F32)
    rank = jnp.sum(member * before, axis=0, keepdims=True)
    place = iota((8, quads), 0)
    indices = jnp.where(
        place == 0, source_a,
        jnp.where(place == 1, source_b, jnp.where(place == 2, column_m, jnp.where(place == 3, column_n, 0))),
    ).astype(F32)
    real = -resid[pl.ds(0, FRAMES, stride=2), :]
    imag = -resid[pl.ds(1, FRAMES, stride=2), :]
    entry = jnp.concatenate([real, imag, indices, jnp.zeros_like(indices)], axis=0)
    entries = jnp.concatenate(
        [jnp.where(rank == float(k), entry, 0.0) for k in range(CAP)], axis=0
    )
    named = member.astype(BF16)
    sorted_rows = sum(dot_nt(named, piece) for piece in split3(entries)[::-1])
    for line in range(lines):
        slots[line] = sorted_rows[line * nz:(line + 1) * nz, :]

    pl.semaphore_wait(barrier, len(peers))

    for d in range(1, lines):
        send(slots.at[(p + d) % lines], a_buf.at[pl.ds((d - 1) * nz, nz)],
             stage_send_sem.at[0], stage_recv_sem.at[0], line_peer(d))
    for s in range(0, halo_ends[0]):
        send_halo(s)
    a_buf[pl.ds((lines - 1) * nz, nz), :] = slots[p]
    own_copy.wait()
    arrived = a_buf.at[pl.ds(0, (lines - 1) * nz)]
    drain(arrived, stage_recv_sem.at[0])
    for to in range(nz):
        b_send[to] = a_buf[pl.ds(to, lines, stride=nz), :]
    for d in range(1, nz):
        send(b_send.at[(z + d) % nz], b_buf.at[pl.ds((d - 1) * lines, lines)],
             stage_send_sem.at[1], stage_recv_sem.at[1], z_peer(d))
    for s in range(halo_ends[0], halo_ends[1]):
        send_halo(s)
    b_buf[pl.ds((nz - 1) * lines, lines), :] = b_send[z]
    drain(b_buf.at[pl.ds(0, (nz - 1) * lines)], stage_recv_sem.at[1])

    received = b_buf[...]
    both = jnp.concatenate([received, pltpu.roll(received, 64, 1)], axis=0)
    turned = both.T
    terms = []
    columns = []
    for half in range(2):
        block = turned[half * SLOT:(half + 1) * SLOT, :]
        at_a = block[16:17].astype(jnp.int32)
        at_b = block[17:18].astype(jnp.int32)
        at_m = block[18:19].astype(jnp.int32)
        at_n = block[19:20].astype(jnp.int32)
        place = iota((PER_GROUP, 128), 0)
        sign = jnp.where(place == at_a, 1.0, 0.0) - jnp.where(place == at_b, 1.0, 0.0)
        terms.append(jnp.concatenate([block[k:k + 1] * sign for k in range(2 * FRAMES)], axis=0))
        place = iota((WINDOW, 128), 0)
        columns.append((jnp.where(place == at_m, 1.0, 0.0) - jnp.where(place == at_n, 1.0, 0.0)).astype(BF16))
    band = jnp.zeros((WINDOW, 128), F32)
    for half in range(2):
        for piece in split3(terms[half])[::-1]:
            band = band + dot_nt(columns[half], piece)
    c_send[...] = band
    for d in range(1, ny):
        send(c_send, c_buf.at[d - 1], stage_send_sem.at[2], stage_recv_sem.at[2], y_peer(d))
    for s in range(halo_ends[1], nz):
        send_halo(s)
    drain(c_buf, stage_recv_sem.at[2])
    for d in range(ny - 1):
        band = band + c_buf[d]
    band = band.astype(BF16).astype(F32)
    upper = jnp.concatenate([band, jnp.zeros((128 - WINDOW, 128), F32)], axis=0).T
    lower = jnp.concatenate([upper[64:], -upper[:64]], axis=0)
    first = upper + pltpu.roll(lower, WINDOW, 1)
    second = pltpu.roll(first, 2 * WINDOW, 1)
    third = pltpu.roll(first, 4 * WINDOW, 1)
    lane = iota((128, 128), 1)
    nothing = jnp.zeros((128, 128), BF16)
    weights[pl.ds(0, 128), pl.ds(0, 128)] = first.astype(BF16)
    weights[pl.ds(0, 128), pl.ds(128, 128)] = nothing
    weights[pl.ds(128, 128), pl.ds(0, 128)] = second.astype(BF16)
    weights[pl.ds(128, 128), pl.ds(128, 128)] = nothing
    weights[pl.ds(256, 128), pl.ds(0, 128)] = jnp.where(lane >= 4 * WINDOW, third, 0.0).astype(BF16)
    weights[pl.ds(256, 128), pl.ds(128, 128)] = jnp.where(lane < 2 * WINDOW, third, 0.0).astype(BF16)

    sublane = iota((PER_GROUP, 128), 0)

    def fold(first, second, width):
        keep = sublane % (2 * width) < width
        return jnp.where(keep, first, second) + pltpu.roll(
            jnp.where(keep, second, first), PER_GROUP - width, 0
        )

    def collect(rows):
        for width in (1, 2, 4):
            rows = [fold(rows[k], rows[k + 1], width) for k in range(0, len(rows), 2)]
        return rows[0]

    def compute(s):
        base = ((z + z_step(s)) % nz) * chunk
        arrived_lanes = chunk_lanes(z, s)
        drain(low.at[:, :, :, arrived_lanes], halo_recv_sem.at[0, s])
        drain(high.at[:, :, :, arrived_lanes], halo_recv_sem.at[1, s])
        matrix = weights[...][:, :3 * 2 * WINDOW]
        for chip in range(nx):
            lanes = pl.ds(pl.multiple_of(base + chip * 256, 256), 256)
            middle = [[own[i, c, :, lanes].astype(F32) for i in range(2)] for c in range(3)]
            window = []
            for c in range(3):
                for i in range(2):
                    window += [low[i, c, :, lanes].astype(F32), middle[c][i], high[i, c, :, lanes].astype(F32)]
            window = jnp.concatenate(window, axis=0).astype(BF16)
            adjoint = jnp.dot(matrix, window, preferred_element_type=F32)
            for k in range(2):
                half = slice(k * 128, (k + 1) * 128)
                real = []
                imag = []
                for t in range(FRAMES):
                    total_real = jnp.zeros((PER_GROUP, 128), F32)
                    total_imag = jnp.zeros((PER_GROUP, 128), F32)
                    for c in range(3):
                        at = c * 128 + t * 8
                        adj_real = adjoint[at:at + 8, half]
                        adj_imag = adjoint[at + 64:at + 72, half]
                        mid_real = middle[c][0][:, half]
                        mid_imag = middle[c][1][:, half]
                        total_real = total_real + mid_real * adj_real + mid_imag * adj_imag
                        total_imag = total_imag + mid_real * adj_imag - mid_imag * adj_real
                    real.append(total_real)
                    imag.append(total_imag)
                total_rows = jnp.concatenate([collect(real), collect(imag)], axis=0)
                part[s, k, chip] = total_rows
                near[chip * 2 + k] = total_rows.astype(BF16)

    def swap_core(s):
        send(part.at[s, 1 - core], core_recv.at[s], core_send_sem, core_recv_sem.at[s], core_peer)

    def send_near():
        for d in range(1, lines):
            send(near.at[(p + d) % lines], near_shares.at[d - 1], near_send_sem, near_recv_sem, line_peer(d))

    def add_core(s):
        drain(core_recv.at[s], core_recv_sem.at[s])
        rounded[s] = (part[s, core] + core_recv[s]).astype(BF16)
        for d in range(nx):
            send(rounded.at[s, (x + d) % nx], shares.at[s, d],
                 share_send_sem, share_recv_sem.at[s], chip_peer(z_step(s), d))

    core_lag = 2

    def step(s, carry):
        compute(s)

        @pl.when(s < nz - 1)
        def _():
            swap_core(s)

        @pl.when(s >= core_lag)
        def _():
            add_core(s - core_lag)

        return carry

    lax.fori_loop(0, nz, step, 0)
    send_near()
    for s in range(max(nz - core_lag, 0), nz - 1):
        add_core(s)
    total = part[nz - 1, core, x]
    for s in range(nz - 1):
        drain(shares.at[s], share_recv_sem.at[s])
        for d in range(nx):
            total = total + shares[s, d].astype(F32)
    drain(near_shares, near_recv_sem)
    for d in range(lines - 1):
        total = total + near_shares[d].astype(F32)
    out[pl.ds(0, FRAMES, stride=2), :] = total[0:8]
    out[pl.ds(1, FRAMES, stride=2), :] = total[8:16]

    drain(low, halo_send_sem.at[0])
    drain(high, halo_send_sem.at[1])
    drain(arrived, stage_send_sem.at[0])
    drain(b_buf.at[pl.ds(0, (nz - 1) * lines)], stage_send_sem.at[1])
    drain(c_buf, stage_send_sem.at[2])
    drain(core_recv, core_send_sem)
    drain(shares, share_send_sem)
    drain(near_shares, near_send_sem)


def local(fields, residual, quad_group, offsets, b_step, sides):
    groups = lax.axis_size("elec")
    ny = lax.axis_size("cell")
    nx = X_CHIPS
    lines = 2 * nx
    nz = groups // lines
    cells = fields.shape[3]
    count = residual.shape[0]
    resid = jnp.transpose(residual, (1, 2, 0)).reshape(2 * FRAMES, count)
    vmem = pl.BlockSpec(memory_space=pltpu.VMEM)
    field_shape = (2, 3, PER_GROUP, cells)
    dma = pltpu.SemaphoreType.DMA
    gradient = pl.pallas_call(
        functools.partial(kernel, (nz, nx, ny)),
        out_shape=jax.ShapeDtypeStruct((2 * FRAMES, 128), F32),
        in_specs=[pl.BlockSpec(memory_space=pltpu.HBM)] * 6,
        out_specs=vmem,
        scratch_shapes=[
            pltpu.VMEM((2 * FRAMES, count), F32),
            pltpu.VMEM((1, count), jnp.int32),
            pltpu.VMEM((3, count), jnp.int32),
            pltpu.VMEM((1, count), jnp.int32),
            pltpu.VMEM((2, count), jnp.int32),
            pltpu.VMEM(field_shape, BF16),
            pltpu.VMEM(field_shape, BF16),
            pltpu.VMEM(field_shape, BF16),
            pltpu.VMEM((lines, nz, 128), F32),
            pltpu.VMEM((groups, 128), F32),
            pltpu.VMEM((nz, lines, 128), F32),
            pltpu.VMEM((64, 128), F32),
            pltpu.VMEM((WINDOW, 128), F32),
            pltpu.VMEM((ny - 1, WINDOW, 128), F32),
            pltpu.VMEM((384, 256), BF16),
            pltpu.VMEM((nz, 2, nx, 16, 128), F32),
            pltpu.VMEM((nz - 1, nx, 16, 128), F32),
            pltpu.VMEM((nz - 1, nx, 16, 128), BF16),
            pltpu.VMEM((nz - 1, nx, 16, 128), BF16),
            pltpu.VMEM((lines, 16, 128), BF16),
            pltpu.VMEM((lines - 1, 16, 128), BF16),
            dma((5,)), dma, dma((2,)), dma((2, nz)),
            dma((3,)), dma((3,)),
            dma, dma((nz - 1,)), dma, dma((nz - 1,)), dma, dma,
        ],
        compiler_params=pltpu.CompilerParams(
            collective_id=0, has_side_effects=True, vmem_limit_bytes=40 * 1024 * 1024
        ),
    )(*(
        pltpu.with_memory_space_constraint(value, pltpu.HBM)
        for value in (fields, resid, quad_group.T, offsets.T, b_step.T, sides.T)
    ))
    return gradient.reshape(FRAMES, 2, 1, 128)


def solution(mesh):
    return jax.shard_map(
        local,
        mesh=mesh,
        in_specs=(
            P(None, None, "elec", "cell"),
            P(("elec", "cell"), None, None),
            P(("elec", "cell"), None),
            P(("elec", "cell"), None),
            P(("elec", "cell"), None),
            P(("elec", "cell"), None),
        ),
        out_specs=P(None, None, "cell", "elec"),
        check_vma=False,
    )
```

```python
import functools

import jax
import jax.numpy as jnp
from jax import lax
from jax.experimental import pallas as pl
from jax.experimental.pallas import tpu as pltpu
from jax.sharding import PartitionSpec as P

X_CHIPS = 4
PER_GROUP = 8
FRAMES = 8
CAP = 4
SLOT = 32
WINDOW = 3 * PER_GROUP
F32 = jnp.float32
BF16 = jnp.bfloat16


def iota(shape, dim):
    return lax.broadcasted_iota(jnp.int32, shape, dim)


def split3(value):
    high = value.astype(BF16)
    rest = value - high.astype(F32)
    middle = rest.astype(BF16)
    low = (rest - middle.astype(F32)).astype(BF16)
    return high, middle, low


def dot_nt(left, right):
    return lax.dot_general(left, right, (((1,), (1,)), ((), ())), preferred_element_type=F32)


def drain(ref, sem):
    pltpu.make_async_copy(ref, ref, sem).wait()


def kernel(
    sizes,
    fields, resid_in, group_in, offs_in, bstep_in, sides_in,
    out,
    resid, group, offs, bstep, sides,
    own, low, high,
    slots, a_buf, b_send, b_buf, c_send, c_buf, weights,
    part, core_recv, rounded, shares, near, near_shares,
    in_sem, own_sem, halo_send_sem, halo_recv_sem,
    stage_send_sem, stage_recv_sem,
    core_send_sem, core_recv_sem, share_send_sem, share_recv_sem, near_send_sem, near_recv_sem,
):
    nz, nx, ny = sizes
    lines = 2 * nx
    groups = nz * lines
    quads = resid.shape[1]
    halo_ends = (0, 3 * nz // 8)
    elec = lax.axis_index("elec")
    cell = lax.axis_index("cell")
    z = elec // lines
    p = elec % lines
    x = p // 2
    core = p % 2

    inputs = [
        pltpu.make_async_copy(source, target, in_sem.at[number])
        for number, (source, target) in enumerate(
            zip((resid_in, group_in, offs_in, bstep_in, sides_in), (resid, group, offs, bstep, sides))
        )
    ]
    for copy in inputs:
        copy.start()

    def line_peer(d):
        return {"elec": z * lines + (p + d) % lines}

    def z_peer(d):
        return {"elec": ((z + d) % nz) * lines + p}

    def chip_peer(dz, dx):
        return {"elec": ((z + dz) % nz) * lines + ((x + dx) % nx) * 2 + core}

    def y_peer(d):
        return {"cell": (cell + d) % ny}

    core_peer = {"elec": z * lines + x * 2 + 1 - core}
    next_peer = {"elec": (elec + 1) % groups}
    prev_peer = {"elec": (elec + groups - 1) % groups}

    if groups < 64:
        b_buf[...] = jnp.zeros_like(b_buf)
    barrier = pltpu.get_barrier_semaphore()
    peers = (
        [line_peer(d) for d in range(1, lines)]
        + [chip_peer(dz, dx) for dz in range(1, nz) for dx in range(nx)]
        + [y_peer(d) for d in range(1, ny)]
        + [next_peer, prev_peer]
    )
    for peer in peers:
        pl.semaphore_signal(barrier, inc=1, device_id=peer, device_id_type=pl.DeviceIdType.MESH)

    own_copy = pltpu.make_async_copy(fields, own, own_sem)
    own_copy.start()

    def send(source, target, send_sem, recv_sem, peer):
        pltpu.make_async_remote_copy(
            src_ref=source, dst_ref=target, send_sem=send_sem, recv_sem=recv_sem,
            device_id=peer, device_id_type=pl.DeviceIdType.MESH,
        ).start()

    def z_step(s):
        return nz // 2 + (1 - 2 * (s % 2)) * ((s + 1) // 2)

    chunk = lines * 128

    def chunk_lanes(row, s):
        return pl.ds(pl.multiple_of(((row + z_step(s)) % nz) * chunk, chunk), chunk)

    def send_halo(s):
        for way, (peer, target, turn) in enumerate(((next_peer, low, 1), (prev_peer, high, groups - 1))):
            lanes = chunk_lanes((elec + turn) % groups // lines, s)
            send(fields.at[:, :, :, lanes], target.at[:, :, :, lanes],
                 halo_send_sem.at[way], halo_recv_sem.at[way, s], peer)

    for copy in inputs:
        copy.wait()
    owner = group[...]
    source_a = offs[pl.ds(0, 1), :]
    source_b = (source_a + bstep[...]) % PER_GROUP
    group_m = jnp.clip(owner + sides[pl.ds(0, 1), :], 0, groups - 1)
    group_n = jnp.clip(owner + sides[pl.ds(1, 1), :], 0, groups - 1)
    column_m = (group_m - owner + 1) * PER_GROUP + offs[pl.ds(1, 1), :]
    column_n = (group_n - owner + 1) * PER_GROUP + offs[pl.ds(2, 1), :]
    row = iota((groups, quads), 0)
    names = (row % nz) * lines + row // nz
    member = jnp.where(names == owner, 1.0, 0.0).astype(F32)
    earlier = jnp.where(iota((quads, quads), 0) < iota((quads, quads), 1), 1.0, 0.0).astype(BF16)
    before = jnp.dot(member.astype(BF16), earlier, preferred_element_type=F32)
    rank = jnp.sum(member * before, axis=0, keepdims=True)
    place = iota((8, quads), 0)
    indices = jnp.where(
        place == 0, source_a,
        jnp.where(place == 1, source_b, jnp.where(place == 2, column_m, jnp.where(place == 3, column_n, 0))),
    ).astype(F32)
    real = -resid[pl.ds(0, FRAMES, stride=2), :]
    imag = -resid[pl.ds(1, FRAMES, stride=2), :]
    entry = jnp.concatenate([real, imag, indices, jnp.zeros_like(indices)], axis=0)
    entries = jnp.concatenate(
        [jnp.where(rank == float(k), entry, 0.0) for k in range(CAP)], axis=0
    )
    named = member.astype(BF16)
    sorted_rows = sum(dot_nt(named, piece) for piece in split3(entries)[::-1])
    for line in range(lines):
        slots[line] = sorted_rows[line * nz:(line + 1) * nz, :]

    pl.semaphore_wait(barrier, len(peers))

    for d in range(1, lines):
        send(slots.at[(p + d) % lines], a_buf.at[pl.ds((d - 1) * nz, nz)],
             stage_send_sem.at[0], stage_recv_sem.at[0], line_peer(d))
    for s in range(0, halo_ends[0]):
        send_halo(s)
    a_buf[pl.ds((lines - 1) * nz, nz), :] = slots[p]
    own_copy.wait()
    arrived = a_buf.at[pl.ds(0, (lines - 1) * nz)]
    drain(arrived, stage_recv_sem.at[0])
    for to in range(nz):
        b_send[to] = a_buf[pl.ds(to, lines, stride=nz), :]
    for d in range(1, nz):
        send(b_send.at[(z + d) % nz], b_buf.at[pl.ds((d - 1) * lines, lines)],
             stage_send_sem.at[1], stage_recv_sem.at[1], z_peer(d))
    for s in range(halo_ends[0], halo_ends[1]):
        send_halo(s)
    b_buf[pl.ds((nz - 1) * lines, lines), :] = b_send[z]
    drain(b_buf.at[pl.ds(0, (nz - 1) * lines)], stage_recv_sem.at[1])

    received = b_buf[...]
    both = jnp.concatenate([received, pltpu.roll(received, 64, 1)], axis=0)
    turned = both.T
    terms = []
    columns = []
    for half in range(2):
        block = turned[half * SLOT:(half + 1) * SLOT, :]
        at_a = block[16:17].astype(jnp.int32)
        at_b = block[17:18].astype(jnp.int32)
        at_m = block[18:19].astype(jnp.int32)
        at_n = block[19:20].astype(jnp.int32)
        place = iota((PER_GROUP, 128), 0)
        sign = jnp.where(place == at_a, 1.0, 0.0) - jnp.where(place == at_b, 1.0, 0.0)
        terms.append(jnp.concatenate([block[k:k + 1] * sign for k in range(2 * FRAMES)], axis=0))
        place = iota((WINDOW, 128), 0)
        columns.append((jnp.where(place == at_m, 1.0, 0.0) - jnp.where(place == at_n, 1.0, 0.0)).astype(BF16))
    band = jnp.zeros((WINDOW, 128), F32)
    for half in range(2):
        for piece in split3(terms[half])[::-1]:
            band = band + dot_nt(columns[half], piece)
    c_send[...] = band
    for d in range(1, ny):
        send(c_send, c_buf.at[d - 1], stage_send_sem.at[2], stage_recv_sem.at[2], y_peer(d))
    for s in range(halo_ends[1], nz):
        send_halo(s)
    drain(c_buf, stage_recv_sem.at[2])
    for d in range(ny - 1):
        band = band + c_buf[d]
    band = band.astype(BF16).astype(F32)
    upper = jnp.concatenate([band, jnp.zeros((128 - WINDOW, 128), F32)], axis=0).T
    lower = jnp.concatenate([upper[64:], -upper[:64]], axis=0)
    first = upper + pltpu.roll(lower, WINDOW, 1)
    second = pltpu.roll(first, 2 * WINDOW, 1)
    third = pltpu.roll(first, 4 * WINDOW, 1)
    lane = iota((128, 128), 1)
    nothing = jnp.zeros((128, 128), F32)
    left = (first, second, jnp.where(lane >= 4 * WINDOW, third, 0.0))
    right = (nothing, nothing, jnp.where(lane < 2 * WINDOW, third, 0.0))
    for half, blocks in enumerate((left, right)):
        rows = [
            blocks[c][at:at + PER_GROUP]
            for t in range(FRAMES) for c in range(3) for at in (t * PER_GROUP, 64 + t * PER_GROUP)
        ]
        weights[:, pl.ds(half * 128, 128)] = jnp.concatenate(rows, axis=0).astype(BF16)

    sublane = iota((PER_GROUP, 128), 0)

    def fold(first, second, width):
        keep = sublane % (2 * width) < width
        return jnp.where(keep, first, second) + pltpu.roll(
            jnp.where(keep, second, first), PER_GROUP - width, 0
        )

    def collect(rows):
        for width in (1, 2, 4):
            rows = [fold(rows[k], rows[k + 1], width) for k in range(0, len(rows), 2)]
        return rows[0]

    def compute(s):
        base = ((z + z_step(s)) % nz) * chunk
        arrived_lanes = chunk_lanes(z, s)
        drain(low.at[:, :, :, arrived_lanes], halo_recv_sem.at[0, s])
        drain(high.at[:, :, :, arrived_lanes], halo_recv_sem.at[1, s])
        matrix = weights[...][:, :3 * 2 * WINDOW]
        for chip in range(nx):
            lanes = pl.ds(pl.multiple_of(base + chip * 256, 256), 256)
            middle = [[own[i, c, :, lanes].astype(F32) for i in range(2)] for c in range(3)]
            window = []
            for c in range(3):
                for i in range(2):
                    window += [low[i, c, :, lanes].astype(F32), middle[c][i], high[i, c, :, lanes].astype(F32)]
            window = jnp.concatenate(window, axis=0).astype(BF16)
            adjoint = jnp.dot(matrix, window, preferred_element_type=F32)
            for k in range(2):
                half = slice(k * 128, (k + 1) * 128)
                real = []
                imag = []
                for t in range(FRAMES):
                    total_real = jnp.zeros((PER_GROUP, 128), F32)
                    total_imag = jnp.zeros((PER_GROUP, 128), F32)
                    for c in range(3):
                        at = (t * 3 + c) * 16
                        adj_real = adjoint[at:at + 8, half]
                        adj_imag = adjoint[at + 8:at + 16, half]
                        mid_real = middle[c][0][:, half]
                        mid_imag = middle[c][1][:, half]
                        total_real = total_real + mid_real * adj_real + mid_imag * adj_imag
                        total_imag = total_imag + mid_real * adj_imag - mid_imag * adj_real
                    real.append(total_real)
                    imag.append(total_imag)
                total_rows = jnp.concatenate([collect(real), collect(imag)], axis=0)
                part[s, k, chip] = total_rows
                near[chip * 2 + k] = total_rows.astype(BF16)

    def swap_core(s):
        send(part.at[s, 1 - core], core_recv.at[s], core_send_sem, core_recv_sem.at[s], core_peer)

    def send_near():
        for d in range(1, lines):
            send(near.at[(p + d) % lines], near_shares.at[d - 1], near_send_sem, near_recv_sem, line_peer(d))

    def add_core(s):
        drain(core_recv.at[s], core_recv_sem.at[s])
        rounded[s] = (part[s, core] + core_recv[s]).astype(BF16)
        for d in range(nx):
            send(rounded.at[s, (x + d) % nx], shares.at[s, d],
                 share_send_sem, share_recv_sem.at[s], chip_peer(z_step(s), d))

    core_lag = 2

    def step(s, carry):
        compute(s)

        @pl.when(s < nz - 1)
        def _():
            swap_core(s)

        @pl.when(s >= core_lag)
        def _():
            add_core(s - core_lag)

        return carry

    lax.fori_loop(0, nz, step, 0)
    send_near()
    for s in range(max(nz - core_lag, 0), nz - 1):
        add_core(s)
    total = part[nz - 1, core, x]
    for s in range(nz - 1):
        drain(shares.at[s], share_recv_sem.at[s])
        for d in range(nx):
            total = total + shares[s, d].astype(F32)
    drain(near_shares, near_recv_sem)
    for d in range(lines - 1):
        total = total + near_shares[d].astype(F32)
    out[pl.ds(0, FRAMES, stride=2), :] = total[0:8]
    out[pl.ds(1, FRAMES, stride=2), :] = total[8:16]

    drain(low, halo_send_sem.at[0])
    drain(high, halo_send_sem.at[1])
    drain(arrived, stage_send_sem.at[0])
    drain(b_buf.at[pl.ds(0, (nz - 1) * lines)], stage_send_sem.at[1])
    drain(c_buf, stage_send_sem.at[2])
    drain(core_recv, core_send_sem)
    drain(shares, share_send_sem)
    drain(near_shares, near_send_sem)


def local(fields, residual, quad_group, offsets, b_step, sides):
    groups = lax.axis_size("elec")
    ny = lax.axis_size("cell")
    nx = X_CHIPS
    lines = 2 * nx
    nz = groups // lines
    cells = fields.shape[3]
    count = residual.shape[0]
    resid = jnp.transpose(residual, (1, 2, 0)).reshape(2 * FRAMES, count)
    vmem = pl.BlockSpec(memory_space=pltpu.VMEM)
    field_shape = (2, 3, PER_GROUP, cells)
    dma = pltpu.SemaphoreType.DMA
    gradient = pl.pallas_call(
        functools.partial(kernel, (nz, nx, ny)),
        out_shape=jax.ShapeDtypeStruct((2 * FRAMES, 128), F32),
        in_specs=[pl.BlockSpec(memory_space=pltpu.HBM)] * 6,
        out_specs=vmem,
        scratch_shapes=[
            pltpu.VMEM((2 * FRAMES, count), F32),
            pltpu.VMEM((1, count), jnp.int32),
            pltpu.VMEM((3, count), jnp.int32),
            pltpu.VMEM((1, count), jnp.int32),
            pltpu.VMEM((2, count), jnp.int32),
            pltpu.VMEM(field_shape, BF16),
            pltpu.VMEM(field_shape, BF16),
            pltpu.VMEM(field_shape, BF16),
            pltpu.VMEM((lines, nz, 128), F32),
            pltpu.VMEM((groups, 128), F32),
            pltpu.VMEM((nz, lines, 128), F32),
            pltpu.VMEM((64, 128), F32),
            pltpu.VMEM((WINDOW, 128), F32),
            pltpu.VMEM((ny - 1, WINDOW, 128), F32),
            pltpu.VMEM((384, 256), BF16),
            pltpu.VMEM((nz, 2, nx, 16, 128), F32),
            pltpu.VMEM((nz - 1, nx, 16, 128), F32),
            pltpu.VMEM((nz - 1, nx, 16, 128), BF16),
            pltpu.VMEM((nz - 1, nx, 16, 128), BF16),
            pltpu.VMEM((lines, 16, 128), BF16),
            pltpu.VMEM((lines - 1, 16, 128), BF16),
            dma((5,)), dma, dma((2,)), dma((2, nz)),
            dma((3,)), dma((3,)),
            dma, dma((nz - 1,)), dma, dma((nz - 1,)), dma, dma,
        ],
        compiler_params=pltpu.CompilerParams(
            collective_id=0, has_side_effects=True, vmem_limit_bytes=40 * 1024 * 1024
        ),
    )(*(
        pltpu.with_memory_space_constraint(value, pltpu.HBM)
        for value in (fields, resid, quad_group.T, offsets.T, b_step.T, sides.T)
    ))
    return gradient.reshape(FRAMES, 2, 1, 128)


def solution(mesh):
    return jax.shard_map(
        local,
        mesh=mesh,
        in_specs=(
            P(None, None, "elec", "cell"),
            P(("elec", "cell"), None, None),
            P(("elec", "cell"), None),
            P(("elec", "cell"), None),
            P(("elec", "cell"), None),
            P(("elec", "cell"), None),
        ),
        out_specs=P(None, None, "cell", "elec"),
        check_vma=False,
    )
```

```python
import functools

import jax
import jax.numpy as jnp
from jax import lax
from jax.experimental import pallas as pl
from jax.experimental.pallas import tpu as pltpu
from jax.sharding import PartitionSpec as P

X_CHIPS = 4
PER_GROUP = 8
FRAMES = 8
CAP = 4
SLOT = 32
WINDOW = 3 * PER_GROUP
F32 = jnp.float32
BF16 = jnp.bfloat16


def iota(shape, dim):
    return lax.broadcasted_iota(jnp.int32, shape, dim)


def split3(value):
    high = value.astype(BF16)
    rest = value - high.astype(F32)
    middle = rest.astype(BF16)
    low = (rest - middle.astype(F32)).astype(BF16)
    return high, middle, low


def dot_nt(left, right):
    return lax.dot_general(left, right, (((1,), (1,)), ((), ())), preferred_element_type=F32)


def far_chunks(nz):
    return 3 * (nz - 1) // 7


def drain(ref, sem):
    pltpu.make_async_copy(ref, ref, sem).wait()


def kernel(
    sizes,
    fields, resid_in, group_in, offs_in, bstep_in, sides_in,
    out,
    resid, group, offs, bstep, sides,
    own, low, high,
    slots, a_buf, b_send, b_buf, c_send, c_buf, weights,
    part, core_recv, rounded, shares, near, near_shares, row_recv, row_send, far_shares,
    in_sem, own_sem, halo_send_sem, halo_recv_sem,
    stage_send_sem, stage_recv_sem,
    core_send_sem, core_recv_sem, share_send_sem, share_recv_sem, near_send_sem, near_recv_sem,
    row_send_sem, row_recv_sem, far_send_sem, far_recv_sem,
):
    nz, nx, ny = sizes
    lines = 2 * nx
    groups = nz * lines
    quads = resid.shape[1]
    halo_ends = (0, 3 * nz // 8)
    far = far_chunks(nz)
    elec = lax.axis_index("elec")
    cell = lax.axis_index("cell")
    z = elec // lines
    p = elec % lines
    x = p // 2
    core = p % 2

    inputs = [
        pltpu.make_async_copy(source, target, in_sem.at[number])
        for number, (source, target) in enumerate(
            zip((resid_in, group_in, offs_in, bstep_in, sides_in), (resid, group, offs, bstep, sides))
        )
    ]
    for copy in inputs:
        copy.start()

    def line_peer(d):
        return {"elec": z * lines + (p + d) % lines}

    def z_peer(d):
        return {"elec": ((z + d) % nz) * lines + p}

    def chip_peer(dz, dx):
        return {"elec": ((z + dz) % nz) * lines + ((x + dx) % nx) * 2 + core}

    def y_peer(d):
        return {"cell": (cell + d) % ny}

    core_peer = {"elec": z * lines + x * 2 + 1 - core}
    next_peer = {"elec": (elec + 1) % groups}
    prev_peer = {"elec": (elec + groups - 1) % groups}

    if groups < 64:
        b_buf[...] = jnp.zeros_like(b_buf)
    barrier = pltpu.get_barrier_semaphore()
    peers = (
        [line_peer(d) for d in range(1, lines)]
        + [chip_peer(dz, dx) for dz in range(1, nz) for dx in range(nx)]
        + [y_peer(d) for d in range(1, ny)]
        + [next_peer, prev_peer]
    )
    for peer in peers:
        pl.semaphore_signal(barrier, inc=1, device_id=peer, device_id_type=pl.DeviceIdType.MESH)

    own_copy = pltpu.make_async_copy(fields, own, own_sem)
    own_copy.start()

    def send(source, target, send_sem, recv_sem, peer):
        pltpu.make_async_remote_copy(
            src_ref=source, dst_ref=target, send_sem=send_sem, recv_sem=recv_sem,
            device_id=peer, device_id_type=pl.DeviceIdType.MESH,
        ).start()

    def z_step(s):
        return nz // 2 + (1 - 2 * (s % 2)) * ((s + 1) // 2)

    chunk = lines * 128

    def chunk_lanes(row, s):
        return pl.ds(pl.multiple_of(((row + z_step(s)) % nz) * chunk, chunk), chunk)

    def send_halo(s):
        for way, (peer, target, turn) in enumerate(((next_peer, low, 1), (prev_peer, high, groups - 1))):
            lanes = chunk_lanes((elec + turn) % groups // lines, s)
            send(fields.at[:, :, :, lanes], target.at[:, :, :, lanes],
                 halo_send_sem.at[way], halo_recv_sem.at[way, s], peer)

    for copy in inputs:
        copy.wait()
    owner = group[...]
    source_a = offs[pl.ds(0, 1), :]
    source_b = (source_a + bstep[...]) % PER_GROUP
    group_m = jnp.clip(owner + sides[pl.ds(0, 1), :], 0, groups - 1)
    group_n = jnp.clip(owner + sides[pl.ds(1, 1), :], 0, groups - 1)
    column_m = (group_m - owner + 1) * PER_GROUP + offs[pl.ds(1, 1), :]
    column_n = (group_n - owner + 1) * PER_GROUP + offs[pl.ds(2, 1), :]
    row = iota((groups, quads), 0)
    names = (row % nz) * lines + row // nz
    member = jnp.where(names == owner, 1.0, 0.0).astype(F32)
    earlier = jnp.where(iota((quads, quads), 0) < iota((quads, quads), 1), 1.0, 0.0).astype(BF16)
    before = jnp.dot(member.astype(BF16), earlier, preferred_element_type=F32)
    rank = jnp.sum(member * before, axis=0, keepdims=True)
    place = iota((8, quads), 0)
    indices = jnp.where(
        place == 0, source_a,
        jnp.where(place == 1, source_b, jnp.where(place == 2, column_m, jnp.where(place == 3, column_n, 0))),
    ).astype(F32)
    real = -resid[pl.ds(0, FRAMES, stride=2), :]
    imag = -resid[pl.ds(1, FRAMES, stride=2), :]
    entry = jnp.concatenate([real, imag, indices, jnp.zeros_like(indices)], axis=0)
    entries = jnp.concatenate(
        [jnp.where(rank == float(k), entry, 0.0) for k in range(CAP)], axis=0
    )
    named = member.astype(BF16)
    sorted_rows = sum(dot_nt(named, piece) for piece in split3(entries)[::-1])
    for line in range(lines):
        slots[line] = sorted_rows[line * nz:(line + 1) * nz, :]

    pl.semaphore_wait(barrier, len(peers))

    for d in range(1, lines):
        send(slots.at[(p + d) % lines], a_buf.at[pl.ds((d - 1) * nz, nz)],
             stage_send_sem.at[0], stage_recv_sem.at[0], line_peer(d))
    for s in range(0, halo_ends[0]):
        send_halo(s)
    a_buf[pl.ds((lines - 1) * nz, nz), :] = slots[p]
    own_copy.wait()
    arrived = a_buf.at[pl.ds(0, (lines - 1) * nz)]
    drain(arrived, stage_recv_sem.at[0])
    for to in range(nz):
        b_send[to] = a_buf[pl.ds(to, lines, stride=nz), :]
    for d in range(1, nz):
        send(b_send.at[(z + d) % nz], b_buf.at[pl.ds((d - 1) * lines, lines)],
             stage_send_sem.at[1], stage_recv_sem.at[1], z_peer(d))
    for s in range(halo_ends[0], halo_ends[1]):
        send_halo(s)
    b_buf[pl.ds((nz - 1) * lines, lines), :] = b_send[z]
    drain(b_buf.at[pl.ds(0, (nz - 1) * lines)], stage_recv_sem.at[1])

    received = b_buf[...]
    both = jnp.concatenate([received, pltpu.roll(received, 64, 1)], axis=0)
    turned = both.T
    terms = []
    columns = []
    for half in range(2):
        block = turned[half * SLOT:(half + 1) * SLOT, :]
        at_a = block[16:17].astype(jnp.int32)
        at_b = block[17:18].astype(jnp.int32)
        at_m = block[18:19].astype(jnp.int32)
        at_n = block[19:20].astype(jnp.int32)
        place = iota((PER_GROUP, 128), 0)
        sign = jnp.where(place == at_a, 1.0, 0.0) - jnp.where(place == at_b, 1.0, 0.0)
        terms.append(jnp.concatenate([block[k:k + 1] * sign for k in range(2 * FRAMES)], axis=0))
        place = iota((WINDOW, 128), 0)
        columns.append((jnp.where(place == at_m, 1.0, 0.0) - jnp.where(place == at_n, 1.0, 0.0)).astype(BF16))
    band = jnp.zeros((WINDOW, 128), F32)
    for half in range(2):
        for piece in split3(terms[half])[::-1]:
            band = band + dot_nt(columns[half], piece)
    c_send[...] = band
    for d in range(1, ny):
        send(c_send, c_buf.at[d - 1], stage_send_sem.at[2], stage_recv_sem.at[2], y_peer(d))
    for s in range(halo_ends[1], nz):
        send_halo(s)
    drain(c_buf, stage_recv_sem.at[2])
    for d in range(ny - 1):
        band = band + c_buf[d]
    band = band.astype(BF16).astype(F32)
    upper = jnp.concatenate([band, jnp.zeros((128 - WINDOW, 128), F32)], axis=0).T
    lower = jnp.concatenate([upper[64:], -upper[:64]], axis=0)
    first = upper + pltpu.roll(lower, WINDOW, 1)
    second = pltpu.roll(first, 2 * WINDOW, 1)
    third = pltpu.roll(first, 4 * WINDOW, 1)
    lane = iota((128, 128), 1)
    nothing = jnp.zeros((128, 128), F32)
    left = (first, second, jnp.where(lane >= 4 * WINDOW, third, 0.0))
    right = (nothing, nothing, jnp.where(lane < 2 * WINDOW, third, 0.0))
    for half, blocks in enumerate((left, right)):
        rows = [
            blocks[c][at:at + PER_GROUP]
            for t in range(FRAMES) for c in range(3) for at in (t * PER_GROUP, 64 + t * PER_GROUP)
        ]
        weights[:, pl.ds(half * 128, 128)] = jnp.concatenate(rows, axis=0).astype(BF16)

    sublane = iota((PER_GROUP, 128), 0)

    def fold(first, second, width):
        keep = sublane % (2 * width) < width
        return jnp.where(keep, first, second) + pltpu.roll(
            jnp.where(keep, second, first), PER_GROUP - width, 0
        )

    def collect(rows):
        for width in (1, 2, 4):
            rows = [fold(rows[k], rows[k + 1], width) for k in range(0, len(rows), 2)]
        return rows[0]

    def compute(s):
        base = ((z + z_step(s)) % nz) * chunk
        arrived_lanes = chunk_lanes(z, s)
        drain(low.at[:, :, :, arrived_lanes], halo_recv_sem.at[0, s])
        drain(high.at[:, :, :, arrived_lanes], halo_recv_sem.at[1, s])
        matrix = weights[...][:, :3 * 2 * WINDOW]
        for chip in range(nx):
            lanes = pl.ds(pl.multiple_of(base + chip * 256, 256), 256)
            middle = [[own[i, c, :, lanes].astype(F32) for i in range(2)] for c in range(3)]
            window = []
            for c in range(3):
                for i in range(2):
                    window += [low[i, c, :, lanes].astype(F32), middle[c][i], high[i, c, :, lanes].astype(F32)]
            window = jnp.concatenate(window, axis=0).astype(BF16)
            adjoint = jnp.dot(matrix, window, preferred_element_type=F32)
            for k in range(2):
                half = slice(k * 128, (k + 1) * 128)
                real = []
                imag = []
                for t in range(FRAMES):
                    total_real = jnp.zeros((PER_GROUP, 128), F32)
                    total_imag = jnp.zeros((PER_GROUP, 128), F32)
                    for c in range(3):
                        at = (t * 3 + c) * 16
                        adj_real = adjoint[at:at + 8, half]
                        adj_imag = adjoint[at + 8:at + 16, half]
                        mid_real = middle[c][0][:, half]
                        mid_imag = middle[c][1][:, half]
                        total_real = total_real + mid_real * adj_real + mid_imag * adj_imag
                        total_imag = total_imag + mid_real * adj_imag - mid_imag * adj_real
                    real.append(total_real)
                    imag.append(total_imag)
                total_rows = jnp.concatenate([collect(real), collect(imag)], axis=0)
                part[s, k, chip] = total_rows
                near[chip * 2 + k] = total_rows.astype(BF16)

    def swap_core(s):
        send(part.at[s, 1 - core], core_recv.at[s], core_send_sem, core_recv_sem.at[s], core_peer)

    def send_near():
        for d in range(1, lines):
            send(near.at[(p + d) % lines], near_shares.at[d - 1], near_send_sem, near_recv_sem, line_peer(d))

    def add_core(s):
        drain(core_recv.at[s], core_recv_sem.at[s])
        rounded[s] = (part[s, core] + core_recv[s]).astype(BF16)

        @pl.when(s < far)
        def _():
            for d in range(1, nx):
                send(rounded.at[s, (x + d) % nx], row_recv.at[s, d - 1],
                     row_send_sem, row_recv_sem.at[s], chip_peer(0, d))

        @pl.when(s >= far)
        def _():
            for d in range(nx):
                send(rounded.at[s, (x + d) % nx], shares.at[s - far, d],
                     share_send_sem, share_recv_sem.at[s - far], chip_peer(z_step(s), d))

    def pass_far(s):
        drain(row_recv.at[s], row_recv_sem.at[s])
        total = part[s, core, x] + core_recv[s, x]
        for d in range(nx - 1):
            total = total + row_recv[s, d].astype(F32)
        row_send[s] = total.astype(BF16)
        send(row_send.at[s], far_shares.at[s], far_send_sem, far_recv_sem, chip_peer(z_step(s), 0))

    core_lag = 2
    row_lag = 4

    def step(s, carry):
        compute(s)

        @pl.when(s < nz - 1)
        def _():
            swap_core(s)

        @pl.when(s >= core_lag)
        def _():
            add_core(s - core_lag)

        @pl.when((s >= row_lag) & (s < row_lag + far))
        def _():
            pass_far(s - row_lag)

        return carry

    lax.fori_loop(0, nz, step, 0)
    send_near()
    for s in range(max(nz - core_lag, 0), nz - 1):
        add_core(s)
    for s in range(max(nz - row_lag, 0), far):
        pass_far(s)
    total = part[nz - 1, core, x]
    drain(far_shares, far_recv_sem)
    for s in range(far):
        total = total + far_shares[s].astype(F32)
    for s in range(nz - 1 - far):
        drain(shares.at[s], share_recv_sem.at[s])
        for d in range(nx):
            total = total + shares[s, d].astype(F32)
    drain(near_shares, near_recv_sem)
    for d in range(lines - 1):
        total = total + near_shares[d].astype(F32)
    out[pl.ds(0, FRAMES, stride=2), :] = total[0:8]
    out[pl.ds(1, FRAMES, stride=2), :] = total[8:16]

    drain(low, halo_send_sem.at[0])
    drain(high, halo_send_sem.at[1])
    drain(arrived, stage_send_sem.at[0])
    drain(b_buf.at[pl.ds(0, (nz - 1) * lines)], stage_send_sem.at[1])
    drain(c_buf, stage_send_sem.at[2])
    drain(core_recv, core_send_sem)
    drain(shares, share_send_sem)
    drain(near_shares, near_send_sem)
    drain(row_recv, row_send_sem)
    drain(far_shares, far_send_sem)


def local(fields, residual, quad_group, offsets, b_step, sides):
    groups = lax.axis_size("elec")
    ny = lax.axis_size("cell")
    nx = X_CHIPS
    lines = 2 * nx
    nz = groups // lines
    far = far_chunks(nz)
    cells = fields.shape[3]
    count = residual.shape[0]
    resid = jnp.transpose(residual, (1, 2, 0)).reshape(2 * FRAMES, count)
    vmem = pl.BlockSpec(memory_space=pltpu.VMEM)
    field_shape = (2, 3, PER_GROUP, cells)
    dma = pltpu.SemaphoreType.DMA
    gradient = pl.pallas_call(
        functools.partial(kernel, (nz, nx, ny)),
        out_shape=jax.ShapeDtypeStruct((2 * FRAMES, 128), F32),
        in_specs=[pl.BlockSpec(memory_space=pltpu.HBM)] * 6,
        out_specs=vmem,
        scratch_shapes=[
            pltpu.VMEM((2 * FRAMES, count), F32),
            pltpu.VMEM((1, count), jnp.int32),
            pltpu.VMEM((3, count), jnp.int32),
            pltpu.VMEM((1, count), jnp.int32),
            pltpu.VMEM((2, count), jnp.int32),
            pltpu.VMEM(field_shape, BF16),
            pltpu.VMEM(field_shape, BF16),
            pltpu.VMEM(field_shape, BF16),
            pltpu.VMEM((lines, nz, 128), F32),
            pltpu.VMEM((groups, 128), F32),
            pltpu.VMEM((nz, lines, 128), F32),
            pltpu.VMEM((64, 128), F32),
            pltpu.VMEM((WINDOW, 128), F32),
            pltpu.VMEM((ny - 1, WINDOW, 128), F32),
            pltpu.VMEM((384, 256), BF16),
            pltpu.VMEM((nz, 2, nx, 16, 128), F32),
            pltpu.VMEM((nz - 1, nx, 16, 128), F32),
            pltpu.VMEM((nz - 1, nx, 16, 128), BF16),
            pltpu.VMEM((nz - 1 - far, nx, 16, 128), BF16),
            pltpu.VMEM((lines, 16, 128), BF16),
            pltpu.VMEM((lines - 1, 16, 128), BF16),
            pltpu.VMEM((far, nx - 1, 16, 128), BF16),
            pltpu.VMEM((far, 16, 128), BF16),
            pltpu.VMEM((far, 16, 128), BF16),
            dma((5,)), dma, dma((2,)), dma((2, nz)),
            dma((3,)), dma((3,)),
            dma, dma((nz - 1,)), dma, dma((nz - 1 - far,)), dma, dma,
            dma, dma((far,)), dma, dma,
        ],
        compiler_params=pltpu.CompilerParams(
            collective_id=0, has_side_effects=True, vmem_limit_bytes=40 * 1024 * 1024
        ),
    )(*(
        pltpu.with_memory_space_constraint(value, pltpu.HBM)
        for value in (fields, resid, quad_group.T, offsets.T, b_step.T, sides.T)
    ))
    return gradient.reshape(FRAMES, 2, 1, 128)


def solution(mesh):
    return jax.shard_map(
        local,
        mesh=mesh,
        in_specs=(
            P(None, None, "elec", "cell"),
            P(("elec", "cell"), None, None),
            P(("elec", "cell"), None),
            P(("elec", "cell"), None),
            P(("elec", "cell"), None),
            P(("elec", "cell"), None),
        ),
        out_specs=P(None, None, "cell", "elec"),
        check_vma=False,
    )
```

```python
import functools

import jax
import jax.numpy as jnp
from jax import lax
from jax.experimental import pallas as pl
from jax.experimental.pallas import tpu as pltpu
from jax.sharding import PartitionSpec as P

X_CHIPS = 4
PER_GROUP = 8
FRAMES = 8
CAP = 4
SLOT = 32
WINDOW = 3 * PER_GROUP
F32 = jnp.float32
BF16 = jnp.bfloat16


def iota(shape, dim):
    return lax.broadcasted_iota(jnp.int32, shape, dim)


def split3(value):
    high = value.astype(BF16)
    rest = value - high.astype(F32)
    middle = rest.astype(BF16)
    low = (rest - middle.astype(F32)).astype(BF16)
    return high, middle, low


def dot_nt(left, right):
    return lax.dot_general(left, right, (((1,), (1,)), ((), ())), preferred_element_type=F32)


def far_first(count):
    return sorted(range(1, count), key=lambda d: -min(d, count - d))


def drain(ref, sem):
    pltpu.make_async_copy(ref, ref, sem).wait()


def kernel(
    sizes,
    fields, resid_in, group_in, offs_in, bstep_in, sides_in,
    out,
    resid, group, offs, bstep, sides,
    own, low, high,
    slots, a_buf, b_send, b_buf, c_send, c_buf, weights,
    part, core_recv, sums, rounded, shares,
    in_sem, own_sem, halo_send_sem, halo_recv_sem,
    stage_send_sem, stage_recv_sem,
    core_send_sem, core_recv_sem, share_send_sem, share_recv_sem,
):
    nz, nx, ny = sizes
    lines = 2 * nx
    groups = nz * lines
    quads = resid.shape[1]
    halo_ends = (0, 3 * nz // 8)
    elec = lax.axis_index("elec")
    cell = lax.axis_index("cell")
    z = elec // lines
    p = elec % lines
    x = p // 2
    core = p % 2

    def line_peer(d):
        return {"elec": z * lines + (p + d) % lines}

    def z_peer(d):
        return {"elec": ((z + d) % nz) * lines + p}

    def chip_peer(dz, dx):
        return {"elec": ((z + dz) % nz) * lines + ((x + dx) % nx) * 2 + core}

    def y_peer(d):
        return {"cell": (cell + d) % ny}

    core_peer = {"elec": z * lines + x * 2 + 1 - core}
    next_peer = {"elec": (elec + 1) % groups}
    prev_peer = {"elec": (elec + groups - 1) % groups}

    if groups < 64:
        b_buf[...] = jnp.zeros_like(b_buf)
    barrier = pltpu.get_barrier_semaphore()
    peers = (
        [y_peer(d) for d in far_first(ny)]
        + [chip_peer(dz, dx) for dz in far_first(nz) for dx in range(nx)]
        + [line_peer(d) for d in far_first(lines)]
        + [next_peer, prev_peer]
    )
    for peer in peers:
        pl.semaphore_signal(barrier, inc=1, device_id=peer, device_id_type=pl.DeviceIdType.MESH)

    inputs = [
        pltpu.make_async_copy(source, target, in_sem.at[number])
        for number, (source, target) in enumerate(
            zip((resid_in, group_in, offs_in, bstep_in, sides_in), (resid, group, offs, bstep, sides))
        )
    ]
    for copy in inputs:
        copy.start()

    own_copy = pltpu.make_async_copy(fields, own, own_sem)
    own_copy.start()

    def send(source, target, send_sem, recv_sem, peer):
        pltpu.make_async_remote_copy(
            src_ref=source, dst_ref=target, send_sem=send_sem, recv_sem=recv_sem,
            device_id=peer, device_id_type=pl.DeviceIdType.MESH,
        ).start()

    def z_step(s):
        return nz // 2 + (1 - 2 * (s % 2)) * ((s + 1) // 2)

    chunk = lines * 128

    def chunk_lanes(row, s):
        return pl.ds(pl.multiple_of(((row + z_step(s)) % nz) * chunk, chunk), chunk)

    def send_halo(s):
        for way, (peer, target, turn) in enumerate(((next_peer, low, 1), (prev_peer, high, groups - 1))):
            lanes = chunk_lanes((elec + turn) % groups // lines, s)
            send(fields.at[:, :, :, lanes], target.at[:, :, :, lanes],
                 halo_send_sem.at[way], halo_recv_sem.at[way, s], peer)

    for copy in inputs:
        copy.wait()
    owner = group[...]
    source_a = offs[pl.ds(0, 1), :]
    source_b = (source_a + bstep[...]) % PER_GROUP
    group_m = jnp.clip(owner + sides[pl.ds(0, 1), :], 0, groups - 1)
    group_n = jnp.clip(owner + sides[pl.ds(1, 1), :], 0, groups - 1)
    column_m = (group_m - owner + 1) * PER_GROUP + offs[pl.ds(1, 1), :]
    column_n = (group_n - owner + 1) * PER_GROUP + offs[pl.ds(2, 1), :]
    row = iota((groups, quads), 0)
    names = (row % nz) * lines + row // nz
    member = jnp.where(names == owner, 1.0, 0.0).astype(F32)
    earlier = jnp.where(iota((quads, quads), 0) < iota((quads, quads), 1), 1.0, 0.0).astype(BF16)
    before = jnp.dot(member.astype(BF16), earlier, preferred_element_type=F32)
    rank = jnp.sum(member * before, axis=0, keepdims=True)
    place = iota((8, quads), 0)
    indices = jnp.where(
        place == 0, source_a,
        jnp.where(place == 1, source_b, jnp.where(place == 2, column_m, jnp.where(place == 3, column_n, 0))),
    ).astype(F32)
    real = -resid[pl.ds(0, FRAMES, stride=2), :]
    imag = -resid[pl.ds(1, FRAMES, stride=2), :]
    entry = jnp.concatenate([real, imag, indices, jnp.zeros_like(indices)], axis=0)
    entries = jnp.concatenate(
        [jnp.where(rank == float(k), entry, 0.0) for k in range(CAP)], axis=0
    )
    named = member.astype(BF16)
    sorted_rows = sum(dot_nt(named, piece) for piece in split3(entries)[::-1])
    for line in range(lines):
        slots[line] = sorted_rows[line * nz:(line + 1) * nz, :]

    pl.semaphore_wait(barrier, len(peers))

    for d in far_first(lines):
        send(slots.at[(p + d) % lines], a_buf.at[pl.ds((d - 1) * nz, nz)],
             stage_send_sem.at[0], stage_recv_sem.at[0], line_peer(d))
    for s in range(0, halo_ends[0]):
        send_halo(s)
    a_buf[pl.ds((lines - 1) * nz, nz), :] = slots[p]
    own_copy.wait()
    arrived = a_buf.at[pl.ds(0, (lines - 1) * nz)]
    drain(arrived, stage_recv_sem.at[0])
    for to in range(nz):
        b_send[to] = a_buf[pl.ds(to, lines, stride=nz), :]
    for d in far_first(nz):
        send(b_send.at[(z + d) % nz], b_buf.at[pl.ds((d - 1) * lines, lines)],
             stage_send_sem.at[1], stage_recv_sem.at[1], z_peer(d))
    for s in range(halo_ends[0], halo_ends[1]):
        send_halo(s)
    b_buf[pl.ds((nz - 1) * lines, lines), :] = b_send[z]
    drain(b_buf.at[pl.ds(0, (nz - 1) * lines)], stage_recv_sem.at[1])

    received = b_buf[...]
    both = jnp.concatenate([received, pltpu.roll(received, 64, 1)], axis=0)
    turned = both.T
    terms = []
    columns = []
    for half in range(2):
        block = turned[half * SLOT:(half + 1) * SLOT, :]
        at_a = block[16:17].astype(jnp.int32)
        at_b = block[17:18].astype(jnp.int32)
        at_m = block[18:19].astype(jnp.int32)
        at_n = block[19:20].astype(jnp.int32)
        place = iota((PER_GROUP, 128), 0)
        sign = jnp.where(place == at_a, 1.0, 0.0) - jnp.where(place == at_b, 1.0, 0.0)
        terms.append(jnp.concatenate([block[k:k + 1] * sign for k in range(2 * FRAMES)], axis=0))
        place = iota((WINDOW, 128), 0)
        columns.append((jnp.where(place == at_m, 1.0, 0.0) - jnp.where(place == at_n, 1.0, 0.0)).astype(BF16))
    band = jnp.zeros((WINDOW, 128), F32)
    for half in range(2):
        for piece in split3(terms[half])[::-1]:
            band = band + dot_nt(columns[half], piece)
    c_send[...] = band
    for d in far_first(ny):
        send(c_send, c_buf.at[d - 1], stage_send_sem.at[2], stage_recv_sem.at[2], y_peer(d))
    for s in range(halo_ends[1], nz):
        send_halo(s)
    drain(c_buf, stage_recv_sem.at[2])
    for d in range(ny - 1):
        band = band + c_buf[d]
    band = band.astype(BF16).astype(F32)
    upper = jnp.concatenate([band, jnp.zeros((128 - WINDOW, 128), F32)], axis=0).T
    lower = jnp.concatenate([upper[64:], -upper[:64]], axis=0)
    first = upper + pltpu.roll(lower, WINDOW, 1)
    second = pltpu.roll(first, 2 * WINDOW, 1)
    third = pltpu.roll(first, 4 * WINDOW, 1)
    lane = iota((128, 128), 1)
    nothing = jnp.zeros((128, 128), BF16)
    weights[pl.ds(0, 128), pl.ds(0, 128)] = first.astype(BF16)
    weights[pl.ds(0, 128), pl.ds(128, 128)] = nothing
    weights[pl.ds(128, 128), pl.ds(0, 128)] = second.astype(BF16)
    weights[pl.ds(128, 128), pl.ds(128, 128)] = nothing
    weights[pl.ds(256, 128), pl.ds(0, 128)] = jnp.where(lane >= 4 * WINDOW, third, 0.0).astype(BF16)
    weights[pl.ds(256, 128), pl.ds(128, 128)] = jnp.where(lane < 2 * WINDOW, third, 0.0).astype(BF16)

    sublane = iota((PER_GROUP, 128), 0)

    def fold(first, second, width):
        keep = sublane % (2 * width) < width
        return jnp.where(keep, first, second) + pltpu.roll(
            jnp.where(keep, second, first), PER_GROUP - width, 0
        )

    def collect(rows):
        for width in (1, 2, 4):
            rows = [fold(rows[k], rows[k + 1], width) for k in range(0, len(rows), 2)]
        return rows[0]

    def compute(s):
        base = ((z + z_step(s)) % nz) * chunk
        arrived_lanes = chunk_lanes(z, s)
        drain(low.at[:, :, :, arrived_lanes], halo_recv_sem.at[0, s])
        drain(high.at[:, :, :, arrived_lanes], halo_recv_sem.at[1, s])
        matrix = weights[...][:, :3 * 2 * WINDOW]
        for chip in range(nx):
            lanes = pl.ds(pl.multiple_of(base + chip * 256, 256), 256)
            middle = [[own[i, c, :, lanes].astype(F32) for i in range(2)] for c in range(3)]
            window = []
            for c in range(3):
                for i in range(2):
                    window += [low[i, c, :, lanes].astype(F32), middle[c][i], high[i, c, :, lanes].astype(F32)]
            window = jnp.concatenate(window, axis=0).astype(BF16)
            adjoint = jnp.dot(matrix, window, preferred_element_type=F32)
            for k in range(2):
                half = slice(k * 128, (k + 1) * 128)
                real = []
                imag = []
                for t in range(FRAMES):
                    total_real = jnp.zeros((PER_GROUP, 128), F32)
                    total_imag = jnp.zeros((PER_GROUP, 128), F32)
                    for c in range(3):
                        at = c * 128 + t * 8
                        adj_real = adjoint[at:at + 8, half]
                        adj_imag = adjoint[at + 64:at + 72, half]
                        mid_real = middle[c][0][:, half]
                        mid_imag = middle[c][1][:, half]
                        total_real = total_real + mid_real * adj_real + mid_imag * adj_imag
                        total_imag = total_imag + mid_real * adj_imag - mid_imag * adj_real
                    real.append(total_real)
                    imag.append(total_imag)
                part[s, k, chip, pl.ds(0, 8), :] = collect(real)
                part[s, k, chip, pl.ds(8, 8), :] = collect(imag)
        send(part.at[s, 1 - core], core_recv.at[s], core_send_sem, core_recv_sem.at[s], core_peer)

    def share(s, d):
        send(rounded.at[s, (x + d) % nx], shares.at[s * nx + (d + nx - 1) % nx],
             share_send_sem, share_recv_sem.at[s], chip_peer(z_step(s), d))

    def add_core(s):
        drain(core_recv.at[s], core_recv_sem.at[s])
        both_cores = part[s, core] + core_recv[s]
        sums[s] = both_cores
        rounded[s] = both_cores.astype(BF16)
        for d in range(1, nx):
            share(s, d)

        @pl.when(s < nz - 1)
        def _():
            share(s, 0)

    core_lag = 2

    def step(s, carry):
        @pl.when(s < nz)
        def _():
            compute(s)

        @pl.when(s >= core_lag)
        def _():
            add_core(s - core_lag)

        return carry

    lax.fori_loop(0, nz + core_lag, step, 0)
    total = sums[nz - 1, x]
    for s in range(nz):
        count = nx if s < nz - 1 else nx - 1
        drain(shares.at[pl.ds(s * nx, count)], share_recv_sem.at[s])
        for d in range(count):
            total = total + shares[s * nx + d].astype(F32)
    out[pl.ds(0, FRAMES, stride=2), :] = total[0:8]
    out[pl.ds(1, FRAMES, stride=2), :] = total[8:16]

    drain(low, halo_send_sem.at[0])
    drain(high, halo_send_sem.at[1])
    drain(arrived, stage_send_sem.at[0])
    drain(b_buf.at[pl.ds(0, (nz - 1) * lines)], stage_send_sem.at[1])
    drain(c_buf, stage_send_sem.at[2])
    drain(core_recv, core_send_sem)
    drain(shares.at[pl.ds(0, nz * nx - 1)], share_send_sem)


def local(fields, residual, quad_group, offsets, b_step, sides):
    groups = lax.axis_size("elec")
    ny = lax.axis_size("cell")
    nx = X_CHIPS
    lines = 2 * nx
    nz = groups // lines
    cells = fields.shape[3]
    count = residual.shape[0]
    resid = jnp.transpose(residual, (1, 2, 0)).reshape(2 * FRAMES, count)
    vmem = pl.BlockSpec(memory_space=pltpu.VMEM)
    field_shape = (2, 3, PER_GROUP, cells)
    dma = pltpu.SemaphoreType.DMA
    gradient = pl.pallas_call(
        functools.partial(kernel, (nz, nx, ny)),
        out_shape=jax.ShapeDtypeStruct((2 * FRAMES, 128), F32),
        in_specs=[pl.BlockSpec(memory_space=pltpu.HBM)] * 6,
        out_specs=vmem,
        scratch_shapes=[
            pltpu.VMEM((2 * FRAMES, count), F32),
            pltpu.VMEM((1, count), jnp.int32),
            pltpu.VMEM((3, count), jnp.int32),
            pltpu.VMEM((1, count), jnp.int32),
            pltpu.VMEM((2, count), jnp.int32),
            pltpu.VMEM(field_shape, BF16),
            pltpu.VMEM(field_shape, BF16),
            pltpu.VMEM(field_shape, BF16),
            pltpu.VMEM((lines, nz, 128), F32),
            pltpu.VMEM((groups, 128), F32),
            pltpu.VMEM((nz, lines, 128), F32),
            pltpu.VMEM((64, 128), F32),
            pltpu.VMEM((WINDOW, 128), F32),
            pltpu.VMEM((ny - 1, WINDOW, 128), F32),
            pltpu.VMEM((384, 256), BF16),
            pltpu.VMEM((nz, 2, nx, 16, 128), F32),
            pltpu.VMEM((nz, nx, 16, 128), F32),
            pltpu.VMEM((nz, nx, 16, 128), F32),
            pltpu.VMEM((nz, nx, 16, 128), BF16),
            pltpu.VMEM((nz * nx, 16, 128), BF16),
            dma((5,)), dma, dma((2,)), dma((2, nz)),
            dma((3,)), dma((3,)),
            dma, dma((nz,)), dma, dma((nz,)),
        ],
        compiler_params=pltpu.CompilerParams(
            collective_id=0, has_side_effects=True, vmem_limit_bytes=40 * 1024 * 1024
        ),
    )(*(
        pltpu.with_memory_space_constraint(value, pltpu.HBM)
        for value in (fields, resid, quad_group.T, offsets.T, b_step.T, sides.T)
    ))
    return gradient.reshape(FRAMES, 2, 1, 128)


def solution(mesh):
    return jax.shard_map(
        local,
        mesh=mesh,
        in_specs=(
            P(None, None, "elec", "cell"),
            P(("elec", "cell"), None, None),
            P(("elec", "cell"), None),
            P(("elec", "cell"), None),
            P(("elec", "cell"), None),
            P(("elec", "cell"), None),
        ),
        out_specs=P(None, None, "cell", "elec"),
        check_vma=False,
    )
```

```python
import functools

import jax
import jax.numpy as jnp
from jax import lax
from jax.experimental import pallas as pl
from jax.experimental.pallas import tpu as pltpu
from jax.sharding import PartitionSpec as P

X_CHIPS = 4
PER_GROUP = 8
FRAMES = 8
CAP = 4
SLOT = 32
WINDOW = 3 * PER_GROUP
F32 = jnp.float32
BF16 = jnp.bfloat16


def iota(shape, dim):
    return lax.broadcasted_iota(jnp.int32, shape, dim)


def split3(value):
    high = value.astype(BF16)
    rest = value - high.astype(F32)
    middle = rest.astype(BF16)
    low = (rest - middle.astype(F32)).astype(BF16)
    return high, middle, low


def dot_nt(left, right):
    return lax.dot_general(left, right, (((1,), (1,)), ((), ())), preferred_element_type=F32)


def far_first(count):
    return sorted(range(1, count), key=lambda d: -min(d, count - d))


def drain(ref, sem):
    pltpu.make_async_copy(ref, ref, sem).wait()


def kernel(
    sizes,
    fields, resid_in, group_in, offs_in, bstep_in, sides_in,
    out,
    resid, group, offs, bstep, sides,
    own, low, high,
    slots, a_buf, b_send, b_buf, c_send, c_buf, weights,
    part, core_recv, sums, rounded, shares,
    in_sem, own_sem, halo_send_sem, halo_recv_sem,
    stage_send_sem, stage_recv_sem,
    core_send_sem, core_recv_sem, share_send_sem, share_recv_sem,
):
    nz, nx, ny = sizes
    lines = 2 * nx
    groups = nz * lines
    quads = resid.shape[1]
    halo_ends = (0, nz // 4)
    elec = lax.axis_index("elec")
    cell = lax.axis_index("cell")
    z = elec // lines
    p = elec % lines
    x = p // 2
    core = p % 2

    def line_peer(d):
        return {"elec": z * lines + (p + d) % lines}

    def z_peer(d):
        return {"elec": ((z + d) % nz) * lines + p}

    def chip_peer(dz, dx):
        return {"elec": ((z + dz) % nz) * lines + ((x + dx) % nx) * 2 + core}

    def y_peer(d):
        return {"cell": (cell + d) % ny}

    core_peer = {"elec": z * lines + x * 2 + 1 - core}
    next_peer = {"elec": (elec + 1) % groups}
    prev_peer = {"elec": (elec + groups - 1) % groups}

    if groups < 64:
        b_buf[...] = jnp.zeros_like(b_buf)
    barrier = pltpu.get_barrier_semaphore()
    peers = (
        [y_peer(d) for d in far_first(ny)]
        + [chip_peer(dz, dx) for dz in far_first(nz) for dx in range(nx)]
        + [line_peer(d) for d in far_first(lines)]
        + [next_peer, prev_peer]
    )
    for peer in peers:
        pl.semaphore_signal(barrier, inc=1, device_id=peer, device_id_type=pl.DeviceIdType.MESH)

    inputs = [
        pltpu.make_async_copy(source, target, in_sem.at[number])
        for number, (source, target) in enumerate(
            zip((resid_in, group_in, offs_in, bstep_in, sides_in), (resid, group, offs, bstep, sides))
        )
    ]
    for copy in inputs:
        copy.start()

    own_copy = pltpu.make_async_copy(fields, own, own_sem)
    own_copy.start()

    def send(source, target, send_sem, recv_sem, peer):
        pltpu.make_async_remote_copy(
            src_ref=source, dst_ref=target, send_sem=send_sem, recv_sem=recv_sem,
            device_id=peer, device_id_type=pl.DeviceIdType.MESH,
        ).start()

    def z_step(s):
        return nz // 2 + (1 - 2 * (s % 2)) * ((s + 1) // 2)

    chunk = lines * 128

    def chunk_lanes(row, s):
        return pl.ds(pl.multiple_of(((row + z_step(s)) % nz) * chunk, chunk), chunk)

    def send_halo(s):
        for way, (peer, target, turn) in enumerate(((next_peer, low, 1), (prev_peer, high, groups - 1))):
            lanes = chunk_lanes((elec + turn) % groups // lines, s)
            send(fields.at[:, :, :, lanes], target.at[:, :, :, lanes],
                 halo_send_sem.at[way], halo_recv_sem.at[way, s], peer)

    for copy in inputs:
        copy.wait()
    owner = group[...]
    source_a = offs[pl.ds(0, 1), :]
    source_b = (source_a + bstep[...]) % PER_GROUP
    group_m = jnp.clip(owner + sides[pl.ds(0, 1), :], 0, groups - 1)
    group_n = jnp.clip(owner + sides[pl.ds(1, 1), :], 0, groups - 1)
    column_m = (group_m - owner + 1) * PER_GROUP + offs[pl.ds(1, 1), :]
    column_n = (group_n - owner + 1) * PER_GROUP + offs[pl.ds(2, 1), :]
    row = iota((groups, quads), 0)
    names = (row % nz) * lines + row // nz
    member = jnp.where(names == owner, 1.0, 0.0).astype(F32)
    earlier = jnp.where(iota((quads, quads), 0) < iota((quads, quads), 1), 1.0, 0.0).astype(BF16)
    before = jnp.dot(member.astype(BF16), earlier, preferred_element_type=F32)
    rank = jnp.sum(member * before, axis=0, keepdims=True)
    place = iota((8, quads), 0)
    indices = jnp.where(
        place == 0, source_a,
        jnp.where(place == 1, source_b, jnp.where(place == 2, column_m, jnp.where(place == 3, column_n, 0))),
    ).astype(F32)
    real = -resid[pl.ds(0, FRAMES, stride=2), :]
    imag = -resid[pl.ds(1, FRAMES, stride=2), :]
    entry = jnp.concatenate([real, imag, indices, jnp.zeros_like(indices)], axis=0)
    entries = jnp.concatenate(
        [jnp.where(rank == float(k), entry, 0.0) for k in range(CAP)], axis=0
    )
    named = member.astype(BF16)
    sorted_rows = sum(dot_nt(named, piece) for piece in split3(entries)[::-1])
    for line in range(lines):
        slots[line] = sorted_rows[line * nz:(line + 1) * nz, :]

    pl.semaphore_wait(barrier, len(peers))

    for d in far_first(lines):
        send(slots.at[(p + d) % lines], a_buf.at[pl.ds((d - 1) * nz, nz)],
             stage_send_sem.at[0], stage_recv_sem.at[0], line_peer(d))
    for s in range(0, halo_ends[0]):
        send_halo(s)
    a_buf[pl.ds((lines - 1) * nz, nz), :] = slots[p]
    own_copy.wait()
    arrived = a_buf.at[pl.ds(0, (lines - 1) * nz)]
    drain(arrived, stage_recv_sem.at[0])
    for to in range(nz):
        b_send[to] = a_buf[pl.ds(to, lines, stride=nz), :]
    for d in far_first(nz):
        send(b_send.at[(z + d) % nz], b_buf.at[pl.ds((d - 1) * lines, lines)],
             stage_send_sem.at[1], stage_recv_sem.at[1], z_peer(d))
    for s in range(halo_ends[0], halo_ends[1]):
        send_halo(s)
    b_buf[pl.ds((nz - 1) * lines, lines), :] = b_send[z]
    drain(b_buf.at[pl.ds(0, (nz - 1) * lines)], stage_recv_sem.at[1])

    received = b_buf[...]
    both = jnp.concatenate([received, pltpu.roll(received, 64, 1)], axis=0)
    turned = both.T
    terms = []
    columns = []
    for half in range(2):
        block = turned[half * SLOT:(half + 1) * SLOT, :]
        at_a = block[16:17].astype(jnp.int32)
        at_b = block[17:18].astype(jnp.int32)
        at_m = block[18:19].astype(jnp.int32)
        at_n = block[19:20].astype(jnp.int32)
        place = iota((PER_GROUP, 128), 0)
        sign = jnp.where(place == at_a, 1.0, 0.0) - jnp.where(place == at_b, 1.0, 0.0)
        terms.append(jnp.concatenate([block[k:k + 1] * sign for k in range(2 * FRAMES)], axis=0))
        place = iota((WINDOW, 128), 0)
        columns.append((jnp.where(place == at_m, 1.0, 0.0) - jnp.where(place == at_n, 1.0, 0.0)).astype(BF16))
    band = jnp.zeros((WINDOW, 128), F32)
    for half in range(2):
        for piece in split3(terms[half])[::-1]:
            band = band + dot_nt(columns[half], piece)
    c_send[...] = band
    for d in far_first(ny):
        send(c_send, c_buf.at[d - 1], stage_send_sem.at[2], stage_recv_sem.at[2], y_peer(d))
    for s in range(halo_ends[1], nz):
        send_halo(s)
    drain(c_buf, stage_recv_sem.at[2])
    for d in range(ny - 1):
        band = band + c_buf[d]
    band = band.astype(BF16).astype(F32)
    upper = jnp.concatenate([band, jnp.zeros((128 - WINDOW, 128), F32)], axis=0).T
    lower = jnp.concatenate([upper[64:], -upper[:64]], axis=0)
    first = upper + pltpu.roll(lower, WINDOW, 1)
    second = pltpu.roll(first, 2 * WINDOW, 1)
    third = pltpu.roll(first, 4 * WINDOW, 1)
    lane = iota((128, 128), 1)
    nothing = jnp.zeros((128, 128), BF16)
    weights[pl.ds(0, 128), pl.ds(0, 128)] = first.astype(BF16)
    weights[pl.ds(0, 128), pl.ds(128, 128)] = nothing
    weights[pl.ds(128, 128), pl.ds(0, 128)] = second.astype(BF16)
    weights[pl.ds(128, 128), pl.ds(128, 128)] = nothing
    weights[pl.ds(256, 128), pl.ds(0, 128)] = jnp.where(lane >= 4 * WINDOW, third, 0.0).astype(BF16)
    weights[pl.ds(256, 128), pl.ds(128, 128)] = jnp.where(lane < 2 * WINDOW, third, 0.0).astype(BF16)

    sublane = iota((PER_GROUP, 128), 0)

    def fold(first, second, width):
        keep = sublane % (2 * width) < width
        return jnp.where(keep, first, second) + pltpu.roll(
            jnp.where(keep, second, first), PER_GROUP - width, 0
        )

    def collect(rows):
        for width in (1, 2, 4):
            rows = [fold(rows[k], rows[k + 1], width) for k in range(0, len(rows), 2)]
        return rows[0]

    def compute(s):
        base = ((z + z_step(s)) % nz) * chunk
        arrived_lanes = chunk_lanes(z, s)
        drain(low.at[:, :, :, arrived_lanes], halo_recv_sem.at[0, s])
        drain(high.at[:, :, :, arrived_lanes], halo_recv_sem.at[1, s])
        matrix = weights[...][:, :3 * 2 * WINDOW]
        for chip in range(nx):
            lanes = pl.ds(pl.multiple_of(base + chip * 256, 256), 256)
            middle = [[own[i, c, :, lanes].astype(F32) for i in range(2)] for c in range(3)]
            window = []
            for c in range(3):
                for i in range(2):
                    window += [low[i, c, :, lanes].astype(F32), middle[c][i], high[i, c, :, lanes].astype(F32)]
            window = jnp.concatenate(window, axis=0).astype(BF16)
            adjoint = jnp.dot(matrix, window, preferred_element_type=F32)
            for k in range(2):
                half = slice(k * 128, (k + 1) * 128)
                real = []
                imag = []
                for t in range(FRAMES):
                    total_real = jnp.zeros((PER_GROUP, 128), F32)
                    total_imag = jnp.zeros((PER_GROUP, 128), F32)
                    for c in range(3):
                        at = c * 128 + t * 8
                        adj_real = adjoint[at:at + 8, half]
                        adj_imag = adjoint[at + 64:at + 72, half]
                        mid_real = middle[c][0][:, half]
                        mid_imag = middle[c][1][:, half]
                        total_real = total_real + mid_real * adj_real + mid_imag * adj_imag
                        total_imag = total_imag + mid_real * adj_imag - mid_imag * adj_real
                    real.append(total_real)
                    imag.append(total_imag)
                part[s, k, chip, pl.ds(0, 8), :] = collect(real)
                part[s, k, chip, pl.ds(8, 8), :] = collect(imag)
        send(part.at[s, 1 - core], core_recv.at[s], core_send_sem, core_recv_sem.at[s], core_peer)

    def share(s, d):
        send(rounded.at[s, (x + d) % nx], shares.at[s * nx + (d + nx - 1) % nx],
             share_send_sem, share_recv_sem.at[s], chip_peer(z_step(s), d))

    def add_core(s):
        drain(core_recv.at[s], core_recv_sem.at[s])
        both_cores = part[s, core] + core_recv[s]
        sums[s] = both_cores
        rounded[s] = both_cores.astype(BF16)
        for d in range(1, nx):
            share(s, d)

        @pl.when(s < nz - 1)
        def _():
            share(s, 0)

    core_lag = 2

    def step(s, carry):
        @pl.when(s < nz)
        def _():
            compute(s)

        @pl.when(s >= core_lag)
        def _():
            add_core(s - core_lag)

        return carry

    lax.fori_loop(0, nz + core_lag, step, 0)
    total = sums[nz - 1, x]
    for s in range(nz):
        count = nx if s < nz - 1 else nx - 1
        drain(shares.at[pl.ds(s * nx, count)], share_recv_sem.at[s])
        for d in range(count):
            total = total + shares[s * nx + d].astype(F32)
    out[pl.ds(0, FRAMES, stride=2), :] = total[0:8]
    out[pl.ds(1, FRAMES, stride=2), :] = total[8:16]

    drain(low, halo_send_sem.at[0])
    drain(high, halo_send_sem.at[1])
    drain(arrived, stage_send_sem.at[0])
    drain(b_buf.at[pl.ds(0, (nz - 1) * lines)], stage_send_sem.at[1])
    drain(c_buf, stage_send_sem.at[2])
    drain(core_recv, core_send_sem)
    drain(shares.at[pl.ds(0, nz * nx - 1)], share_send_sem)


def local(fields, residual, quad_group, offsets, b_step, sides):
    groups = lax.axis_size("elec")
    ny = lax.axis_size("cell")
    nx = X_CHIPS
    lines = 2 * nx
    nz = groups // lines
    cells = fields.shape[3]
    count = residual.shape[0]
    resid = jnp.transpose(residual, (1, 2, 0)).reshape(2 * FRAMES, count)
    vmem = pl.BlockSpec(memory_space=pltpu.VMEM)
    field_shape = (2, 3, PER_GROUP, cells)
    dma = pltpu.SemaphoreType.DMA
    gradient = pl.pallas_call(
        functools.partial(kernel, (nz, nx, ny)),
        out_shape=jax.ShapeDtypeStruct((2 * FRAMES, 128), F32),
        in_specs=[pl.BlockSpec(memory_space=pltpu.HBM)] * 6,
        out_specs=vmem,
        scratch_shapes=[
            pltpu.VMEM((2 * FRAMES, count), F32),
            pltpu.VMEM((1, count), jnp.int32),
            pltpu.VMEM((3, count), jnp.int32),
            pltpu.VMEM((1, count), jnp.int32),
            pltpu.VMEM((2, count), jnp.int32),
            pltpu.VMEM(field_shape, BF16),
            pltpu.VMEM(field_shape, BF16),
            pltpu.VMEM(field_shape, BF16),
            pltpu.VMEM((lines, nz, 128), F32),
            pltpu.VMEM((groups, 128), F32),
            pltpu.VMEM((nz, lines, 128), F32),
            pltpu.VMEM((64, 128), F32),
            pltpu.VMEM((WINDOW, 128), F32),
            pltpu.VMEM((ny - 1, WINDOW, 128), F32),
            pltpu.VMEM((384, 256), BF16),
            pltpu.VMEM((nz, 2, nx, 16, 128), F32),
            pltpu.VMEM((nz, nx, 16, 128), F32),
            pltpu.VMEM((nz, nx, 16, 128), F32),
            pltpu.VMEM((nz, nx, 16, 128), BF16),
            pltpu.VMEM((nz * nx, 16, 128), BF16),
            dma((5,)), dma, dma((2,)), dma((2, nz)),
            dma((3,)), dma((3,)),
            dma, dma((nz,)), dma, dma((nz,)),
        ],
        compiler_params=pltpu.CompilerParams(
            collective_id=0, has_side_effects=True, vmem_limit_bytes=40 * 1024 * 1024
        ),
    )(*(
        pltpu.with_memory_space_constraint(value, pltpu.HBM)
        for value in (fields, resid, quad_group.T, offsets.T, b_step.T, sides.T)
    ))
    return gradient.reshape(FRAMES, 2, 1, 128)


def solution(mesh):
    return jax.shard_map(
        local,
        mesh=mesh,
        in_specs=(
            P(None, None, "elec", "cell"),
            P(("elec", "cell"), None, None),
            P(("elec", "cell"), None),
            P(("elec", "cell"), None),
            P(("elec", "cell"), None),
            P(("elec", "cell"), None),
        ),
        out_specs=P(None, None, "cell", "elec"),
        check_vma=False,
    )
```

```python
import functools

import jax
import jax.numpy as jnp
from jax import lax
from jax.experimental import pallas as pl
from jax.experimental.pallas import tpu as pltpu
from jax.sharding import PartitionSpec as P

X_CHIPS = 4
PER_GROUP = 8
FRAMES = 8
CAP = 4
SLOT = 32
WINDOW = 3 * PER_GROUP
F32 = jnp.float32
BF16 = jnp.bfloat16


def iota(shape, dim):
    return lax.broadcasted_iota(jnp.int32, shape, dim)


def split3(value):
    high = value.astype(BF16)
    rest = value - high.astype(F32)
    middle = rest.astype(BF16)
    low = (rest - middle.astype(F32)).astype(BF16)
    return high, middle, low


def dot_nt(left, right):
    return lax.dot_general(left, right, (((1,), (1,)), ((), ())), preferred_element_type=F32)


def far_first(count):
    return sorted(range(1, count), key=lambda d: -min(d, count - d))


def drain(ref, sem):
    pltpu.make_async_copy(ref, ref, sem).wait()


def kernel(
    sizes,
    fields, resid_in, group_in, offs_in, bstep_in, sides_in,
    out,
    resid, group, offs, bstep, sides,
    own, low, high,
    slots, a_buf, b_send, b_buf, c_send, c_buf, weights,
    part, core_recv, sums, rounded, shares,
    in_sem, own_sem, halo_send_sem, halo_recv_sem,
    stage_send_sem, stage_recv_sem,
    core_send_sem, core_recv_sem, share_send_sem, share_recv_sem,
):
    nz, nx, ny = sizes
    lines = 2 * nx
    groups = nz * lines
    quads = resid.shape[1]
    halo_ends = (0, nz // 4)
    elec = lax.axis_index("elec")
    cell = lax.axis_index("cell")
    z = elec // lines
    p = elec % lines
    x = p // 2
    core = p % 2

    inputs = [
        pltpu.make_async_copy(source, target, in_sem.at[number])
        for number, (source, target) in enumerate(
            zip((resid_in, group_in, offs_in, bstep_in, sides_in), (resid, group, offs, bstep, sides))
        )
    ]
    for copy in inputs:
        copy.start()

    def line_peer(d):
        return {"elec": z * lines + (p + d) % lines}

    def z_peer(d):
        return {"elec": ((z + d) % nz) * lines + p}

    def chip_peer(dz, dx):
        return {"elec": ((z + dz) % nz) * lines + ((x + dx) % nx) * 2 + core}

    def y_peer(d):
        return {"cell": (cell + d) % ny}

    core_peer = {"elec": z * lines + x * 2 + 1 - core}
    next_peer = {"elec": (elec + 1) % groups}
    prev_peer = {"elec": (elec + groups - 1) % groups}

    if groups < 64:
        b_buf[...] = jnp.zeros_like(b_buf)
    barrier = pltpu.get_barrier_semaphore()
    peers = (
        [y_peer(d) for d in far_first(ny)]
        + [chip_peer(dz, dx) for dz in far_first(nz) for dx in range(nx)]
        + [line_peer(d) for d in far_first(lines)]
        + [next_peer, prev_peer]
    )
    for peer in peers:
        pl.semaphore_signal(barrier, inc=1, device_id=peer, device_id_type=pl.DeviceIdType.MESH)

    own_copy = pltpu.make_async_copy(fields, own, own_sem)
    own_copy.start()

    def send(source, target, send_sem, recv_sem, peer):
        pltpu.make_async_remote_copy(
            src_ref=source, dst_ref=target, send_sem=send_sem, recv_sem=recv_sem,
            device_id=peer, device_id_type=pl.DeviceIdType.MESH,
        ).start()

    def z_step(s):
        return nz // 2 + (1 - 2 * (s % 2)) * ((s + 1) // 2)

    chunk = lines * 128

    def chunk_lanes(row, s):
        return pl.ds(pl.multiple_of(((row + z_step(s)) % nz) * chunk, chunk), chunk)

    def send_halo(s):
        for way, (peer, target, turn) in enumerate(((next_peer, low, 1), (prev_peer, high, groups - 1))):
            lanes = chunk_lanes((elec + turn) % groups // lines, s)
            send(fields.at[:, :, :, lanes], target.at[:, :, :, lanes],
                 halo_send_sem.at[way], halo_recv_sem.at[way, s], peer)

    for copy in inputs:
        copy.wait()
    owner = group[...]
    source_a = offs[pl.ds(0, 1), :]
    source_b = (source_a + bstep[...]) % PER_GROUP
    group_m = jnp.clip(owner + sides[pl.ds(0, 1), :], 0, groups - 1)
    group_n = jnp.clip(owner + sides[pl.ds(1, 1), :], 0, groups - 1)
    column_m = (group_m - owner + 1) * PER_GROUP + offs[pl.ds(1, 1), :]
    column_n = (group_n - owner + 1) * PER_GROUP + offs[pl.ds(2, 1), :]
    row = iota((groups, quads), 0)
    names = (row % nz) * lines + row // nz
    member = jnp.where(names == owner, 1.0, 0.0).astype(F32)
    earlier = jnp.where(iota((quads, quads), 0) < iota((quads, quads), 1), 1.0, 0.0).astype(BF16)
    before = jnp.dot(member.astype(BF16), earlier, preferred_element_type=F32)
    rank = jnp.sum(member * before, axis=0, keepdims=True)
    place = iota((8, quads), 0)
    indices = jnp.where(
        place == 0, source_a,
        jnp.where(place == 1, source_b, jnp.where(place == 2, column_m, jnp.where(place == 3, column_n, 0))),
    ).astype(F32)
    real = -resid[pl.ds(0, FRAMES, stride=2), :]
    imag = -resid[pl.ds(1, FRAMES, stride=2), :]
    entry = jnp.concatenate([real, imag, indices, jnp.zeros_like(indices)], axis=0)
    entries = jnp.concatenate(
        [jnp.where(rank == float(k), entry, 0.0) for k in range(CAP)], axis=0
    )
    named = member.astype(BF16)
    sorted_rows = sum(dot_nt(named, piece) for piece in split3(entries)[::-1])
    for line in range(lines):
        slots[line] = sorted_rows[line * nz:(line + 1) * nz, :]

    pl.semaphore_wait(barrier, len(peers))

    for d in far_first(lines):
        send(slots.at[(p + d) % lines], a_buf.at[pl.ds((d - 1) * nz, nz)],
             stage_send_sem.at[0], stage_recv_sem.at[0], line_peer(d))
    for s in range(0, halo_ends[0]):
        send_halo(s)
    a_buf[pl.ds((lines - 1) * nz, nz), :] = slots[p]
    own_copy.wait()
    arrived = a_buf.at[pl.ds(0, (lines - 1) * nz)]
    drain(arrived, stage_recv_sem.at[0])
    for to in range(nz):
        b_send[to] = a_buf[pl.ds(to, lines, stride=nz), :]
    for d in far_first(nz):
        send(b_send.at[(z + d) % nz], b_buf.at[pl.ds((d - 1) * lines, lines)],
             stage_send_sem.at[1], stage_recv_sem.at[1], z_peer(d))
    for s in range(halo_ends[0], halo_ends[1]):
        send_halo(s)
    b_buf[pl.ds((nz - 1) * lines, lines), :] = b_send[z]
    drain(b_buf.at[pl.ds(0, (nz - 1) * lines)], stage_recv_sem.at[1])

    received = b_buf[...]
    both = jnp.concatenate([received, pltpu.roll(received, 64, 1)], axis=0)
    turned = both.T
    terms = []
    columns = []
    for half in range(2):
        block = turned[half * SLOT:(half + 1) * SLOT, :]
        at_a = block[16:17].astype(jnp.int32)
        at_b = block[17:18].astype(jnp.int32)
        at_m = block[18:19].astype(jnp.int32)
        at_n = block[19:20].astype(jnp.int32)
        place = iota((PER_GROUP, 128), 0)
        sign = jnp.where(place == at_a, 1.0, 0.0) - jnp.where(place == at_b, 1.0, 0.0)
        terms.append(jnp.concatenate([block[k:k + 1] * sign for k in range(2 * FRAMES)], axis=0))
        place = iota((WINDOW, 128), 0)
        columns.append((jnp.where(place == at_m, 1.0, 0.0) - jnp.where(place == at_n, 1.0, 0.0)).astype(BF16))
    band = jnp.zeros((WINDOW, 128), F32)
    for half in range(2):
        for piece in split3(terms[half])[::-1]:
            band = band + dot_nt(columns[half], piece)
    c_send[...] = band
    for d in far_first(ny):
        send(c_send, c_buf.at[d - 1], stage_send_sem.at[2], stage_recv_sem.at[2], y_peer(d))
    for s in range(halo_ends[1], nz):
        send_halo(s)
    drain(c_buf, stage_recv_sem.at[2])
    for d in range(ny - 1):
        band = band + c_buf[d]
    band = band.astype(BF16).astype(F32)
    upper = jnp.concatenate([band, jnp.zeros((128 - WINDOW, 128), F32)], axis=0).T
    lower = jnp.concatenate([upper[64:], -upper[:64]], axis=0)
    first = upper + pltpu.roll(lower, WINDOW, 1)
    second = pltpu.roll(first, 2 * WINDOW, 1)
    third = pltpu.roll(first, 4 * WINDOW, 1)
    lane = iota((128, 128), 1)
    nothing = jnp.zeros((128, 128), BF16)
    weights[pl.ds(0, 128), pl.ds(0, 128)] = first.astype(BF16)
    weights[pl.ds(0, 128), pl.ds(128, 128)] = nothing
    weights[pl.ds(128, 128), pl.ds(0, 128)] = second.astype(BF16)
    weights[pl.ds(128, 128), pl.ds(128, 128)] = nothing
    weights[pl.ds(256, 128), pl.ds(0, 128)] = jnp.where(lane >= 4 * WINDOW, third, 0.0).astype(BF16)
    weights[pl.ds(256, 128), pl.ds(128, 128)] = jnp.where(lane < 2 * WINDOW, third, 0.0).astype(BF16)

    sublane = iota((PER_GROUP, 128), 0)

    def fold(first, second, width):
        keep = sublane % (2 * width) < width
        return jnp.where(keep, first, second) + pltpu.roll(
            jnp.where(keep, second, first), PER_GROUP - width, 0
        )

    def collect(rows):
        for width in (1, 2, 4):
            rows = [fold(rows[k], rows[k + 1], width) for k in range(0, len(rows), 2)]
        return rows[0]

    def compute(s):
        base = ((z + z_step(s)) % nz) * chunk
        arrived_lanes = chunk_lanes(z, s)
        drain(low.at[:, :, :, arrived_lanes], halo_recv_sem.at[0, s])
        drain(high.at[:, :, :, arrived_lanes], halo_recv_sem.at[1, s])
        matrix = weights[...][:, :3 * 2 * WINDOW]
        for chip in range(nx):
            lanes = pl.ds(pl.multiple_of(base + chip * 256, 256), 256)
            middle = [[own[i, c, :, lanes].astype(F32) for i in range(2)] for c in range(3)]
            window = []
            for c in range(3):
                for i in range(2):
                    window += [low[i, c, :, lanes].astype(F32), middle[c][i], high[i, c, :, lanes].astype(F32)]
            window = jnp.concatenate(window, axis=0).astype(BF16)
            adjoint = jnp.dot(matrix, window, preferred_element_type=F32)
            for k in range(2):
                half = slice(k * 128, (k + 1) * 128)
                real = []
                imag = []
                for t in range(FRAMES):
                    total_real = jnp.zeros((PER_GROUP, 128), F32)
                    total_imag = jnp.zeros((PER_GROUP, 128), F32)
                    for c in range(3):
                        at = c * 128 + t * 8
                        adj_real = adjoint[at:at + 8, half]
                        adj_imag = adjoint[at + 64:at + 72, half]
                        mid_real = middle[c][0][:, half]
                        mid_imag = middle[c][1][:, half]
                        total_real = total_real + mid_real * adj_real + mid_imag * adj_imag
                        total_imag = total_imag + mid_real * adj_imag - mid_imag * adj_real
                    real.append(total_real)
                    imag.append(total_imag)
                part[s, k, chip, pl.ds(0, 8), :] = collect(real)
                part[s, k, chip, pl.ds(8, 8), :] = collect(imag)
        send(part.at[s, 1 - core], core_recv.at[s], core_send_sem, core_recv_sem.at[s], core_peer)

    def share(s, d):
        send(rounded.at[s, (x + d) % nx], shares.at[s * nx + (d + nx - 1) % nx],
             share_send_sem, share_recv_sem.at[s], chip_peer(z_step(s), d))

    def add_core(s):
        drain(core_recv.at[s], core_recv_sem.at[s])
        both_cores = part[s, core] + core_recv[s]
        sums[s] = both_cores
        rounded[s] = both_cores.astype(BF16)
        for d in range(1, nx):
            share(s, d)

        @pl.when(s < nz - 1)
        def _():
            share(s, 0)

    core_lag = 2

    def step(s, carry):
        @pl.when(s < nz)
        def _():
            compute(s)

        @pl.when(s >= core_lag)
        def _():
            add_core(s - core_lag)

        return carry

    lax.fori_loop(0, nz + core_lag, step, 0)
    total = sums[nz - 1, x]
    for s in range(nz):
        count = nx if s < nz - 1 else nx - 1
        drain(shares.at[pl.ds(s * nx, count)], share_recv_sem.at[s])
        for d in range(count):
            total = total + shares[s * nx + d].astype(F32)
    out[pl.ds(0, FRAMES, stride=2), :] = total[0:8]
    out[pl.ds(1, FRAMES, stride=2), :] = total[8:16]

    drain(low, halo_send_sem.at[0])
    drain(high, halo_send_sem.at[1])
    drain(arrived, stage_send_sem.at[0])
    drain(b_buf.at[pl.ds(0, (nz - 1) * lines)], stage_send_sem.at[1])
    drain(c_buf, stage_send_sem.at[2])
    drain(core_recv, core_send_sem)
    drain(shares.at[pl.ds(0, nz * nx - 1)], share_send_sem)


def local(fields, residual, quad_group, offsets, b_step, sides):
    groups = lax.axis_size("elec")
    ny = lax.axis_size("cell")
    nx = X_CHIPS
    lines = 2 * nx
    nz = groups // lines
    cells = fields.shape[3]
    count = residual.shape[0]
    resid = jnp.transpose(residual, (1, 2, 0)).reshape(2 * FRAMES, count)
    vmem = pl.BlockSpec(memory_space=pltpu.VMEM)
    field_shape = (2, 3, PER_GROUP, cells)
    dma = pltpu.SemaphoreType.DMA
    gradient = pl.pallas_call(
        functools.partial(kernel, (nz, nx, ny)),
        out_shape=jax.ShapeDtypeStruct((2 * FRAMES, 128), F32),
        in_specs=[pl.BlockSpec(memory_space=pltpu.HBM)] * 6,
        out_specs=vmem,
        scratch_shapes=[
            pltpu.VMEM((2 * FRAMES, count), F32),
            pltpu.VMEM((1, count), jnp.int32),
            pltpu.VMEM((3, count), jnp.int32),
            pltpu.VMEM((1, count), jnp.int32),
            pltpu.VMEM((2, count), jnp.int32),
            pltpu.VMEM(field_shape, BF16),
            pltpu.VMEM(field_shape, BF16),
            pltpu.VMEM(field_shape, BF16),
            pltpu.VMEM((lines, nz, 128), F32),
            pltpu.VMEM((groups, 128), F32),
            pltpu.VMEM((nz, lines, 128), F32),
            pltpu.VMEM((64, 128), F32),
            pltpu.VMEM((WINDOW, 128), F32),
            pltpu.VMEM((ny - 1, WINDOW, 128), F32),
            pltpu.VMEM((384, 256), BF16),
            pltpu.VMEM((nz, 2, nx, 16, 128), F32),
            pltpu.VMEM((nz, nx, 16, 128), F32),
            pltpu.VMEM((nz, nx, 16, 128), F32),
            pltpu.VMEM((nz, nx, 16, 128), BF16),
            pltpu.VMEM((nz * nx, 16, 128), BF16),
            dma((5,)), dma, dma((2,)), dma((2, nz)),
            dma((3,)), dma((3,)),
            dma, dma((nz,)), dma, dma((nz,)),
        ],
        compiler_params=pltpu.CompilerParams(
            collective_id=0, has_side_effects=True, vmem_limit_bytes=40 * 1024 * 1024
        ),
    )(*(
        pltpu.with_memory_space_constraint(value, pltpu.HBM)
        for value in (fields, resid, quad_group.T, offsets.T, b_step.T, sides.T)
    ))
    return gradient.reshape(FRAMES, 2, 1, 128)


def solution(mesh):
    return jax.shard_map(
        local,
        mesh=mesh,
        in_specs=(
            P(None, None, "elec", "cell"),
            P(("elec", "cell"), None, None),
            P(("elec", "cell"), None),
            P(("elec", "cell"), None),
            P(("elec", "cell"), None),
            P(("elec", "cell"), None),
        ),
        out_specs=P(None, None, "cell", "elec"),
        check_vma=False,
    )
```

```python
import functools

import jax
import jax.numpy as jnp
from jax import lax
from jax.experimental import pallas as pl
from jax.experimental.pallas import tpu as pltpu
from jax.sharding import PartitionSpec as P

X_CHIPS = 4
PER_GROUP = 8
FRAMES = 8
CAP = 4
SLOT = 32
WINDOW = 3 * PER_GROUP
F32 = jnp.float32
BF16 = jnp.bfloat16


def iota(shape, dim):
    return lax.broadcasted_iota(jnp.int32, shape, dim)


def split3(value):
    high = value.astype(BF16)
    rest = value - high.astype(F32)
    middle = rest.astype(BF16)
    low = (rest - middle.astype(F32)).astype(BF16)
    return high, middle, low


def dot_nt(left, right):
    return lax.dot_general(left, right, (((1,), (1,)), ((), ())), preferred_element_type=F32)


def far_first(count):
    return sorted(range(1, count), key=lambda d: -min(d, count - d))


def drain(ref, sem):
    pltpu.make_async_copy(ref, ref, sem).wait()


def kernel(
    sizes,
    fields, resid_in, group_in, offs_in, bstep_in, sides_in,
    out,
    resid, group, offs, bstep, sides,
    own, low, high,
    slots, b_buf, c_send, c_buf, weights,
    part, core_recv, sums, rounded, shares,
    in_sem, own_sem, halo_send_sem, halo_recv_sem,
    stage_send_sem, stage_recv_sem,
    core_send_sem, core_recv_sem, share_send_sem, share_recv_sem,
):
    nz, nx, ny = sizes
    lines = 2 * nx
    groups = nz * lines
    quads = resid.shape[1]
    halo_ends = (0, nz // 4)
    elec = lax.axis_index("elec")
    cell = lax.axis_index("cell")
    z = elec // lines
    p = elec % lines
    x = p // 2
    core = p % 2

    inputs = [
        pltpu.make_async_copy(source, target, in_sem.at[number])
        for number, (source, target) in enumerate(
            zip((resid_in, group_in, offs_in, bstep_in, sides_in), (resid, group, offs, bstep, sides))
        )
    ]
    for copy in inputs:
        copy.start()

    def line_peer(d):
        return {"elec": z * lines + (p + d) % lines}

    def z_peer(d):
        return {"elec": ((z + d) % nz) * lines + p}

    def plane_peer(dz, dp):
        return {"elec": ((z + dz) % nz) * lines + (p + dp) % lines}

    def chip_peer(dz, dx):
        return {"elec": ((z + dz) % nz) * lines + ((x + dx) % nx) * 2 + core}

    def y_peer(d):
        return {"cell": (cell + d) % ny}

    core_peer = {"elec": z * lines + x * 2 + 1 - core}
    next_peer = {"elec": (elec + 1) % groups}
    prev_peer = {"elec": (elec + groups - 1) % groups}

    if groups < 64:
        b_buf[...] = jnp.zeros_like(b_buf)
    barrier = pltpu.get_barrier_semaphore()
    plane = [(dz, dp) for dz in far_first(nz) + [0] for dp in far_first(lines) + [0]][:-1]
    peers = (
        [y_peer(d) for d in far_first(ny)]
        + [plane_peer(dz, dp) for dz, dp in plane]
        + [next_peer, prev_peer]
    )
    for peer in peers:
        pl.semaphore_signal(barrier, inc=1, device_id=peer, device_id_type=pl.DeviceIdType.MESH)

    own_copy = pltpu.make_async_copy(fields, own, own_sem)
    own_copy.start()

    def send(source, target, send_sem, recv_sem, peer):
        pltpu.make_async_remote_copy(
            src_ref=source, dst_ref=target, send_sem=send_sem, recv_sem=recv_sem,
            device_id=peer, device_id_type=pl.DeviceIdType.MESH,
        ).start()

    def z_step(s):
        return nz // 2 + (1 - 2 * (s % 2)) * ((s + 1) // 2)

    chunk = lines * 128

    def chunk_lanes(row, s):
        return pl.ds(pl.multiple_of(((row + z_step(s)) % nz) * chunk, chunk), chunk)

    def send_halo(s):
        for way, (peer, target, turn) in enumerate(((next_peer, low, 1), (prev_peer, high, groups - 1))):
            lanes = chunk_lanes((elec + turn) % groups // lines, s)
            send(fields.at[:, :, :, lanes], target.at[:, :, :, lanes],
                 halo_send_sem.at[way], halo_recv_sem.at[way, s], peer)

    for copy in inputs:
        copy.wait()
    owner = group[...]
    source_a = offs[pl.ds(0, 1), :]
    source_b = (source_a + bstep[...]) % PER_GROUP
    group_m = jnp.clip(owner + sides[pl.ds(0, 1), :], 0, groups - 1)
    group_n = jnp.clip(owner + sides[pl.ds(1, 1), :], 0, groups - 1)
    column_m = (group_m - owner + 1) * PER_GROUP + offs[pl.ds(1, 1), :]
    column_n = (group_n - owner + 1) * PER_GROUP + offs[pl.ds(2, 1), :]
    row = iota((groups, quads), 0)
    names = (row % nz) * lines + row // nz
    member = jnp.where(names == owner, 1.0, 0.0).astype(F32)
    earlier = jnp.where(iota((quads, quads), 0) < iota((quads, quads), 1), 1.0, 0.0).astype(BF16)
    before = jnp.dot(member.astype(BF16), earlier, preferred_element_type=F32)
    rank = jnp.sum(member * before, axis=0, keepdims=True)
    place = iota((8, quads), 0)
    indices = jnp.where(
        place == 0, source_a,
        jnp.where(place == 1, source_b, jnp.where(place == 2, column_m, jnp.where(place == 3, column_n, 0))),
    ).astype(F32)
    real = -resid[pl.ds(0, FRAMES, stride=2), :]
    imag = -resid[pl.ds(1, FRAMES, stride=2), :]
    entry = jnp.concatenate([real, imag, indices, jnp.zeros_like(indices)], axis=0)
    entries = jnp.concatenate(
        [jnp.where(rank == float(k), entry, 0.0) for k in range(CAP)], axis=0
    )
    named = member.astype(BF16)
    sorted_rows = sum(dot_nt(named, piece) for piece in split3(entries)[::-1])
    slots[...] = sorted_rows.reshape(groups, 1, 128)

    pl.semaphore_wait(barrier, len(peers))

    for dz, dp in plane:
        to = (p + dp) % lines * nz + (z + dz) % nz
        send(slots.at[to], b_buf.at[dz * lines + dp - 1],
             stage_send_sem.at[0], stage_recv_sem.at[0], plane_peer(dz, dp))
    for s in range(halo_ends[0], halo_ends[1]):
        send_halo(s)
    b_buf[groups - 1] = slots[p * nz + z]
    own_copy.wait()
    arrived = b_buf.at[pl.ds(0, groups - 1)]
    drain(arrived, stage_recv_sem.at[0])

    received = b_buf[...].reshape(64, 128)
    both = jnp.concatenate([received, pltpu.roll(received, 64, 1)], axis=0)
    turned = both.T
    terms = []
    columns = []
    for half in range(2):
        block = turned[half * SLOT:(half + 1) * SLOT, :]
        at_a = block[16:17].astype(jnp.int32)
        at_b = block[17:18].astype(jnp.int32)
        at_m = block[18:19].astype(jnp.int32)
        at_n = block[19:20].astype(jnp.int32)
        place = iota((PER_GROUP, 128), 0)
        sign = jnp.where(place == at_a, 1.0, 0.0) - jnp.where(place == at_b, 1.0, 0.0)
        terms.append(jnp.concatenate([block[k:k + 1] * sign for k in range(2 * FRAMES)], axis=0))
        place = iota((WINDOW, 128), 0)
        columns.append((jnp.where(place == at_m, 1.0, 0.0) - jnp.where(place == at_n, 1.0, 0.0)).astype(BF16))
    band = jnp.zeros((WINDOW, 128), F32)
    for half in range(2):
        for piece in split3(terms[half])[::-1]:
            band = band + dot_nt(columns[half], piece)
    c_send[...] = band
    for d in far_first(ny):
        send(c_send, c_buf.at[d - 1], stage_send_sem.at[1], stage_recv_sem.at[1], y_peer(d))
    for s in range(halo_ends[1], nz):
        send_halo(s)
    drain(c_buf, stage_recv_sem.at[1])
    for d in range(ny - 1):
        band = band + c_buf[d]
    band = band.astype(BF16).astype(F32)
    upper = jnp.concatenate([band, jnp.zeros((128 - WINDOW, 128), F32)], axis=0).T
    lower = jnp.concatenate([upper[64:], -upper[:64]], axis=0)
    first = upper + pltpu.roll(lower, WINDOW, 1)
    second = pltpu.roll(first, 2 * WINDOW, 1)
    third = pltpu.roll(first, 4 * WINDOW, 1)
    lane = iota((128, 128), 1)
    nothing = jnp.zeros((128, 128), BF16)
    weights[pl.ds(0, 128), pl.ds(0, 128)] = first.astype(BF16)
    weights[pl.ds(0, 128), pl.ds(128, 128)] = nothing
    weights[pl.ds(128, 128), pl.ds(0, 128)] = second.astype(BF16)
    weights[pl.ds(128, 128), pl.ds(128, 128)] = nothing
    weights[pl.ds(256, 128), pl.ds(0, 128)] = jnp.where(lane >= 4 * WINDOW, third, 0.0).astype(BF16)
    weights[pl.ds(256, 128), pl.ds(128, 128)] = jnp.where(lane < 2 * WINDOW, third, 0.0).astype(BF16)

    sublane = iota((PER_GROUP, 128), 0)

    def fold(first, second, width):
        keep = sublane % (2 * width) < width
        return jnp.where(keep, first, second) + pltpu.roll(
            jnp.where(keep, second, first), PER_GROUP - width, 0
        )

    def collect(rows):
        for width in (1, 2, 4):
            rows = [fold(rows[k], rows[k + 1], width) for k in range(0, len(rows), 2)]
        return rows[0]

    def compute(s):
        base = ((z + z_step(s)) % nz) * chunk
        arrived_lanes = chunk_lanes(z, s)
        drain(low.at[:, :, :, arrived_lanes], halo_recv_sem.at[0, s])
        drain(high.at[:, :, :, arrived_lanes], halo_recv_sem.at[1, s])
        matrix = weights[...][:, :3 * 2 * WINDOW]
        for chip in range(nx):
            lanes = pl.ds(pl.multiple_of(base + chip * 256, 256), 256)
            middle = [[own[i, c, :, lanes].astype(F32) for i in range(2)] for c in range(3)]
            window = []
            for c in range(3):
                for i in range(2):
                    window += [low[i, c, :, lanes].astype(F32), middle[c][i], high[i, c, :, lanes].astype(F32)]
            window = jnp.concatenate(window, axis=0).astype(BF16)
            adjoint = jnp.dot(matrix, window, preferred_element_type=F32)
            for k in range(2):
                half = slice(k * 128, (k + 1) * 128)
                real = []
                imag = []
                for t in range(FRAMES):
                    total_real = jnp.zeros((PER_GROUP, 128), F32)
                    total_imag = jnp.zeros((PER_GROUP, 128), F32)
                    for c in range(3):
                        at = c * 128 + t * 8
                        adj_real = adjoint[at:at + 8, half]
                        adj_imag = adjoint[at + 64:at + 72, half]
                        mid_real = middle[c][0][:, half]
                        mid_imag = middle[c][1][:, half]
                        total_real = total_real + mid_real * adj_real + mid_imag * adj_imag
                        total_imag = total_imag + mid_real * adj_imag - mid_imag * adj_real
                    real.append(total_real)
                    imag.append(total_imag)
                part[s, k, chip, pl.ds(0, 8), :] = collect(real)
                part[s, k, chip, pl.ds(8, 8), :] = collect(imag)
        send(part.at[s, 1 - core], core_recv.at[s], core_send_sem, core_recv_sem.at[s], core_peer)

    def share(s, d):
        send(rounded.at[s, (x + d) % nx], shares.at[s * nx + (d + nx - 1) % nx],
             share_send_sem, share_recv_sem.at[s], chip_peer(z_step(s), d))

    def add_core(s):
        drain(core_recv.at[s], core_recv_sem.at[s])
        both_cores = part[s, core] + core_recv[s]
        sums[s] = both_cores
        rounded[s] = both_cores.astype(BF16)
        for d in range(1, nx):
            share(s, d)

        @pl.when(s < nz - 1)
        def _():
            share(s, 0)

    core_lag = 2

    def step(s, carry):
        @pl.when(s < nz)
        def _():
            compute(s)

        @pl.when(s >= core_lag)
        def _():
            add_core(s - core_lag)

        return carry

    lax.fori_loop(0, nz + core_lag, step, 0)
    total = sums[nz - 1, x]
    for s in range(nz):
        count = nx if s < nz - 1 else nx - 1
        drain(shares.at[pl.ds(s * nx, count)], share_recv_sem.at[s])
        for d in range(count):
            total = total + shares[s * nx + d].astype(F32)
    out[pl.ds(0, FRAMES, stride=2), :] = total[0:8]
    out[pl.ds(1, FRAMES, stride=2), :] = total[8:16]

    drain(low, halo_send_sem.at[0])
    drain(high, halo_send_sem.at[1])
    drain(arrived, stage_send_sem.at[0])
    drain(c_buf, stage_send_sem.at[1])
    drain(core_recv, core_send_sem)
    drain(shares.at[pl.ds(0, nz * nx - 1)], share_send_sem)


def local(fields, residual, quad_group, offsets, b_step, sides):
    groups = lax.axis_size("elec")
    ny = lax.axis_size("cell")
    nx = X_CHIPS
    lines = 2 * nx
    nz = groups // lines
    cells = fields.shape[3]
    count = residual.shape[0]
    resid = jnp.transpose(residual, (1, 2, 0)).reshape(2 * FRAMES, count)
    vmem = pl.BlockSpec(memory_space=pltpu.VMEM)
    field_shape = (2, 3, PER_GROUP, cells)
    dma = pltpu.SemaphoreType.DMA
    gradient = pl.pallas_call(
        functools.partial(kernel, (nz, nx, ny)),
        out_shape=jax.ShapeDtypeStruct((2 * FRAMES, 128), F32),
        in_specs=[pl.BlockSpec(memory_space=pltpu.HBM)] * 6,
        out_specs=vmem,
        scratch_shapes=[
            pltpu.VMEM((2 * FRAMES, count), F32),
            pltpu.VMEM((1, count), jnp.int32),
            pltpu.VMEM((3, count), jnp.int32),
            pltpu.VMEM((1, count), jnp.int32),
            pltpu.VMEM((2, count), jnp.int32),
            pltpu.VMEM(field_shape, BF16),
            pltpu.VMEM(field_shape, BF16),
            pltpu.VMEM(field_shape, BF16),
            pltpu.VMEM((groups, 1, 128), F32),
            pltpu.VMEM((64, 1, 128), F32),
            pltpu.VMEM((WINDOW, 128), F32),
            pltpu.VMEM((ny - 1, WINDOW, 128), F32),
            pltpu.VMEM((384, 256), BF16),
            pltpu.VMEM((nz, 2, nx, 16, 128), F32),
            pltpu.VMEM((nz, nx, 16, 128), F32),
            pltpu.VMEM((nz, nx, 16, 128), F32),
            pltpu.VMEM((nz, nx, 16, 128), BF16),
            pltpu.VMEM((nz * nx, 16, 128), BF16),
            dma((5,)), dma, dma((2,)), dma((2, nz)),
            dma((2,)), dma((2,)),
            dma, dma((nz,)), dma, dma((nz,)),
        ],
        compiler_params=pltpu.CompilerParams(
            collective_id=0, has_side_effects=True, vmem_limit_bytes=40 * 1024 * 1024
        ),
    )(*(
        pltpu.with_memory_space_constraint(value, pltpu.HBM)
        for value in (fields, resid, quad_group.T, offsets.T, b_step.T, sides.T)
    ))
    return gradient.reshape(FRAMES, 2, 1, 128)


def solution(mesh):
    return jax.shard_map(
        local,
        mesh=mesh,
        in_specs=(
            P(None, None, "elec", "cell"),
            P(("elec", "cell"), None, None),
            P(("elec", "cell"), None),
            P(("elec", "cell"), None),
            P(("elec", "cell"), None),
            P(("elec", "cell"), None),
        ),
        out_specs=P(None, None, "cell", "elec"),
        check_vma=False,
    )
```

```python
import functools

import jax
import jax.numpy as jnp
from jax import lax
from jax.experimental import pallas as pl
from jax.experimental.pallas import tpu as pltpu
from jax.sharding import PartitionSpec as P

X_CHIPS = 4
PER_GROUP = 8
FRAMES = 8
CAP = 4
SLOT = 32
WINDOW = 3 * PER_GROUP
F32 = jnp.float32
BF16 = jnp.bfloat16


def iota(shape, dim):
    return lax.broadcasted_iota(jnp.int32, shape, dim)


def split3(value):
    high = value.astype(BF16)
    rest = value - high.astype(F32)
    middle = rest.astype(BF16)
    low = (rest - middle.astype(F32)).astype(BF16)
    return high, middle, low


def dot_nt(left, right):
    return lax.dot_general(left, right, (((1,), (1,)), ((), ())), preferred_element_type=F32)


def far_first(count):
    return sorted(range(1, count), key=lambda d: -min(d, count - d))


def drain(ref, sem):
    pltpu.make_async_copy(ref, ref, sem).wait()


def kernel(
    sizes,
    fields, resid_in, group_in, offs_in, bstep_in, sides_in,
    out,
    resid, group, offs, bstep, sides,
    own, low, high,
    slots, b_buf, c_send, c_buf, weights,
    part, core_recv, sums, rounded, shares,
    in_sem, own_sem, halo_send_sem, halo_recv_sem,
    stage_send_sem, stage_recv_sem,
    core_send_sem, core_recv_sem, share_send_sem, share_recv_sem,
):
    nz, nx, ny = sizes
    lines = 2 * nx
    groups = nz * lines
    quads = resid.shape[1]
    halo_ends = (0, nz // 4)
    elec = lax.axis_index("elec")
    cell = lax.axis_index("cell")
    z = elec // lines
    p = elec % lines
    x = p // 2
    core = p % 2

    inputs = [
        pltpu.make_async_copy(source, target, in_sem.at[number])
        for number, (source, target) in enumerate(
            zip((resid_in, group_in, offs_in, bstep_in, sides_in), (resid, group, offs, bstep, sides))
        )
    ]
    for copy in inputs:
        copy.start()

    def line_peer(d):
        return {"elec": z * lines + (p + d) % lines}

    def z_peer(d):
        return {"elec": ((z + d) % nz) * lines + p}

    def plane_peer(dz, dp):
        return {"elec": ((z + dz) % nz) * lines + (p + dp) % lines}

    def chip_peer(dz, dx):
        return {"elec": ((z + dz) % nz) * lines + ((x + dx) % nx) * 2 + core}

    def y_peer(d):
        return {"cell": (cell + d) % ny}

    core_peer = {"elec": z * lines + x * 2 + 1 - core}
    next_peer = {"elec": (elec + 1) % groups}
    prev_peer = {"elec": (elec + groups - 1) % groups}

    if groups < 64:
        b_buf[...] = jnp.zeros_like(b_buf)
    barrier = pltpu.get_barrier_semaphore()
    plane = [(dz, dp) for dz in far_first(nz) + [0] for dp in far_first(lines) + [0]][:-1]
    peers = (
        [y_peer(d) for d in far_first(ny)]
        + [plane_peer(dz, dp) for dz, dp in plane]
        + [next_peer, prev_peer]
    )
    for peer in peers:
        pl.semaphore_signal(barrier, inc=1, device_id=peer, device_id_type=pl.DeviceIdType.MESH)

    own_copy = pltpu.make_async_copy(fields, own, own_sem)
    own_copy.start()

    def send(source, target, send_sem, recv_sem, peer):
        pltpu.make_async_remote_copy(
            src_ref=source, dst_ref=target, send_sem=send_sem, recv_sem=recv_sem,
            device_id=peer, device_id_type=pl.DeviceIdType.MESH,
        ).start()

    def z_step(s):
        return nz // 2 + (1 - 2 * (s % 2)) * ((s + 1) // 2)

    chunk = lines * 128

    def chunk_lanes(row, s):
        return pl.ds(pl.multiple_of(((row + z_step(s)) % nz) * chunk, chunk), chunk)

    def send_halo(s):
        for way, (peer, target, turn) in enumerate(((next_peer, low, 1), (prev_peer, high, groups - 1))):
            lanes = chunk_lanes((elec + turn) % groups // lines, s)
            send(fields.at[:, :, :, lanes], target.at[:, :, :, lanes],
                 halo_send_sem.at[way], halo_recv_sem.at[way, s], peer)

    for copy in inputs:
        copy.wait()
    owner = group[...]
    source_a = offs[pl.ds(0, 1), :]
    source_b = (source_a + bstep[...]) % PER_GROUP
    group_m = jnp.clip(owner + sides[pl.ds(0, 1), :], 0, groups - 1)
    group_n = jnp.clip(owner + sides[pl.ds(1, 1), :], 0, groups - 1)
    column_m = (group_m - owner + 1) * PER_GROUP + offs[pl.ds(1, 1), :]
    column_n = (group_n - owner + 1) * PER_GROUP + offs[pl.ds(2, 1), :]
    row = iota((groups, quads), 0)
    names = (row % nz) * lines + row // nz
    member = jnp.where(names == owner, 1.0, 0.0).astype(F32)
    earlier = jnp.where(iota((quads, quads), 0) < iota((quads, quads), 1), 1.0, 0.0).astype(BF16)
    before = jnp.dot(member.astype(BF16), earlier, preferred_element_type=F32)
    rank = jnp.sum(member * before, axis=0, keepdims=True)
    place = iota((8, quads), 0)
    indices = jnp.where(
        place == 0, source_a,
        jnp.where(place == 1, source_b, jnp.where(place == 2, column_m, jnp.where(place == 3, column_n, 0))),
    ).astype(F32)
    real = -resid[pl.ds(0, FRAMES, stride=2), :]
    imag = -resid[pl.ds(1, FRAMES, stride=2), :]
    entry = jnp.concatenate([real, imag, indices, jnp.zeros_like(indices)], axis=0)
    entries = jnp.concatenate(
        [jnp.where(rank == float(k), entry, 0.0) for k in range(CAP)], axis=0
    )
    named = member.astype(BF16)
    sorted_rows = sum(dot_nt(named, piece) for piece in split3(entries)[::-1])
    slots[...] = sorted_rows.reshape(groups, 1, 128)

    pl.semaphore_wait(barrier, len(peers))

    for dz, dp in plane:
        to = (p + dp) % lines * nz + (z + dz) % nz
        send(slots.at[to], b_buf.at[dz * lines + dp - 1],
             stage_send_sem.at[0], stage_recv_sem.at[0], plane_peer(dz, dp))
    for s in range(halo_ends[0], halo_ends[1]):
        send_halo(s)
    b_buf[groups - 1] = slots[p * nz + z]
    own_copy.wait()
    arrived = b_buf.at[pl.ds(0, groups - 1)]
    drain(arrived, stage_recv_sem.at[0])

    received = b_buf[...].reshape(64, 128)
    both = jnp.concatenate([received, pltpu.roll(received, 64, 1)], axis=0)
    turned = both.T
    terms = []
    columns = []
    for half in range(2):
        block = turned[half * SLOT:(half + 1) * SLOT, :]
        at_a = block[16:17].astype(jnp.int32)
        at_b = block[17:18].astype(jnp.int32)
        at_m = block[18:19].astype(jnp.int32)
        at_n = block[19:20].astype(jnp.int32)
        place = iota((PER_GROUP, 128), 0)
        sign = jnp.where(place == at_a, 1.0, 0.0) - jnp.where(place == at_b, 1.0, 0.0)
        terms.append(jnp.concatenate([block[k:k + 1] * sign for k in range(2 * FRAMES)], axis=0))
        place = iota((WINDOW, 128), 0)
        columns.append((jnp.where(place == at_m, 1.0, 0.0) - jnp.where(place == at_n, 1.0, 0.0)).astype(BF16))
    band = jnp.zeros((WINDOW, 128), F32)
    for half in range(2):
        for piece in split3(terms[half])[::-1]:
            band = band + dot_nt(columns[half], piece)
    c_send[...] = band
    for d in far_first(ny):
        send(c_send, c_buf.at[d - 1], stage_send_sem.at[1], stage_recv_sem.at[1], y_peer(d))
    for s in range(halo_ends[1], nz):
        send_halo(s)
    drain(c_buf, stage_recv_sem.at[1])
    for d in range(ny - 1):
        band = band + c_buf[d]
    band = band.astype(BF16).astype(F32)
    upper = jnp.concatenate([band, jnp.zeros((128 - WINDOW, 128), F32)], axis=0).T
    lower = jnp.concatenate([upper[64:], -upper[:64]], axis=0)
    first = upper + pltpu.roll(lower, WINDOW, 1)
    second = pltpu.roll(first, 2 * WINDOW, 1)
    third = pltpu.roll(first, 4 * WINDOW, 1)
    lane = iota((128, 128), 1)
    nothing = jnp.zeros((128, 128), BF16)
    weights[pl.ds(0, 128), pl.ds(0, 128)] = first.astype(BF16)
    weights[pl.ds(0, 128), pl.ds(128, 128)] = nothing
    weights[pl.ds(128, 128), pl.ds(0, 128)] = second.astype(BF16)
    weights[pl.ds(128, 128), pl.ds(128, 128)] = nothing
    weights[pl.ds(256, 128), pl.ds(0, 128)] = jnp.where(lane >= 4 * WINDOW, third, 0.0).astype(BF16)
    weights[pl.ds(256, 128), pl.ds(128, 128)] = jnp.where(lane < 2 * WINDOW, third, 0.0).astype(BF16)

    sublane = iota((PER_GROUP, 128), 0)

    def fold(first, second, width):
        keep = sublane % (2 * width) < width
        return jnp.where(keep, first, second) + pltpu.roll(
            jnp.where(keep, second, first), PER_GROUP - width, 0
        )

    def collect(rows):
        for width in (1, 2, 4):
            rows = [fold(rows[k], rows[k + 1], width) for k in range(0, len(rows), 2)]
        return rows[0]

    def compute(s):
        base = ((z + z_step(s)) % nz) * chunk
        arrived_lanes = chunk_lanes(z, s)
        drain(low.at[:, :, :, arrived_lanes], halo_recv_sem.at[0, s])
        drain(high.at[:, :, :, arrived_lanes], halo_recv_sem.at[1, s])
        matrix = weights[...][:, :3 * 2 * WINDOW]
        for chip in range(nx):
            lanes = pl.ds(pl.multiple_of(base + chip * 256, 256), 256)
            middle = [[own[i, c, :, lanes].astype(F32) for i in range(2)] for c in range(3)]
            window = []
            for c in range(3):
                for i in range(2):
                    window += [low[i, c, :, lanes].astype(F32), middle[c][i], high[i, c, :, lanes].astype(F32)]
            window = jnp.concatenate(window, axis=0).astype(BF16)
            adjoint = jnp.dot(matrix, window, preferred_element_type=F32)
            for k in range(2):
                half = slice(k * 128, (k + 1) * 128)
                real = []
                imag = []
                for t in range(FRAMES):
                    total_real = jnp.zeros((PER_GROUP, 128), F32)
                    total_imag = jnp.zeros((PER_GROUP, 128), F32)
                    for c in range(3):
                        at = c * 128 + t * 8
                        adj_real = adjoint[at:at + 8, half]
                        adj_imag = adjoint[at + 64:at + 72, half]
                        mid_real = middle[c][0][:, half]
                        mid_imag = middle[c][1][:, half]
                        total_real = total_real + mid_real * adj_real + mid_imag * adj_imag
                        total_imag = total_imag + mid_real * adj_imag - mid_imag * adj_real
                    real.append(total_real)
                    imag.append(total_imag)
                part[s, k, chip, pl.ds(0, 8), :] = collect(real)
                part[s, k, chip, pl.ds(8, 8), :] = collect(imag)
        send(part.at[s, 1 - core], core_recv.at[s], core_send_sem, core_recv_sem.at[s], core_peer)

    def share(s, d):
        send(rounded.at[s, (x + d) % nx], shares.at[s * nx + (d + nx - 1) % nx],
             share_send_sem, share_recv_sem.at[s], chip_peer(z_step(s), d))

    def add_core(s):
        drain(core_recv.at[s], core_recv_sem.at[s])
        both_cores = part[s, core] + core_recv[s]
        sums[s] = both_cores
        rounded[s] = both_cores.astype(BF16)
        for d in range(1, nx):
            share(s, d)

        @pl.when(s < nz - 1)
        def _():
            share(s, 0)

    core_lag = 3

    def step(s, carry):
        @pl.when(s < nz)
        def _():
            compute(s)

        @pl.when(s >= core_lag)
        def _():
            add_core(s - core_lag)

        return carry

    lax.fori_loop(0, nz + core_lag, step, 0)
    total = sums[nz - 1, x]
    for s in range(nz):
        count = nx if s < nz - 1 else nx - 1
        drain(shares.at[pl.ds(s * nx, count)], share_recv_sem.at[s])
        for d in range(count):
            total = total + shares[s * nx + d].astype(F32)
    out[pl.ds(0, FRAMES, stride=2), :] = total[0:8]
    out[pl.ds(1, FRAMES, stride=2), :] = total[8:16]

    drain(low, halo_send_sem.at[0])
    drain(high, halo_send_sem.at[1])
    drain(arrived, stage_send_sem.at[0])
    drain(c_buf, stage_send_sem.at[1])
    drain(core_recv, core_send_sem)
    drain(shares.at[pl.ds(0, nz * nx - 1)], share_send_sem)


def local(fields, residual, quad_group, offsets, b_step, sides):
    groups = lax.axis_size("elec")
    ny = lax.axis_size("cell")
    nx = X_CHIPS
    lines = 2 * nx
    nz = groups // lines
    cells = fields.shape[3]
    count = residual.shape[0]
    resid = jnp.transpose(residual, (1, 2, 0)).reshape(2 * FRAMES, count)
    vmem = pl.BlockSpec(memory_space=pltpu.VMEM)
    field_shape = (2, 3, PER_GROUP, cells)
    dma = pltpu.SemaphoreType.DMA
    gradient = pl.pallas_call(
        functools.partial(kernel, (nz, nx, ny)),
        out_shape=jax.ShapeDtypeStruct((2 * FRAMES, 128), F32),
        in_specs=[pl.BlockSpec(memory_space=pltpu.HBM)] * 6,
        out_specs=vmem,
        scratch_shapes=[
            pltpu.VMEM((2 * FRAMES, count), F32),
            pltpu.VMEM((1, count), jnp.int32),
            pltpu.VMEM((3, count), jnp.int32),
            pltpu.VMEM((1, count), jnp.int32),
            pltpu.VMEM((2, count), jnp.int32),
            pltpu.VMEM(field_shape, BF16),
            pltpu.VMEM(field_shape, BF16),
            pltpu.VMEM(field_shape, BF16),
            pltpu.VMEM((groups, 1, 128), F32),
            pltpu.VMEM((64, 1, 128), F32),
            pltpu.VMEM((WINDOW, 128), F32),
            pltpu.VMEM((ny - 1, WINDOW, 128), F32),
            pltpu.VMEM((384, 256), BF16),
            pltpu.VMEM((nz, 2, nx, 16, 128), F32),
            pltpu.VMEM((nz, nx, 16, 128), F32),
            pltpu.VMEM((nz, nx, 16, 128), F32),
            pltpu.VMEM((nz, nx, 16, 128), BF16),
            pltpu.VMEM((nz * nx, 16, 128), BF16),
            dma((5,)), dma, dma((2,)), dma((2, nz)),
            dma((2,)), dma((2,)),
            dma, dma((nz,)), dma, dma((nz,)),
        ],
        compiler_params=pltpu.CompilerParams(
            collective_id=0, has_side_effects=True, vmem_limit_bytes=40 * 1024 * 1024
        ),
    )(*(
        pltpu.with_memory_space_constraint(value, pltpu.HBM)
        for value in (fields, resid, quad_group.T, offsets.T, b_step.T, sides.T)
    ))
    return gradient.reshape(FRAMES, 2, 1, 128)


def solution(mesh):
    return jax.shard_map(
        local,
        mesh=mesh,
        in_specs=(
            P(None, None, "elec", "cell"),
            P(("elec", "cell"), None, None),
            P(("elec", "cell"), None),
            P(("elec", "cell"), None),
            P(("elec", "cell"), None),
            P(("elec", "cell"), None),
        ),
        out_specs=P(None, None, "cell", "elec"),
        check_vma=False,
    )
```
